32 devices in a mesh: head: 2 (over y), seq: 4 (over z), dp: 4 (over x, core).
Axes of the slice: x: 2, y: 2, z: 4, core: 2. Of those that a mesh axis runs over, the one named last changes fastest.
Arguments:
- teacher_query: bfloat16 [4, 512, 3072], P('dp', 'seq', 'head'), may hold values from -6 to 6
- teacher_key: bfloat16 [4, 512, 3072], P('dp', 'seq', 'head'), may hold values from -6 to 6
- student_query: bfloat16 [4, 512, 512], P('dp', 'seq'), may hold values from -6 to 6
- student_key: bfloat16 [4, 512, 512], P('dp', 'seq'), may hold values from -6 to 6
- head_mix: float32 [24, 8], P('head'), may hold values from 0.02 to 0.25
Outputs:
- grad_query: float32 [4, 512, 512], P('dp', 'seq', 'head')
- grad_key: float32 [4, 512, 512], P('dp', 'seq', 'head')
- grad_mix: float32 [24, 8], P('head')
- head_loss: float32 [24], P('head')
The draws below stay inside these ranges and needn't reach their ends.
All inputs are finite; a program needn't handle non-finite values.
Results may differ from the reference program's by a relative error of at most 0.0012.
Values may be sent and summed in bfloat16 or wider, within the bound.
No kernel may reach another device: no remote copies, remote signals or barrier semaphores. Data moves between devices by JAX's collectives and lax.ppermute only.
A program may use at most 64 MiB of HBM per device.

```python
import math
import jax
import jax.numpy as jnp
from jax import lax

HEADS_T = 24
HD_T = 128
HEADS_S = 8
HD_S = 64
SEQ = 512
IMAGES = 4
N_HEAD = 2


def paired(key, width):
    extent = (IMAGES, SEQ, width)
    draw_one, draw_two = jax.random.split(key, 2)
    queries = jnp.clip(jax.random.normal(draw_one, extent, jnp.float32), -6.0, 6.0)
    key_rows = jnp.clip(jax.random.normal(draw_two, extent, jnp.float32), -6.0, 6.0)
    return (queries, key_rows)


def draw_teacher_query(key, part):
    return paired(jax.random.fold_in(key, 11), HEADS_T * HD_T)[0].astype(jnp.bfloat16)


def draw_teacher_key(key, part):
    return paired(jax.random.fold_in(key, 11), HEADS_T * HD_T)[1].astype(jnp.bfloat16)


def draw_student_query(key, part):
    return paired(jax.random.fold_in(key, 23), HEADS_S * HD_S)[0].astype(jnp.bfloat16)


def draw_student_key(key, part):
    return paired(jax.random.fold_in(key, 23), HEADS_S * HD_S)[1].astype(jnp.bfloat16)


def level_of(stream_key, dims, pieces, low, high):
    loudness, own = 1.0, jax.random.fold_in(stream_key, 6)
    for position, blocks in pieces:
        draws = jnp.exp(jax.random.uniform(jax.random.fold_in(own, position), (blocks,), jnp.float32, low / len(pieces), high / len(pieces)))
        loudness = loudness * jnp.repeat(draws, dims[position] // blocks).reshape([-1 if axis == position else 1 for axis in range(len(dims))])
    return loudness


def setup_inputs(seed: int = 0) -> dict:
    streams_of = jax.random.split(jax.random.key(seed), 6)
    teacher_query = draw_teacher_query(jax.random.fold_in(streams_of[5], 71), 0)
    teacher_key = draw_teacher_key(jax.random.fold_in(streams_of[5], 71), 0)
    student_query = draw_student_query(jax.random.fold_in(streams_of[5], 71), 0)
    student_key = draw_student_key(jax.random.fold_in(streams_of[5], 71), 0)
    head_mix = jnp.clip(jnp.exp(math.log(0.25) - 2.5257287 * jax.random.uniform(streams_of[4], (HEADS_T, HEADS_S), jnp.float32) ** level_of(streams_of[4], (HEADS_T, HEADS_S), ((0, 2),), -0.2, 0.2)), 0.02, 0.25)
    return dict(teacher_query=teacher_query, teacher_key=teacher_key, student_query=student_query, student_key=student_key, head_mix=head_mix)


HIGHEST = lax.Precision.HIGHEST


def one_image(query_t, key_t, query_s, key_s, head_mix):
    per_group = HEADS_T // N_HEAD
    block_rows = min(SEQ, 128)
    block_count = SEQ // block_rows
    all_query_t = query_t.astype(jnp.float32).reshape(SEQ, HEADS_T, HD_T)
    all_key_t = key_t.astype(jnp.float32).reshape(SEQ, HEADS_T, HD_T)
    all_query_s = query_s.astype(jnp.float32).reshape(SEQ, HEADS_S, HD_S)
    all_key_s = key_s.astype(jnp.float32).reshape(SEQ, HEADS_S, HD_S)
    mix_groups = head_mix.reshape(N_HEAD, per_group, HEADS_S)

    def visit(carry, index):
        key_grad, mix_grad = carry
        start = index * block_rows
        rows_t = lax.dynamic_slice_in_dim(all_query_t, start, block_rows, 0)
        rows_s = lax.dynamic_slice_in_dim(all_query_s, start, block_rows, 0)
        teacher = jnp.einsum("rhd,khd->hrk", rows_t, all_key_t, precision=HIGHEST) * HD_T ** -0.5
        student = jnp.einsum("rhd,khd->hrk", rows_s, all_key_s, precision=HIGHEST) * HD_S ** -0.5
        lifted = jnp.einsum("th,hrk->trk", head_mix, student, precision=HIGHEST)
        lse_t = jax.nn.logsumexp(teacher, axis=-1)
        lse_l = jax.nn.logsumexp(lifted, axis=-1)
        prob_t = jnp.exp(teacher - lse_t[..., None])
        prob_l = jnp.exp(lifted - lse_l[..., None])
        kl_rows = jnp.sum(prob_t * (teacher - lifted), axis=-1) - lse_t + lse_l
        excess = prob_l - prob_t
        mix_grad = mix_grad + jnp.einsum("trk,hrk->th", excess, student, precision=HIGHEST)
        grouped = jnp.einsum("gth,gtrk->ghrk", mix_groups, excess.reshape(N_HEAD, per_group, block_rows, SEQ), precision=HIGHEST)
        narrow = lax.optimization_barrier(grouped.astype(jnp.bfloat16))
        summed = jnp.sum(narrow.astype(jnp.float32), axis=0)
        query_grad = jnp.einsum("hrk,khd->rhd", summed, all_key_s, precision=HIGHEST).reshape(block_rows, HEADS_S * HD_S)
        key_grad = key_grad + jnp.einsum("hrk,rhd->khd", summed, rows_s, precision=HIGHEST)
        return (key_grad, mix_grad), (query_grad, jnp.sum(kl_rows, axis=-1))

    initial = (jnp.zeros((SEQ, HEADS_S, HD_S), jnp.float32), jnp.zeros((HEADS_T, HEADS_S), jnp.float32))
    (key_grad, mix_grad), (query_grads, losses) = lax.scan(visit, initial, jnp.arange(block_count, dtype=jnp.int32))
    return query_grads.reshape(SEQ, HEADS_S * HD_S), key_grad.reshape(SEQ, HEADS_S * HD_S), mix_grad, jnp.sum(losses, axis=0)


def reference(teacher_query, teacher_key, student_query, student_key, head_mix):
    weight = SEQ / HEADS_T
    factor = weight * HD_S ** -0.5
    outcomes = [one_image(teacher_query[image], teacher_key[image], student_query[image], student_key[image], head_mix) for image in range(IMAGES)]
    grad_query = jnp.stack([outcome[0] for outcome in outcomes]) * factor
    grad_key = jnp.stack([outcome[1] for outcome in outcomes]) * factor
    mix_total = jnp.sum(jnp.stack([outcome[2] for outcome in outcomes]), axis=0)
    loss_total = jnp.sum(jnp.stack([outcome[3] for outcome in outcomes]), axis=0)
    grad_mix = mix_total * (weight / (IMAGES * SEQ))
    head_loss = loss_total / (IMAGES * SEQ)
    return grad_query, grad_key, grad_mix, head_loss
```

```python
import functools
import math

import jax
import jax.numpy as jnp
from jax import lax
from jax.experimental import pallas as pl
from jax.experimental.pallas import tpu as pltpu
from jax.sharding import PartitionSpec as P

HEADS_T = 24
HD_T = 128
HEADS_S = 8
HD_S = 64
LOG2E = math.log2(math.e)
LN2 = math.log(2.0)
LIFT_BLOCK = 32
BACK_BLOCK = 16
VMEM_LIMIT = 40 * 1024 * 1024

F32 = jnp.float32
BF16 = jnp.bfloat16


def dot(lhs, rhs, dims=((1,), (0,))):
    return lax.dot_general(lhs, rhs, (dims, ((), ())), preferred_element_type=F32)


def split(value):
    high = value.astype(BF16)
    low = (value - high.astype(F32)).astype(BF16)
    return high, low


def expand_kernel(mix_ref, mix_tr_ref, lift_hi, lift_lo, back_hi, back_lo):
    def kron(values, size):
        rows, columns = values.shape
        lane = lax.broadcasted_iota(jnp.int32, (rows, columns * size), 1)
        spread = jnp.zeros((rows, columns * size), F32)
        for index in range(columns):
            inside = (lane >= index * size) & (lane < (index + 1) * size)
            spread = jnp.where(inside, values[:, index : index + 1], spread)
        full = (rows, size, columns * size)
        sub = lax.broadcasted_iota(jnp.int32, full, 1)
        within = lax.broadcasted_iota(jnp.int32, full, 2) & (size - 1)
        picked = jnp.where(sub == within, spread[:, None, :], 0.0)
        return picked.reshape(rows * size, columns * size)

    scaled = mix_ref[...] * (HD_S ** (-0.5) * LOG2E)
    lift_hi[...], lift_lo[...] = split(kron(scaled, LIFT_BLOCK))
    back_hi[...], back_lo[...] = split(kron(mix_tr_ref[...], BACK_BLOCK))


def expand_mix(head_mix):
    heads = head_mix.shape[0]
    lift = jax.ShapeDtypeStruct((heads * LIFT_BLOCK, HEADS_S * LIFT_BLOCK), BF16)
    back = jax.ShapeDtypeStruct((HEADS_S * BACK_BLOCK, heads * BACK_BLOCK), BF16)
    return pl.pallas_call(expand_kernel, out_shape=(lift, lift, back, back))(head_mix, head_mix.T)


def stacked(refs, columns):
    parts = [ref[0, :, columns] for ref in refs]
    return parts[0] if len(parts) == 1 else jnp.concatenate(parts, axis=0)


def maps_kernel(row_parts, key_parts, heads, *refs):
    refs = list(refs)
    query_t = [refs.pop(0) for _ in range(row_parts)]
    key_t = [refs.pop(0) for _ in range(key_parts)]
    query_s = [refs.pop(0) for _ in range(row_parts)]
    key_s = [refs.pop(0) for _ in range(key_parts)]
    lift_hi, lift_lo, exp_t, exp_l, stu_hi, stu_lo, top, lse, kl, lifted = refs
    keys = stu_hi.shape[1]
    rows = stu_hi.shape[2]
    for index in range(HEADS_S):
        columns = slice(index * HD_S, (index + 1) * HD_S)
        student = dot(stacked(key_s, columns), stacked(query_s, columns), ((1,), (1,)))
        stu_hi[index], stu_lo[index] = split(student)
    for start in range(0, keys, LIFT_BLOCK):
        block = slice(start, start + LIFT_BLOCK)
        high = stu_hi[:, block, :].reshape(HEADS_S * LIFT_BLOCK, rows)
        low = stu_lo[:, block, :].reshape(HEADS_S * LIFT_BLOCK, rows)
        total = dot(lift_hi[...], high) + (dot(lift_hi[...], low) + dot(lift_lo[...], high))
        lifted[:, block, :] = total.reshape(heads, LIFT_BLOCK, rows)
    for head in range(heads):
        columns = slice(head * HD_T, (head + 1) * HD_T)
        teacher = dot(stacked(key_t, columns), stacked(query_t, columns), ((1,), (1,)))
        teacher = teacher * (HD_T ** (-0.5) * LOG2E)
        top_t = jnp.max(teacher, axis=0, keepdims=True)
        prob_t = jnp.exp2(teacher - top_t)
        exp_t[head] = prob_t
        mixed = lifted[head]
        kl[head : head + 1, :] = jnp.sum(prob_t * (teacher - mixed), axis=0, keepdims=True)
        top_l = jnp.max(mixed, axis=0, keepdims=True)
        prob_l = jnp.exp2(mixed - top_l)
        exp_l[head] = prob_l
        top[0, head : head + 1, :] = top_t
        top[1, head : head + 1, :] = top_l
        lse[0, head : head + 1, :] = top_t + jnp.log2(jnp.sum(prob_t, axis=0, keepdims=True))
        lse[1, head : head + 1, :] = top_l + jnp.log2(jnp.sum(prob_l, axis=0, keepdims=True))


def back_kernel(row_parts, key_parts, heads, head_axis, factor, *refs):
    refs = list(refs)
    query_s = [refs.pop(0) for _ in range(row_parts)]
    key_s = [refs.pop(0) for _ in range(key_parts)]
    lse = [refs.pop(0) for _ in range(row_parts)]
    back_hi, back_lo, exp_t, exp_l, stu_hi, stu_lo, top, kl = refs[:8]
    refs = refs[8:]
    scale_t, scale_l, back, query_h, key_h, mix_acc = refs[-6:]
    sums = refs[0]
    pieces = refs[1:-6]
    shards = len(pieces) // (row_parts + key_parts)
    keys, rows = stu_hi.shape[1:]
    part = rows // row_parts

    lse_all = []
    for which in range(2):
        parts = [ref[which] for ref in lse]
        best = functools.reduce(jnp.maximum, parts)
        total = sum(jnp.exp2(value - best) for value in parts)
        lse_all.append(best + jnp.log2(total))
    scale_t[...] = jnp.exp2(top[0] - lse_all[0])
    scale_l[...] = jnp.exp2(top[1] - lse_all[1])
    own = lax.broadcasted_iota(jnp.int32, (heads, rows), 1) < part
    loss = scale_t[...] * kl[...] + jnp.where(own, lse_all[1] - lse_all[0], 0.0)
    loss = jnp.sum(loss, axis=1, keepdims=True) * LN2

    mix_acc[...] = jnp.zeros_like(mix_acc)
    for start in range(0, keys, LIFT_BLOCK):
        block = slice(start, start + LIFT_BLOCK)
        excess = exp_l[:, block, :] * scale_l[...][:, None, :] - exp_t[:, block, :] * scale_t[...][:, None, :]
        high, low = split(excess)
        s_high = stu_hi[:, block, :].reshape(HEADS_S * LIFT_BLOCK, rows)
        s_low = stu_lo[:, block, :].reshape(HEADS_S * LIFT_BLOCK, rows)
        f_high = high.reshape(heads * LIFT_BLOCK, rows)
        f_low = low.reshape(heads * LIFT_BLOCK, rows)
        over_rows = ((1,), (1,))
        mix_acc[...] += dot(f_high, s_high, over_rows) + (
            dot(f_high, s_low, over_rows) + dot(f_low, s_high, over_rows)
        )
        for inner in range(0, LIFT_BLOCK, BACK_BLOCK):
            b_high = high[:, inner : inner + BACK_BLOCK, :].reshape(heads * BACK_BLOCK, rows)
            b_low = low[:, inner : inner + BACK_BLOCK, :].reshape(heads * BACK_BLOCK, rows)
            total = dot(back_hi[...], b_high) + (dot(back_hi[...], b_low) + dot(back_lo[...], b_high))
            back[:, start + inner : start + inner + BACK_BLOCK, :] = total.astype(BF16).reshape(
                HEADS_S, BACK_BLOCK, rows
            )

    acc = mix_acc[...].reshape(heads, LIFT_BLOCK, HEADS_S * LIFT_BLOCK)
    sub = lax.broadcasted_iota(jnp.int32, acc.shape, 1)
    within = lax.broadcasted_iota(jnp.int32, acc.shape, 2) & (LIFT_BLOCK - 1)
    diagonal = jnp.sum(jnp.where(sub == within, acc, 0.0), axis=1)
    lane = lax.broadcasted_iota(jnp.int32, diagonal.shape, 1)
    slot = lax.broadcasted_iota(jnp.int32, sums.shape, 1)
    packed = jnp.where(slot == HEADS_S, loss, 0.0)
    for index in range(HEADS_S):
        inside = (lane >= index * LIFT_BLOCK) & (lane < (index + 1) * LIFT_BLOCK)
        column = jnp.sum(jnp.where(inside, diagonal, 0.0), axis=1, keepdims=True)
        packed = jnp.where(slot == index, column, packed)
    sums[...] = packed

    for index in range(HEADS_S):
        columns = slice(index * HD_S, (index + 1) * HD_S)
        query_h[index] = stacked(query_s, columns)
        key_h[index] = stacked(key_s, columns)
    place = lax.axis_index(head_axis)
    per = HEADS_S // shards
    for shard in range(shards):
        first = lax.rem(place + shard, shards) * per
        for index in range(per):
            tile = back[first + index]
            columns = slice(index * HD_S, (index + 1) * HD_S)
            on_keys = dot(tile, query_h[first + index]) * factor
            on_rows = dot(tile, key_h[first + index], ((0,), (0,))) * factor
            for spot in range(row_parts):
                ref = pieces[shard * row_parts + spot]
                ref[:, columns] = on_rows[spot * part : (spot + 1) * part]
            size = keys // key_parts
            for spot in range(key_parts):
                ref = pieces[shards * row_parts + shard * key_parts + spot]
                ref[:, columns] = on_keys[spot * size : (spot + 1) * size]


def body(teacher_query, teacher_key, student_query, student_key, head_mix):
    shard_rows = teacher_query.shape[1]
    heads = head_mix.shape[0]
    length = lax.axis_size("seq")
    shards = lax.axis_size("head")
    copies = lax.axis_size("dp")
    row_parts = max(size for size in range(1, math.isqrt(length) + 1) if length % size == 0)
    key_parts = length // row_parts
    rows, keys = row_parts * shard_rows, key_parts * shard_rows

    def along_rows(position, step):
        return position // row_parts * row_parts + (position % row_parts + step) % row_parts

    def along_keys(position, step):
        return (position + step * row_parts) % length

    def fetch(value, target, step):
        return lax.ppermute(value, "seq", [(target(i, step), i) for i in range(length)])

    def deliver(value, target, step, turn):
        pairs = [
            (h * length + i, (h + turn) % shards * length + target(i, step))
            for h in range(shards)
            for i in range(length)
        ]
        return lax.ppermute(value, ("head", "seq"), pairs)

    key_s = [student_key] + [fetch(student_key, along_keys, d) for d in range(1, key_parts)]
    query_s = [student_query] + [fetch(student_query, along_rows, d) for d in range(1, row_parts)]
    key_t = [teacher_key] + [fetch(teacher_key, along_keys, d) for d in range(1, key_parts)]
    query_t = [teacher_query] + [fetch(teacher_query, along_rows, d) for d in range(1, row_parts)]
    lift_hi, lift_lo, back_hi, back_lo = expand_mix(head_mix)

    maps = pltpu.VMEM((heads, keys, rows), F32)
    student = pltpu.VMEM((HEADS_S, keys, rows), BF16)
    stats = pltpu.VMEM((2, heads, rows), F32)
    exp_t, exp_l, stu_hi, stu_lo, top, lse, kl = pl.pallas_call(
        functools.partial(maps_kernel, row_parts, key_parts, heads),
        out_shape=(maps, maps, student, student, stats, stats, pltpu.VMEM((heads, rows), F32)),
        scratch_shapes=[pltpu.VMEM((heads, keys, rows), F32)],
        compiler_params=pltpu.CompilerParams(vmem_limit_bytes=VMEM_LIMIT),
        name="maps",
    )(*query_t, *key_t, *query_s, *key_s, lift_hi, lift_lo)

    lse_parts = [lse]
    for step in range(1, row_parts):
        turned = jnp.roll(lse.reshape(2, heads, row_parts, shard_rows), -step, axis=2)
        lse_parts.append(fetch(turned.reshape(lse.shape), along_rows, row_parts - step))

    weight = shard_rows * length / HEADS_T
    width = HEADS_S * HD_S // shards
    piece = jax.ShapeDtypeStruct((shard_rows, width), F32)
    count = shards * (row_parts + key_parts)
    sums, *pieces = pl.pallas_call(
        functools.partial(back_kernel, row_parts, key_parts, heads, "head", weight * HD_S ** (-0.5)),
        out_shape=(jax.ShapeDtypeStruct((heads, 128), F32),) + (piece,) * count,
        scratch_shapes=[
            pltpu.VMEM((heads, rows), F32),
            pltpu.VMEM((heads, rows), F32),
            pltpu.VMEM((HEADS_S, keys, rows), BF16),
            pltpu.VMEM((HEADS_S, rows, HD_S), BF16),
            pltpu.VMEM((HEADS_S, keys, HD_S), BF16),
            pltpu.VMEM((heads * LIFT_BLOCK, HEADS_S * LIFT_BLOCK), F32),
        ],
        compiler_params=pltpu.CompilerParams(vmem_limit_bytes=VMEM_LIMIT),
        name="back",
    )(*query_s, *key_s, *lse_parts, back_hi, back_lo, exp_t, exp_l, stu_hi, stu_lo, top, kl)

    def collect(parts, target, count):
        total = None
        for turn in range(shards):
            for step in range(count):
                part = parts[turn * count + step]
                if turn or step:
                    part = deliver(part, target, step, turn)
                total = part if total is None else total + part
        return total[None]

    def everyone(value, axis):
        size = lax.axis_size(axis)
        total = value
        for step in range(1, size):
            total = total + lax.ppermute(value, axis, [(i, (i + step) % size) for i in range(size)])
        return total

    grad_key = collect(pieces[shards * row_parts :], along_keys, key_parts)
    grad_query = collect(pieces[: shards * row_parts], along_rows, row_parts)
    total = everyone(everyone(sums, "dp"), "seq")
    samples = copies * teacher_query.shape[0] * shard_rows * length
    grad_mix = total[:, :HEADS_S] * (HD_S ** (-0.5) * weight / samples)
    head_loss = total[:, HEADS_S] / samples
    return (grad_query, grad_key, grad_mix, head_loss)


def solution(mesh):
    return jax.shard_map(
        body,
        mesh=mesh,
        in_specs=(
            P("dp", "seq", "head"),
            P("dp", "seq", "head"),
            P("dp", "seq", None),
            P("dp", "seq", None),
            P("head", None),
        ),
        out_specs=(P("dp", "seq", "head"), P("dp", "seq", "head"), P("head", None), P("head")),
        check_vma=False,
    )
```

```python
import functools
import math

import jax
import jax.numpy as jnp
from jax import lax
from jax.experimental import pallas as pl
from jax.experimental.pallas import tpu as pltpu
from jax.sharding import PartitionSpec as P

HEADS_T = 24
HD_T = 128
HEADS_S = 8
HD_S = 64
LOG2E = math.log2(math.e)
LN2 = math.log(2.0)
LIFT_BLOCK = 32
BACK_BLOCK = 16
VMEM_LIMIT = 8 * 1024 * 1024

F32 = jnp.float32
BF16 = jnp.bfloat16


def dot(lhs, rhs, dims=((1,), (0,))):
    return lax.dot_general(lhs, rhs, (dims, ((), ())), preferred_element_type=F32)


def split(value):
    high = value.astype(BF16)
    low = (value - high.astype(F32)).astype(BF16)
    return high, low


def expand_kernel(mix_ref, mix_tr_ref, lift_hi, lift_lo, back_hi, back_lo):
    def kron(values, size):
        rows, columns = values.shape
        lane = lax.broadcasted_iota(jnp.int32, (rows, columns * size), 1)
        spread = jnp.zeros((rows, columns * size), F32)
        for index in range(columns):
            inside = (lane >= index * size) & (lane < (index + 1) * size)
            spread = jnp.where(inside, values[:, index : index + 1], spread)
        full = (rows, size, columns * size)
        sub = lax.broadcasted_iota(jnp.int32, full, 1)
        within = lax.broadcasted_iota(jnp.int32, full, 2) & (size - 1)
        picked = jnp.where(sub == within, spread[:, None, :], 0.0)
        return picked.reshape(rows * size, columns * size)

    scaled = mix_ref[...] * (HD_S ** (-0.5) * LOG2E)
    lift_hi[...], lift_lo[...] = split(kron(scaled, LIFT_BLOCK))
    back_hi[...], back_lo[...] = split(kron(mix_tr_ref[...], BACK_BLOCK))


def expand_mix(head_mix):
    heads = head_mix.shape[0]
    lift = jax.ShapeDtypeStruct((heads * LIFT_BLOCK, HEADS_S * LIFT_BLOCK), BF16)
    back = jax.ShapeDtypeStruct((HEADS_S * BACK_BLOCK, heads * BACK_BLOCK), BF16)
    return pl.pallas_call(
        expand_kernel,
        out_shape=(lift, lift, back, back),
        compiler_params=pltpu.CompilerParams(vmem_limit_bytes=VMEM_LIMIT // 2),
        name="expand",
    )(head_mix, head_mix.T)


def stacked(refs, columns):
    parts = [ref[0, :, columns] for ref in refs]
    return parts[0] if len(parts) == 1 else jnp.concatenate(parts, axis=0)


def maps_kernel(row_parts, key_parts, heads, *refs):
    refs = list(refs)
    query_t = [refs.pop(0) for _ in range(row_parts)]
    key_t = [refs.pop(0) for _ in range(key_parts)]
    query_s = [refs.pop(0) for _ in range(row_parts)]
    key_s = [refs.pop(0) for _ in range(key_parts)]
    lift_hi, lift_lo, exp_t, exp_l, stu_hi, stu_lo, top, kl, lse, *turned, lifted = refs
    keys = stu_hi.shape[1]
    rows = stu_hi.shape[2]
    for index in range(HEADS_S):
        columns = slice(index * HD_S, (index + 1) * HD_S)
        student = dot(stacked(key_s, columns), stacked(query_s, columns), ((1,), (1,)))
        stu_hi[index], stu_lo[index] = split(student)
    for start in range(0, keys, LIFT_BLOCK):
        block = slice(start, start + LIFT_BLOCK)
        high = stu_hi[:, block, :].reshape(HEADS_S * LIFT_BLOCK, rows)
        low = stu_lo[:, block, :].reshape(HEADS_S * LIFT_BLOCK, rows)
        total = dot(lift_hi[...], high) + (dot(lift_hi[...], low) + dot(lift_lo[...], high))
        lifted[:, block, :] = total.reshape(heads, LIFT_BLOCK, rows)
    for head in range(heads):
        columns = slice(head * HD_T, (head + 1) * HD_T)
        teacher = dot(stacked(key_t, columns), stacked(query_t, columns), ((1,), (1,)))
        teacher = teacher * (HD_T ** (-0.5) * LOG2E)
        top_t = jnp.max(teacher, axis=0, keepdims=True)
        prob_t = jnp.exp2(teacher - top_t)
        exp_t[head] = prob_t
        mixed = lifted[head]
        kl[head : head + 1, :] = jnp.sum(prob_t * (teacher - mixed), axis=0, keepdims=True)
        top_l = jnp.max(mixed, axis=0, keepdims=True)
        prob_l = jnp.exp2(mixed - top_l)
        exp_l[head] = prob_l
        top[0, head : head + 1, :] = top_t
        top[1, head : head + 1, :] = top_l
        lse[0, head : head + 1, :] = top_t + jnp.log2(jnp.sum(prob_t, axis=0, keepdims=True))
        lse[1, head : head + 1, :] = top_l + jnp.log2(jnp.sum(prob_l, axis=0, keepdims=True))
    part = rows // row_parts
    for step, ref in enumerate(turned, 1):
        for spot in range(row_parts):
            source = (spot + step) % row_parts * part
            ref[:, :, spot * part : (spot + 1) * part] = lse[:, :, source : source + part]


def back_kernel(row_parts, key_parts, heads, head_axis, factor, *refs):
    refs = list(refs)
    query_s = [refs.pop(0) for _ in range(row_parts)]
    key_s = [refs.pop(0) for _ in range(key_parts)]
    lse = [refs.pop(0) for _ in range(row_parts)]
    back_hi, back_lo, exp_t, exp_l, stu_hi, stu_lo, top, kl = refs[:8]
    refs = refs[8:]
    scale_t, scale_l, back, query_h, key_h, mix_acc = refs[-6:]
    sums = refs[0]
    pieces = refs[1:-6]
    shards = len(pieces) // (row_parts + key_parts - 1)
    keys, rows = stu_hi.shape[1:]
    part = rows // row_parts

    lse_all = []
    for which in range(2):
        parts = [ref[which] for ref in lse]
        best = functools.reduce(jnp.maximum, parts)
        total = sum(jnp.exp2(value - best) for value in parts)
        lse_all.append(best + jnp.log2(total))
    scale_t[...] = jnp.exp2(top[0] - lse_all[0])
    scale_l[...] = jnp.exp2(top[1] - lse_all[1])
    own = lax.broadcasted_iota(jnp.int32, (heads, rows), 1) < part
    loss = scale_t[...] * kl[...] + jnp.where(own, lse_all[1] - lse_all[0], 0.0)
    loss = jnp.sum(loss, axis=1, keepdims=True) * LN2

    mix_acc[...] = jnp.zeros_like(mix_acc)
    for start in range(0, keys, LIFT_BLOCK):
        block = slice(start, start + LIFT_BLOCK)
        excess = exp_l[:, block, :] * scale_l[...][:, None, :] - exp_t[:, block, :] * scale_t[...][:, None, :]
        high, low = split(excess)
        s_high = stu_hi[:, block, :].reshape(HEADS_S * LIFT_BLOCK, rows)
        s_low = stu_lo[:, block, :].reshape(HEADS_S * LIFT_BLOCK, rows)
        f_high = high.reshape(heads * LIFT_BLOCK, rows)
        f_low = low.reshape(heads * LIFT_BLOCK, rows)
        over_rows = ((1,), (1,))
        mix_acc[...] += dot(f_high, s_high, over_rows) + (
            dot(f_high, s_low, over_rows) + dot(f_low, s_high, over_rows)
        )
        for inner in range(0, LIFT_BLOCK, BACK_BLOCK):
            b_high = high[:, inner : inner + BACK_BLOCK, :].reshape(heads * BACK_BLOCK, rows)
            b_low = low[:, inner : inner + BACK_BLOCK, :].reshape(heads * BACK_BLOCK, rows)
            total = dot(back_hi[...], b_high) + (dot(back_hi[...], b_low) + dot(back_lo[...], b_high))
            back[:, start + inner : start + inner + BACK_BLOCK, :] = total.astype(BF16).reshape(
                HEADS_S, BACK_BLOCK, rows
            )

    acc = mix_acc[...].reshape(heads, LIFT_BLOCK, HEADS_S * LIFT_BLOCK)
    sub = lax.broadcasted_iota(jnp.int32, acc.shape, 1)
    within = lax.broadcasted_iota(jnp.int32, acc.shape, 2) & (LIFT_BLOCK - 1)
    diagonal = jnp.sum(jnp.where(sub == within, acc, 0.0), axis=1)
    lane = lax.broadcasted_iota(jnp.int32, diagonal.shape, 1)
    slot = lax.broadcasted_iota(jnp.int32, sums.shape, 1)
    packed = jnp.where(slot == HEADS_S, loss, 0.0)
    for index in range(HEADS_S):
        inside = (lane >= index * LIFT_BLOCK) & (lane < (index + 1) * LIFT_BLOCK)
        column = jnp.sum(jnp.where(inside, diagonal, 0.0), axis=1, keepdims=True)
        packed = jnp.where(slot == index, column, packed)
    sums[...] = packed

    for index in range(HEADS_S):
        columns = slice(index * HD_S, (index + 1) * HD_S)
        query_h[index] = stacked(query_s, columns)
        key_h[index] = stacked(key_s, columns)
    place = lax.axis_index(head_axis)
    per = HEADS_S // shards
    for shard in range(shards):
        first = lax.rem(place + shard, shards) * per
        for index in range(per):
            tile = back[first + index]
            columns = slice(index * HD_S, (index + 1) * HD_S)
            on_keys = dot(tile, query_h[first + index]) * factor
            on_rows = dot(tile, key_h[first + index], ((0,), (0,))) * factor
            size = keys // key_parts
            own, *others = pieces[shard * (row_parts + key_parts - 1) :][: row_parts + key_parts - 1]
            own[:part, columns] = on_rows[:part]
            own[part:, columns] = on_keys[:size]
            for spot in range(1, row_parts):
                others[spot - 1][:, columns] = on_rows[spot * part : (spot + 1) * part]
            for spot in range(1, key_parts):
                others[row_parts + spot - 2][:, columns] = on_keys[spot * size : (spot + 1) * size]


def finish_kernel(row_parts, key_parts, *refs):
    *pieces, grad_query, grad_key = refs
    count = row_parts + key_parts - 1
    part = grad_query.shape[1]
    own = pieces[::count]
    on_rows = [ref for i, ref in enumerate(pieces) if 0 < i % count < row_parts]
    on_keys = [ref for i, ref in enumerate(pieces) if i % count >= row_parts]
    grad_query[0] = sum([ref[...] for ref in on_rows], sum([ref[:part] for ref in own[1:]], own[0][:part]))
    grad_key[0] = sum([ref[...] for ref in on_keys], sum([ref[part:] for ref in own[1:]], own[0][part:]))


def body(teacher_query, teacher_key, student_query, student_key, head_mix):
    shard_rows = teacher_query.shape[1]
    heads = head_mix.shape[0]
    length = lax.axis_size("seq")
    shards = lax.axis_size("head")
    copies = lax.axis_size("dp")
    row_parts = max(size for size in range(1, math.isqrt(length) + 1) if length % size == 0)
    key_parts = length // row_parts
    rows, keys = row_parts * shard_rows, key_parts * shard_rows

    def along_rows(position, step):
        return position // row_parts * row_parts + (position % row_parts + step) % row_parts

    def along_keys(position, step):
        return (position + step * row_parts) % length

    def fetch(value, target, step):
        return lax.ppermute(value, "seq", [(target(i, step), i) for i in range(length)])

    def deliver(value, target, step, turn):
        pairs = [
            (h * length + i, (h + turn) % shards * length + target(i, step))
            for h in range(shards)
            for i in range(length)
        ]
        return lax.ppermute(value, ("head", "seq"), pairs)

    key_s = [student_key] + [fetch(student_key, along_keys, d) for d in range(1, key_parts)]
    query_s = [student_query] + [fetch(student_query, along_rows, d) for d in range(1, row_parts)]
    key_t = [teacher_key] + [fetch(teacher_key, along_keys, d) for d in range(1, key_parts)]
    query_t = [teacher_query] + [fetch(teacher_query, along_rows, d) for d in range(1, row_parts)]
    lift_hi, lift_lo, back_hi, back_lo = expand_mix(head_mix)

    maps = pltpu.VMEM((heads, keys, rows), F32)
    student = pltpu.VMEM((HEADS_S, keys, rows), BF16)
    stats = pltpu.VMEM((2, heads, rows), F32)
    exp_t, exp_l, stu_hi, stu_lo, top, kl, lse, *turned = pl.pallas_call(
        functools.partial(maps_kernel, row_parts, key_parts, heads),
        out_shape=(maps, maps, student, student, stats, pltpu.VMEM((heads, rows), F32)) + (stats,) * row_parts,
        scratch_shapes=[pltpu.VMEM((heads, keys, rows), F32)],
        compiler_params=pltpu.CompilerParams(vmem_limit_bytes=VMEM_LIMIT),
        name="maps",
    )(*query_t, *key_t, *query_s, *key_s, lift_hi, lift_lo)

    lse_parts = [lse] + [fetch(turned[step - 1], along_rows, row_parts - step) for step in range(1, row_parts)]

    weight = shard_rows * length / HEADS_T
    width = HEADS_S * HD_S // shards
    own = jax.ShapeDtypeStruct((2 * shard_rows, width), F32)
    piece = jax.ShapeDtypeStruct((shard_rows, width), F32)
    shapes = ((own,) + (piece,) * (row_parts + key_parts - 2)) * shards
    sums, *pieces = pl.pallas_call(
        functools.partial(back_kernel, row_parts, key_parts, heads, "head", weight * HD_S ** (-0.5)),
        out_shape=(jax.ShapeDtypeStruct((heads, 128), F32),) + shapes,
        scratch_shapes=[
            pltpu.VMEM((heads, rows), F32),
            pltpu.VMEM((heads, rows), F32),
            pltpu.VMEM((HEADS_S, keys, rows), BF16),
            pltpu.VMEM((HEADS_S, rows, HD_S), BF16),
            pltpu.VMEM((HEADS_S, keys, HD_S), BF16),
            pltpu.VMEM((heads * LIFT_BLOCK, HEADS_S * LIFT_BLOCK), F32),
        ],
        compiler_params=pltpu.CompilerParams(vmem_limit_bytes=VMEM_LIMIT),
        name="back",
    )(*query_s, *key_s, *lse_parts, back_hi, back_lo, exp_t, exp_l, stu_hi, stu_lo, top, kl)

    moves = [(along_rows, step) for step in range(row_parts)] + [(along_keys, step) for step in range(1, key_parts)]
    arrived = [
        deliver(part, *moves[i % len(moves)], i // len(moves)) if i else part for i, part in enumerate(pieces)
    ]
    grad = jax.ShapeDtypeStruct((1, shard_rows, width), F32)
    grad_query, grad_key = pl.pallas_call(
        functools.partial(finish_kernel, row_parts, key_parts),
        out_shape=(grad, grad),
        compiler_params=pltpu.CompilerParams(vmem_limit_bytes=VMEM_LIMIT),
        name="finish",
    )(*arrived)

    def everyone(value, axis):
        size = lax.axis_size(axis)
        if size & (size - 1) == 0:
            for bit in range(size.bit_length() - 1):
                value = value + lax.ppermute(value, axis, [(i, i ^ (1 << bit)) for i in range(size)])
            return value
        total = value
        for step in range(1, size):
            total = total + lax.ppermute(value, axis, [(i, (i + step) % size) for i in range(size)])
        return total

    total = everyone(everyone(sums, "dp"), "seq")
    samples = copies * teacher_query.shape[0] * shard_rows * length
    grad_mix = total[:, :HEADS_S] * (HD_S ** (-0.5) * weight / samples)
    head_loss = total[:, HEADS_S] / samples
    return (grad_query, grad_key, grad_mix, head_loss)


def solution(mesh):
    return jax.shard_map(
        body,
        mesh=mesh,
        in_specs=(
            P("dp", "seq", "head"),
            P("dp", "seq", "head"),
            P("dp", "seq", None),
            P("dp", "seq", None),
            P("head", None),
        ),
        out_specs=(P("dp", "seq", "head"), P("dp", "seq", "head"), P("head", None), P("head")),
        check_vma=False,
    )
```

```python
import functools
import math

import jax
import jax.numpy as jnp
from jax import lax
from jax.experimental import pallas as pl
from jax.experimental.pallas import tpu as pltpu
from jax.sharding import PartitionSpec as P

HEADS_T = 24
HD_T = 128
HEADS_S = 8
HD_S = 64
LOG2E = math.log2(math.e)
LN2 = math.log(2.0)
LIFT_BLOCK = 32
BACK_BLOCK = 16
VMEM_LIMIT = 8 * 1024 * 1024

F32 = jnp.float32
BF16 = jnp.bfloat16


def dot(lhs, rhs, dims=((1,), (0,))):
    return lax.dot_general(lhs, rhs, (dims, ((), ())), preferred_element_type=F32)


def split(value):
    high = value.astype(BF16)
    low = (value - high.astype(F32)).astype(BF16)
    return high, low


def expand_kernel(mix_ref, mix_tr_ref, lift_hi, lift_lo, back_hi, back_lo):
    def kron(values, size):
        rows, columns = values.shape
        lane = lax.broadcasted_iota(jnp.int32, (rows, columns * size), 1)
        spread = jnp.zeros((rows, columns * size), F32)
        for index in range(columns):
            inside = (lane >= index * size) & (lane < (index + 1) * size)
            spread = jnp.where(inside, values[:, index : index + 1], spread)
        full = (rows, size, columns * size)
        sub = lax.broadcasted_iota(jnp.int32, full, 1)
        within = lax.broadcasted_iota(jnp.int32, full, 2) & (size - 1)
        picked = jnp.where(sub == within, spread[:, None, :], 0.0)
        return picked.reshape(rows * size, columns * size)

    scaled = mix_ref[...] * (HD_S ** (-0.5) * LOG2E)
    lift_hi[...], lift_lo[...] = split(kron(scaled, LIFT_BLOCK))
    back_hi[...], back_lo[...] = split(kron(mix_tr_ref[...], BACK_BLOCK))


def expand_mix(head_mix):
    heads = head_mix.shape[0]
    lift = jax.ShapeDtypeStruct((heads * LIFT_BLOCK, HEADS_S * LIFT_BLOCK), BF16)
    back = jax.ShapeDtypeStruct((HEADS_S * BACK_BLOCK, heads * BACK_BLOCK), BF16)
    return pl.pallas_call(
        expand_kernel,
        out_shape=(lift, lift, back, back),
        compiler_params=pltpu.CompilerParams(vmem_limit_bytes=VMEM_LIMIT // 2),
        name="expand",
    )(head_mix, head_mix.T)


def stacked(refs, columns):
    parts = [ref[0, :, columns] for ref in refs]
    return parts[0] if len(parts) == 1 else jnp.concatenate(parts, axis=0)


def maps_kernel(row_parts, key_parts, heads, carried, *refs):
    refs = list(refs)
    query_t = [refs.pop(0) for _ in range(row_parts)]
    key_t = [refs.pop(0) for _ in range(key_parts)]
    query_s = [refs.pop(0) for _ in range(row_parts)]
    key_s = [refs.pop(0) for _ in range(key_parts)]
    before = refs.pop(0) if carried else None
    lift_hi, lift_lo, exp_t, exp_l, stu_hi, stu_lo, top, kl, lse, *turned, lifted = refs
    keys = stu_hi.shape[1]
    rows = stu_hi.shape[2]
    for index in range(HEADS_S):
        columns = slice(index * HD_S, (index + 1) * HD_S)
        student = dot(stacked(key_s, columns), stacked(query_s, columns), ((1,), (1,)))
        stu_hi[index], stu_lo[index] = split(student)
    for start in range(0, keys, LIFT_BLOCK):
        block = slice(start, start + LIFT_BLOCK)
        high = stu_hi[:, block, :].reshape(HEADS_S * LIFT_BLOCK, rows)
        low = stu_lo[:, block, :].reshape(HEADS_S * LIFT_BLOCK, rows)
        total = dot(lift_hi[...], high) + (dot(lift_hi[...], low) + dot(lift_lo[...], high))
        lifted[:, block, :] = total.reshape(heads, LIFT_BLOCK, rows)
    for head in range(heads):
        columns = slice(head * HD_T, (head + 1) * HD_T)
        teacher = dot(stacked(key_t, columns), stacked(query_t, columns), ((1,), (1,)))
        teacher = teacher * (HD_T ** (-0.5) * LOG2E)
        top_t = jnp.max(teacher, axis=0, keepdims=True)
        prob_t = jnp.exp2(teacher - top_t)
        exp_t[head] = prob_t
        mixed = lifted[head]
        kl[head : head + 1, :] = jnp.sum(prob_t * (teacher - mixed), axis=0, keepdims=True)
        top_l = jnp.max(mixed, axis=0, keepdims=True)
        prob_l = jnp.exp2(mixed - top_l)
        exp_l[head] = prob_l
        top[0, head : head + 1, :] = top_t
        top[1, head : head + 1, :] = top_l
        for which, best, prob in ((0, top_t, prob_t), (1, top_l, prob_l)):
            total = jnp.sum(prob, axis=0, keepdims=True)
            if carried:
                earlier = before[which, head : head + 1, :]
                higher = jnp.maximum(best, earlier)
                total = total * jnp.exp2(best - higher) + jnp.exp2(earlier - higher)
                best = higher
            lse[which, head : head + 1, :] = best + jnp.log2(total)
    part = rows // row_parts
    for step, ref in enumerate(turned, 1):
        for spot in range(row_parts):
            source = (spot + step) % row_parts * part
            ref[:, :, spot * part : (spot + 1) * part] = lse[:, :, source : source + part]


def back_kernel(row_parts, key_parts, blocks, heads, factor, *refs):
    refs = list(refs)
    query_s = [refs.pop(0) for _ in range(row_parts)]
    key_s = [refs.pop(0) for _ in range(key_parts)]
    lse = [refs.pop(0) for _ in range(row_parts)]
    back_hi, back_lo = refs[:2]
    maps = [refs[2 + 6 * i : 8 + 6 * i] for i in range(blocks)]
    sums, for_query, for_key, scale_t, scale_l, back, mix_acc = refs[2 + 6 * blocks :]
    keys, rows = back.shape[1:]
    part, size = rows // row_parts, keys // key_parts
    shards = for_query.shape[0] // row_parts

    lse_all = []
    for which in range(2):
        parts = [ref[which] for ref in lse]
        best = functools.reduce(jnp.maximum, parts)
        total = sum(jnp.exp2(value - best) for value in parts)
        lse_all.append(best + jnp.log2(total))
    own = lax.broadcasted_iota(jnp.int32, (heads, rows), 1) < part
    loss = jnp.where(own, lse_all[1] - lse_all[0], 0.0)
    mix_acc[...] = jnp.zeros_like(mix_acc)
    offset = 0
    for exp_t, exp_l, stu_hi, stu_lo, top, kl in maps:
        scale_t[...] = jnp.exp2(top[0] - lse_all[0])
        scale_l[...] = jnp.exp2(top[1] - lse_all[1])
        loss = loss + scale_t[...] * kl[...]
        for start in range(0, exp_t.shape[1], LIFT_BLOCK):
            block = slice(start, start + LIFT_BLOCK)
            excess = (
                exp_l[:, block, :] * scale_l[...][:, None, :] - exp_t[:, block, :] * scale_t[...][:, None, :]
            )
            high, low = split(excess)
            s_high = stu_hi[:, block, :].reshape(HEADS_S * LIFT_BLOCK, rows)
            s_low = stu_lo[:, block, :].reshape(HEADS_S * LIFT_BLOCK, rows)
            f_high = high.reshape(heads * LIFT_BLOCK, rows)
            f_low = low.reshape(heads * LIFT_BLOCK, rows)
            over_rows = ((1,), (1,))
            mix_acc[...] += dot(f_high, s_high, over_rows) + (
                dot(f_high, s_low, over_rows) + dot(f_low, s_high, over_rows)
            )
            for inner in range(0, LIFT_BLOCK, BACK_BLOCK):
                b_high = high[:, inner : inner + BACK_BLOCK, :].reshape(heads * BACK_BLOCK, rows)
                b_low = low[:, inner : inner + BACK_BLOCK, :].reshape(heads * BACK_BLOCK, rows)
                total = dot(back_hi[...], b_high) + (dot(back_hi[...], b_low) + dot(back_lo[...], b_high))
                first = offset + start + inner
                back[:, first : first + BACK_BLOCK, :] = total.astype(BF16).reshape(HEADS_S, BACK_BLOCK, rows)
        offset += exp_t.shape[1]
    loss = jnp.sum(loss, axis=1, keepdims=True) * LN2

    acc = mix_acc[...].reshape(heads, LIFT_BLOCK, HEADS_S * LIFT_BLOCK)
    sub = lax.broadcasted_iota(jnp.int32, acc.shape, 1)
    within = lax.broadcasted_iota(jnp.int32, acc.shape, 2) & (LIFT_BLOCK - 1)
    diagonal = jnp.sum(jnp.where(sub == within, acc, 0.0), axis=1)
    lane = lax.broadcasted_iota(jnp.int32, diagonal.shape, 1)
    slot = lax.broadcasted_iota(jnp.int32, sums.shape[1:], 1)
    packed = jnp.where(slot == HEADS_S, loss, 0.0)
    for index in range(HEADS_S):
        inside = (lane >= index * LIFT_BLOCK) & (lane < (index + 1) * LIFT_BLOCK)
        column = jnp.sum(jnp.where(inside, diagonal, 0.0), axis=1, keepdims=True)
        packed = jnp.where(slot == index, column, packed)
    sums[...] = jnp.broadcast_to(packed[None], sums.shape)

    place = lax.axis_index("seq")
    across, along = lax.rem(place, row_parts), lax.div(place, row_parts)
    per = HEADS_S // shards
    for index in range(HEADS_S):
        columns = slice(index * HD_S, (index + 1) * HD_S)
        tile = back[index]
        on_keys = dot(tile, stacked(query_s, columns)) * factor
        on_rows = dot(tile, stacked(key_s, columns), ((0,), (0,))) * factor
        shard, inside = index // per, slice(index % per * HD_S, (index % per + 1) * HD_S)
        for spot in range(row_parts):
            owner = shard * row_parts + lax.rem(across + spot, row_parts)
            for_query[owner, :, inside] = on_rows[spot * part : (spot + 1) * part]
        for spot in range(key_parts):
            owner = shard * key_parts + lax.rem(along + spot, key_parts)
            for_key[owner, :, inside] = on_keys[spot * size : (spot + 1) * size]


def finish_kernel(on_rows, on_keys, grad_query, grad_key):
    grad_query[0] = sum([on_rows[i] for i in range(1, on_rows.shape[0])], on_rows[0])
    grad_key[0] = sum([on_keys[i] for i in range(1, on_keys.shape[0])], on_keys[0])


def body(teacher_query, teacher_key, student_query, student_key, head_mix):
    shard_rows = teacher_query.shape[1]
    heads = head_mix.shape[0]
    length = lax.axis_size("seq")
    shards = lax.axis_size("head")
    copies = lax.axis_size("dp")
    row_parts = max(size for size in range(1, math.isqrt(length) + 1) if length % size == 0)
    key_parts = length // row_parts
    rows, keys = row_parts * shard_rows, key_parts * shard_rows

    def along_rows(position, step):
        return position // row_parts * row_parts + (position % row_parts + step) % row_parts

    def along_keys(position, step):
        return (position + step * row_parts) % length

    def fetch(value, target, step):
        return lax.ppermute(value, "seq", [(target(i, step), i) for i in range(length)])

    def swap(value, groups):
        return lax.all_to_all(value, ("head", "seq"), 0, 0, axis_index_groups=groups, tiled=True)

    key_s = [student_key] + [fetch(student_key, along_keys, d) for d in range(1, key_parts)]
    query_s = [student_query] + [fetch(student_query, along_rows, d) for d in range(1, row_parts)]
    key_t = [teacher_key] + [fetch(teacher_key, along_keys, d) for d in range(1, key_parts)]
    query_t = [teacher_query] + [fetch(teacher_query, along_rows, d) for d in range(1, row_parts)]
    lift_hi, lift_lo, back_hi, back_lo = expand_mix(head_mix)

    def maps(block_t, block_s, before):
        count = len(block_t)
        size = count * shard_rows
        exponents = pltpu.VMEM((heads, size, rows), F32)
        student = pltpu.VMEM((HEADS_S, size, rows), BF16)
        stats = pltpu.VMEM((2, heads, rows), F32)
        cells = heads * size * rows
        return pl.pallas_call(
            functools.partial(maps_kernel, row_parts, count, heads, bool(before)),
            out_shape=(exponents, exponents, student, student, stats, pltpu.VMEM((heads, rows), F32))
            + (stats,) * row_parts,
            scratch_shapes=[pltpu.VMEM((heads, size, rows), F32)],
            compiler_params=pltpu.CompilerParams(vmem_limit_bytes=VMEM_LIMIT),
            cost_estimate=pl.CostEstimate(
                flops=cells * 2 * (HD_T + 3 * LIFT_BLOCK * HEADS_S), bytes_accessed=cells * 8, transcendentals=cells * 2
            ),
            name="maps",
        )(*query_t, *block_t, *query_s, *block_s, *before, lift_hi, lift_lo)

    done, before = [], []
    for block in (slice(0, 1), slice(1, key_parts)):
        if key_t[block]:
            results = maps(key_t[block], key_s[block], before)
            done.append(results[:6])
            before, turned = results[6:7], results[7:]
    lse_parts = [*before] + [fetch(turned[step - 1], along_rows, row_parts - step) for step in range(1, row_parts)]

    weight = shard_rows * length / HEADS_T
    width = HEADS_S * HD_S // shards
    peers = length * copies
    sums, for_query, for_key = pl.pallas_call(
        functools.partial(back_kernel, row_parts, key_parts, len(done), heads, weight * HD_S ** (-0.5)),
        out_shape=(
            jax.ShapeDtypeStruct((peers, heads, 128), F32),
            jax.ShapeDtypeStruct((shards * row_parts, shard_rows, width), F32),
            jax.ShapeDtypeStruct((shards * key_parts, shard_rows, width), F32),
        ),
        scratch_shapes=[
            pltpu.VMEM((heads, rows), F32),
            pltpu.VMEM((heads, rows), F32),
            pltpu.VMEM((HEADS_S, keys, rows), BF16),
            pltpu.VMEM((heads * LIFT_BLOCK, HEADS_S * LIFT_BLOCK), F32),
        ],
        compiler_params=pltpu.CompilerParams(vmem_limit_bytes=VMEM_LIMIT),
        name="back",
    )(*query_s, *key_s, *lse_parts, back_hi, back_lo, *[ref for block in done for ref in block])

    row_groups = [
        [h * length + a * row_parts + b for h in range(shards) for b in range(row_parts)] for a in range(key_parts)
    ]
    key_groups = [
        [h * length + a * row_parts + b for h in range(shards) for a in range(key_parts)] for b in range(row_parts)
    ]
    for_query = swap(for_query, row_groups)
    for_key = swap(for_key, key_groups)
    grad = jax.ShapeDtypeStruct((1, shard_rows, width), F32)
    grad_query, grad_key = pl.pallas_call(
        finish_kernel,
        out_shape=(grad, grad),
        compiler_params=pltpu.CompilerParams(vmem_limit_bytes=VMEM_LIMIT),
        name="finish",
    )(for_query, for_key)
    total = jnp.sum(lax.all_to_all(sums, ("seq", "dp"), 0, 0, tiled=True), axis=0)
    samples = copies * teacher_query.shape[0] * shard_rows * length
    grad_mix = total[:, :HEADS_S] * (HD_S ** (-0.5) * weight / samples)
    head_loss = total[:, HEADS_S] / samples
    return (grad_query, grad_key, grad_mix, head_loss)


def solution(mesh):
    return jax.shard_map(
        body,
        mesh=mesh,
        in_specs=(
            P("dp", "seq", "head"),
            P("dp", "seq", "head"),
            P("dp", "seq", None),
            P("dp", "seq", None),
            P("head", None),
        ),
        out_specs=(P("dp", "seq", "head"), P("dp", "seq", "head"), P("head", None), P("head")),
        check_vma=False,
    )
```

```python
import functools
import math

import jax
import jax.numpy as jnp
from jax import lax
from jax.experimental import pallas as pl
from jax.experimental.pallas import tpu as pltpu
from jax.sharding import PartitionSpec as P

HEADS_T = 24
HD_T = 128
HEADS_S = 8
HD_S = 64
LOG2E = math.log2(math.e)
LN2 = math.log(2.0)
LIFT_BLOCK = 32
BACK_BLOCK = 16
RIDE_ROWS = 16
LANES = 128
VMEM_LIMIT = 8 * 1024 * 1024

F32 = jnp.float32
BF16 = jnp.bfloat16


def dot(lhs, rhs, dims=((1,), (0,))):
    return lax.dot_general(lhs, rhs, (dims, ((), ())), preferred_element_type=F32)


def split(value):
    high = value.astype(BF16)
    low = (value - high.astype(F32)).astype(BF16)
    return high, low


def prepare_kernel(count, mix_ref, mix_tr_ref, *refs):
    sources, targets = refs[:count], refs[count : 2 * count]
    lift_hi, lift_lo, back_hi, back_lo, semaphores = refs[2 * count :]
    moves = [pltpu.make_async_copy(sources[i], targets[i], semaphores.at[i]) for i in range(count)]
    for move in moves:
        move.start()

    def kron(values, size):
        rows, columns = values.shape
        lane = lax.broadcasted_iota(jnp.int32, (rows, columns * size), 1)
        spread = jnp.zeros((rows, columns * size), F32)
        for index in range(columns):
            inside = (lane >= index * size) & (lane < (index + 1) * size)
            spread = jnp.where(inside, values[:, index : index + 1], spread)
        full = (rows, size, columns * size)
        sub = lax.broadcasted_iota(jnp.int32, full, 1)
        within = lax.broadcasted_iota(jnp.int32, full, 2) & (size - 1)
        picked = jnp.where(sub == within, spread[:, None, :], 0.0)
        return picked.reshape(rows * size, columns * size)

    scaled = mix_ref[...] * (HD_S ** (-0.5) * LOG2E)
    lift_hi[...], lift_lo[...] = split(kron(scaled, LIFT_BLOCK))
    back_hi[...], back_lo[...] = split(kron(mix_tr_ref[...], BACK_BLOCK))
    for move in moves:
        move.wait()


def prepare(head_mix, arrays):
    heads = head_mix.shape[0]
    lift = pltpu.VMEM((heads * LIFT_BLOCK, HEADS_S * LIFT_BLOCK), BF16)
    back = pltpu.VMEM((HEADS_S * BACK_BLOCK, heads * BACK_BLOCK), BF16)
    count = len(arrays)
    whole = pl.BlockSpec(memory_space=pltpu.VMEM)
    return pl.pallas_call(
        functools.partial(prepare_kernel, count),
        out_shape=[pltpu.VMEM(array.shape, array.dtype) for array in arrays] + [lift, lift, back, back],
        in_specs=[whole, whole] + [pl.BlockSpec(memory_space=pl.ANY)] * count,
        scratch_shapes=[pltpu.SemaphoreType.DMA((count,))],
        compiler_params=pltpu.CompilerParams(vmem_limit_bytes=VMEM_LIMIT // 2),
        name="prepare",
    )(head_mix, head_mix.T, *arrays)


def stacked(refs, columns):
    parts = [ref[0, :, columns] for ref in refs]
    return parts[0] if len(parts) == 1 else jnp.concatenate(parts, axis=0)


def maps_kernel(row_parts, key_parts, heads, carried, *refs):
    refs = list(refs)
    key_t = [refs.pop(0) for _ in range(key_parts)]
    query_t = [refs.pop(0) for _ in range(row_parts)]
    key_s = [refs.pop(0) for _ in range(key_parts)]
    query_s = [refs.pop(0) for _ in range(row_parts)]
    before = refs.pop(0) if carried else None
    lift_hi, lift_lo, exp_t, exp_l, stu_hi, stu_lo, top, kl, lse, *turned, lifted = refs
    keys = stu_hi.shape[1]
    rows = stu_hi.shape[2]
    for index in range(HEADS_S):
        columns = slice(index * HD_S, (index + 1) * HD_S)
        student = dot(stacked(key_s, columns), stacked(query_s, columns), ((1,), (1,)))
        stu_hi[index], stu_lo[index] = split(student)
    for start in range(0, keys, LIFT_BLOCK):
        block = slice(start, start + LIFT_BLOCK)
        high = stu_hi[:, block, :].reshape(HEADS_S * LIFT_BLOCK, rows)
        low = stu_lo[:, block, :].reshape(HEADS_S * LIFT_BLOCK, rows)
        total = dot(lift_hi[...], high) + (dot(lift_hi[...], low) + dot(lift_lo[...], high))
        lifted[:, block, :] = total.reshape(heads, LIFT_BLOCK, rows)
    for head in range(heads):
        columns = slice(head * HD_T, (head + 1) * HD_T)
        teacher = dot(stacked(key_t, columns), stacked(query_t, columns), ((1,), (1,)))
        teacher = teacher * (HD_T ** (-0.5) * LOG2E)
        top_t = jnp.max(teacher, axis=0, keepdims=True)
        prob_t = jnp.exp2(teacher - top_t)
        exp_t[head] = prob_t
        mixed = lifted[head]
        kl[head : head + 1, :] = jnp.sum(prob_t * (teacher - mixed), axis=0, keepdims=True)
        top_l = jnp.max(mixed, axis=0, keepdims=True)
        prob_l = jnp.exp2(mixed - top_l)
        exp_l[head] = prob_l
        top[0, head : head + 1, :] = top_t
        top[1, head : head + 1, :] = top_l
        for which, best, prob in ((0, top_t, prob_t), (1, top_l, prob_l)):
            total = jnp.sum(prob, axis=0, keepdims=True)
            if carried:
                earlier = before[which, head : head + 1, :]
                higher = jnp.maximum(best, earlier)
                total = total * jnp.exp2(best - higher) + jnp.exp2(earlier - higher)
                best = higher
            lse[which, head : head + 1, :] = best + jnp.log2(total)
    part = rows // row_parts
    for step, ref in enumerate(turned, 1):
        for spot in range(row_parts):
            source = (spot + step) % row_parts * part
            ref[:, :, spot * part : (spot + 1) * part] = lse[:, :, source : source + part]


def back_kernel(row_parts, key_parts, shards, blocks, heads, factor, *refs):
    refs = list(refs)
    query_s = [refs.pop(0) for _ in range(row_parts)]
    key_s = [refs.pop(0) for _ in range(key_parts)]
    lse = [refs.pop(0) for _ in range(row_parts)]
    back_hi, back_lo = refs[:2]
    maps = [refs[2 + 6 * i : 8 + 6 * i] for i in range(blocks)]
    *outs, scale_t, scale_l, back, row_side, key_side, mix_acc = refs[2 + 6 * blocks :]
    keys, rows = back.shape[1:]
    part, size = rows // row_parts, keys // key_parts
    sums, pieces = outs[0], outs[1:]

    lse_all = []
    for which in range(2):
        parts = [ref[which] for ref in lse]
        best = functools.reduce(jnp.maximum, parts)
        total = sum(jnp.exp2(value - best) for value in parts)
        lse_all.append(best + jnp.log2(total))
    own = lax.broadcasted_iota(jnp.int32, (heads, rows), 1) < part
    loss = jnp.where(own, lse_all[1] - lse_all[0], 0.0)
    mix_acc[...] = jnp.zeros_like(mix_acc)
    offset = 0
    for exp_t, exp_l, stu_hi, stu_lo, top, kl in maps:
        scale_t[...] = jnp.exp2(top[0] - lse_all[0])
        scale_l[...] = jnp.exp2(top[1] - lse_all[1])
        loss = loss + scale_t[...] * kl[...]
        for start in range(0, exp_t.shape[1], LIFT_BLOCK):
            block = slice(start, start + LIFT_BLOCK)
            excess = (
                exp_l[:, block, :] * scale_l[...][:, None, :] - exp_t[:, block, :] * scale_t[...][:, None, :]
            )
            high, low = split(excess)
            s_high = stu_hi[:, block, :].reshape(HEADS_S * LIFT_BLOCK, rows)
            s_low = stu_lo[:, block, :].reshape(HEADS_S * LIFT_BLOCK, rows)
            f_high = high.reshape(heads * LIFT_BLOCK, rows)
            f_low = low.reshape(heads * LIFT_BLOCK, rows)
            over_rows = ((1,), (1,))
            mix_acc[...] += dot(f_high, s_high, over_rows) + (
                dot(f_high, s_low, over_rows) + dot(f_low, s_high, over_rows)
            )
            for inner in range(0, LIFT_BLOCK, BACK_BLOCK):
                b_high = high[:, inner : inner + BACK_BLOCK, :].reshape(heads * BACK_BLOCK, rows)
                b_low = low[:, inner : inner + BACK_BLOCK, :].reshape(heads * BACK_BLOCK, rows)
                total = dot(back_hi[...], b_high) + (dot(back_hi[...], b_low) + dot(back_lo[...], b_high))
                first = offset + start + inner
                back[:, first : first + BACK_BLOCK, :] = total.astype(BF16).reshape(HEADS_S, BACK_BLOCK, rows)
        offset += exp_t.shape[1]
    loss = jnp.sum(loss, axis=1, keepdims=True) * LN2

    acc = mix_acc[...].reshape(heads, LIFT_BLOCK, HEADS_S * LIFT_BLOCK)
    sub = lax.broadcasted_iota(jnp.int32, acc.shape, 1)
    within = lax.broadcasted_iota(jnp.int32, acc.shape, 2) & (LIFT_BLOCK - 1)
    diagonal = jnp.sum(jnp.where(sub == within, acc, 0.0), axis=1)
    lane = lax.broadcasted_iota(jnp.int32, diagonal.shape, 1)
    slot = lax.broadcasted_iota(jnp.int32, (heads, LANES), 1)
    packed = jnp.where(slot == HEADS_S, loss, 0.0)
    for index in range(HEADS_S):
        inside = (lane >= index * LIFT_BLOCK) & (lane < (index + 1) * LIFT_BLOCK)
        column = jnp.sum(jnp.where(inside, diagonal, 0.0), axis=1, keepdims=True)
        packed = jnp.where(slot == index, column, packed)
    packed = jnp.concatenate([packed, jnp.zeros((LANES - heads, LANES), F32)], axis=0)
    packed = jnp.transpose(packed)[:RIDE_ROWS]
    sums[...] = packed

    for index in range(HEADS_S):
        columns = slice(index * HD_S, (index + 1) * HD_S)
        row_side[index] = stacked(query_s, columns)
        key_side[index] = stacked(key_s, columns)
    place = lax.axis_index("head")
    per = HEADS_S // shards
    count = row_parts + key_parts - 1
    for shard in range(shards):
        own, *others = pieces[shard * count : (shard + 1) * count]
        first = lax.rem(place + shard, shards) * per
        for index in range(per):
            tile = back[first + index]
            columns = slice(index * HD_S, (index + 1) * HD_S)
            on_keys = dot(tile, row_side[first + index]) * factor
            on_rows = dot(tile, key_side[first + index], ((0,), (0,))) * factor
            own[:part, columns] = on_rows[:part]
            own[part:, columns] = on_keys[:size]
            for spot in range(1, row_parts):
                others[spot - 1][:part, columns] = on_rows[spot * part : (spot + 1) * part]
            for spot in range(1, key_parts):
                others[row_parts + spot - 2][:size, columns] = on_keys[spot * size : (spot + 1) * size]
        for ref in others:
            if ref.shape[0] > part:
                ref[part:, :] = jnp.zeros((RIDE_ROWS, ref.shape[1]), F32)
                ref[part:, :LANES] = packed


def tally_kernel(*refs):
    *parts, total = refs
    value = parts[0][...]
    for ref in parts[1:]:
        value = value + ref[ref.shape[0] - RIDE_ROWS :, :LANES]
    total[...] = value


def finish_kernel(row_parts, key_parts, *refs):
    *pieces, grad_query, grad_key = refs
    part = grad_query.shape[1]
    count = row_parts + key_parts - 1
    on_rows, on_keys = [], []
    for i, ref in enumerate(pieces):
        if i % count == 0:
            on_rows.append(ref[:part])
            on_keys.append(ref[part:])
        elif i % count < row_parts:
            on_rows.append(ref[:part])
        else:
            on_keys.append(ref[:part])
    grad_query[0] = sum(on_rows[1:], on_rows[0])
    grad_key[0] = sum(on_keys[1:], on_keys[0])


def close_kernel(mix_scale, loss_scale, total, grad_mix, head_loss):
    heads = grad_mix.shape[1]
    grad_mix[...] = total[:HEADS_S, :heads] * mix_scale
    head_loss[...] = total[HEADS_S : HEADS_S + 1, :heads] * loss_scale


def body(teacher_query, teacher_key, student_query, student_key, head_mix):
    shard_rows = teacher_query.shape[1]
    heads = head_mix.shape[0]
    length = lax.axis_size("seq")
    shards = lax.axis_size("head")
    copies = lax.axis_size("dp")
    row_parts = max(size for size in range(1, math.isqrt(length) + 1) if length % size == 0)
    key_parts = length // row_parts
    rows, keys = row_parts * shard_rows, key_parts * shard_rows

    def along_rows(position, step):
        return position // row_parts * row_parts + (position % row_parts + step) % row_parts

    def along_keys(position, step):
        return (position + step * row_parts) % length

    def fetch(value, target, step):
        return lax.ppermute(value, "seq", [(target(i, step), i) for i in range(length)])

    def deliver(value, target, step, turn):
        pairs = [
            (h * length + i, (h + turn) % shards * length + target(i, step))
            for h in range(shards)
            for i in range(length)
        ]
        return lax.ppermute(value, ("head", "seq"), pairs)

    own = (teacher_key, teacher_query, student_key, student_query)
    key_t = [fetch(teacher_key, along_keys, d) for d in range(1, key_parts)]
    query_t = [fetch(teacher_query, along_rows, d) for d in range(1, row_parts)]
    key_s = [fetch(student_key, along_keys, d) for d in range(1, key_parts)]
    query_s = [fetch(student_query, along_rows, d) for d in range(1, row_parts)]
    *own, lift_hi, lift_lo, back_hi, back_lo = prepare(head_mix, own)
    key_t, query_t, key_s, query_s = [[mine, *rest] for mine, rest in zip(own, (key_t, query_t, key_s, query_s))]

    def maps(block_t, block_s, before):
        count = len(block_t)
        size = count * shard_rows
        exponents = pltpu.VMEM((heads, size, rows), F32)
        student = pltpu.VMEM((HEADS_S, size, rows), BF16)
        stats = pltpu.VMEM((2, heads, rows), F32)
        cells = heads * size * rows
        return pl.pallas_call(
            functools.partial(maps_kernel, row_parts, count, heads, bool(before)),
            out_shape=(exponents, exponents, student, student, stats, pltpu.VMEM((heads, rows), F32))
            + (stats,) * row_parts,
            scratch_shapes=[pltpu.VMEM((heads, size, rows), F32)],
            compiler_params=pltpu.CompilerParams(vmem_limit_bytes=VMEM_LIMIT),
            cost_estimate=pl.CostEstimate(
                flops=cells * 2 * (HD_T + 3 * LIFT_BLOCK * HEADS_S), bytes_accessed=cells * 8, transcendentals=cells * 2
            ),
            name="maps",
        )(*block_t, *query_t, *block_s, *query_s, *before, lift_hi, lift_lo)

    done, before = [], []
    for block in (slice(0, 1), slice(1, key_parts)):
        if key_t[block]:
            results = maps(key_t[block], key_s[block], before)
            done.append(results[:6])
            before, turned = results[6:7], results[7:]
    lse_parts = [*before] + [fetch(turned[step - 1], along_rows, row_parts - step) for step in range(1, row_parts)]

    weight = shard_rows * length / HEADS_T
    width = HEADS_S * HD_S // shards
    ride = RIDE_ROWS if width >= LANES else 0
    count = row_parts + key_parts - 1
    shapes = []
    for shard in range(shards):
        extra = ride if shard == 0 else 0
        shapes += [(2 * shard_rows, width)] + [(shard_rows + extra, width)] * (count - 1)
    sums, *pieces = pl.pallas_call(
        functools.partial(
            back_kernel, row_parts, key_parts, shards, len(done), heads, weight * HD_S ** (-0.5)
        ),
        out_shape=[jax.ShapeDtypeStruct(shape, F32) for shape in [(RIDE_ROWS, LANES)] + shapes],
        scratch_shapes=[
            pltpu.VMEM((heads, rows), F32),
            pltpu.VMEM((heads, rows), F32),
            pltpu.VMEM((HEADS_S, keys, rows), BF16),
            pltpu.VMEM((HEADS_S, rows, HD_S), BF16),
            pltpu.VMEM((HEADS_S, keys, HD_S), BF16),
            pltpu.VMEM((heads * LIFT_BLOCK, HEADS_S * LIFT_BLOCK), F32),
        ],
        compiler_params=pltpu.CompilerParams(vmem_limit_bytes=VMEM_LIMIT),
        name="back",
    )(*query_s, *key_s, *lse_parts, back_hi, back_lo, *[ref for block in done for ref in block])

    moves = [(along_rows, step) for step in range(row_parts)] + [(along_keys, step) for step in range(1, key_parts)]
    arrived = [deliver(part, *moves[i % count], i // count) if i else part for i, part in enumerate(pieces)]
    small = functools.partial(pl.pallas_call, compiler_params=pltpu.CompilerParams(vmem_limit_bytes=VMEM_LIMIT // 4))

    def diagonal(across, along):
        return lambda position, _: along_keys(along_rows(position, across), along)

    if ride:
        others = arrived[1:count]
    else:
        others = [fetch(sums, target, step) for target, step in moves[1:]]
    for across in range(1, row_parts):
        others += [fetch(sums, diagonal(across, along), 0) for along in range(1, key_parts)]
    total = small(tally_kernel, out_shape=jax.ShapeDtypeStruct((RIDE_ROWS, LANES), F32), name="tally")(sums, *others)
    if copies & (copies - 1) == 0:
        for bit in range(copies.bit_length() - 1):
            total = total + lax.ppermute(total, "dp", [(i, i ^ (1 << bit)) for i in range(copies)])
    else:
        mine = total
        for step in range(1, copies):
            total = total + lax.ppermute(mine, "dp", [(i, (i + step) % copies) for i in range(copies)])

    grad = jax.ShapeDtypeStruct((1, shard_rows, width), F32)
    grad_query, grad_key = small(
        functools.partial(finish_kernel, row_parts, key_parts), out_shape=(grad, grad), name="finish"
    )(*arrived)
    samples = copies * teacher_query.shape[0] * shard_rows * length
    grad_mix, head_loss = small(
        functools.partial(close_kernel, HD_S ** (-0.5) * weight / samples, 1.0 / samples),
        out_shape=(jax.ShapeDtypeStruct((HEADS_S, heads), F32), jax.ShapeDtypeStruct((1, heads), F32)),
        name="close",
    )(total)
    return (grad_query, grad_key, grad_mix.T, head_loss[0])


def solution(mesh):
    return jax.shard_map(
        body,
        mesh=mesh,
        in_specs=(
            P("dp", "seq", "head"),
            P("dp", "seq", "head"),
            P("dp", "seq", None),
            P("dp", "seq", None),
            P("head", None),
        ),
        out_specs=(P("dp", "seq", "head"), P("dp", "seq", "head"), P("head", None), P("head")),
        check_vma=False,
    )
```

```python
import functools
import math

import jax
import jax.numpy as jnp
from jax import lax
from jax.experimental import pallas as pl
from jax.experimental.pallas import tpu as pltpu
from jax.sharding import PartitionSpec as P

HEADS_T = 24
HD_T = 128
HEADS_S = 8
HD_S = 64
LOG2E = math.log2(math.e)
LN2 = math.log(2.0)
LIFT_BLOCK = 32
BACK_BLOCK = 16
RIDE_ROWS = 16
LANES = 128
VMEM_LIMIT = 8 * 1024 * 1024

F32 = jnp.float32
BF16 = jnp.bfloat16


def dot(lhs, rhs, dims=((1,), (0,))):
    return lax.dot_general(lhs, rhs, (dims, ((), ())), preferred_element_type=F32)


def split(value):
    high = value.astype(BF16)
    low = (value - high.astype(F32)).astype(BF16)
    return high, low


def prepare_kernel(count, mix_ref, mix_tr_ref, *refs):
    sources, targets = refs[:count], refs[count : 2 * count]
    lift_hi, lift_lo, back_hi, back_lo, semaphores = refs[2 * count :]
    moves = [pltpu.make_async_copy(sources[i], targets[i], semaphores.at[i]) for i in range(count)]
    for move in moves:
        move.start()

    def kron(values, size):
        rows, columns = values.shape
        lane = lax.broadcasted_iota(jnp.int32, (rows, columns * size), 1)
        spread = jnp.zeros((rows, columns * size), F32)
        for index in range(columns):
            inside = (lane >= index * size) & (lane < (index + 1) * size)
            spread = jnp.where(inside, values[:, index : index + 1], spread)
        full = (rows, size, columns * size)
        sub = lax.broadcasted_iota(jnp.int32, full, 1)
        within = lax.broadcasted_iota(jnp.int32, full, 2) & (size - 1)
        picked = jnp.where(sub == within, spread[:, None, :], 0.0)
        return picked.reshape(rows * size, columns * size)

    scaled = mix_ref[...] * (HD_S ** (-0.5) * LOG2E)
    lift_hi[...], lift_lo[...] = split(kron(scaled, LIFT_BLOCK))
    back_hi[...], back_lo[...] = split(kron(mix_tr_ref[...], BACK_BLOCK))
    for move in moves:
        move.wait()


def prepare(head_mix, arrays):
    heads = head_mix.shape[0]
    lift = pltpu.VMEM((heads * LIFT_BLOCK, HEADS_S * LIFT_BLOCK), BF16)
    back = pltpu.VMEM((HEADS_S * BACK_BLOCK, heads * BACK_BLOCK), BF16)
    count = len(arrays)
    whole = pl.BlockSpec(memory_space=pltpu.VMEM)
    return pl.pallas_call(
        functools.partial(prepare_kernel, count),
        out_shape=[pltpu.VMEM(array.shape, array.dtype) for array in arrays] + [lift, lift, back, back],
        in_specs=[whole, whole] + [pl.BlockSpec(memory_space=pl.ANY)] * count,
        scratch_shapes=[pltpu.SemaphoreType.DMA((count,))],
        compiler_params=pltpu.CompilerParams(vmem_limit_bytes=VMEM_LIMIT // 2),
        name="prepare",
    )(head_mix, head_mix.T, *arrays)


def stacked(refs, columns):
    parts = [ref[0, :, columns] for ref in refs]
    return parts[0] if len(parts) == 1 else jnp.concatenate(parts, axis=0)


def by_head(place, shards, pieces, side):
    per = HEADS_S // shards
    low = turn = 0
    for piece in pieces:
        size, columns = piece.shape[1], piece.shape[2]
        whole = columns == HEADS_S * HD_S
        first = 0 if whole else lax.rem(place + shards - turn, shards) * per
        for index in range(columns // HD_S):
            side[first + index, low : low + size] = piece[0, :, index * HD_S : (index + 1) * HD_S]
        turn = 0 if whole else (turn + 1) % shards
        low += size if turn == 0 else 0


def maps_kernel(row_parts, key_parts, shards, student_parts, heads, carried, *refs):
    refs = list(refs)

    def take(count):
        return [refs.pop(0) for _ in range(count)]

    key_t, query_t = take(key_parts), take(row_parts)
    key_s, query_s = take(student_parts[0]), take(student_parts[1])
    before = refs.pop(0) if carried else None
    lift_hi, lift_lo, exp_t, exp_l, stu_hi, stu_lo, top, kl, key_side, *rest = refs
    query_side = query_s[0]
    place = lax.axis_index("head")
    if not carried:
        query_side = rest.pop(0)
        by_head(place, shards, query_s, query_side)
    by_head(place, shards, key_s, key_side)
    lse, *turned, lifted = rest
    keys = stu_hi.shape[1]
    rows = stu_hi.shape[2]
    for index in range(HEADS_S):
        stu_hi[index], stu_lo[index] = split(dot(key_side[index], query_side[index], ((1,), (1,))))
    for start in range(0, keys, LIFT_BLOCK):
        block = slice(start, start + LIFT_BLOCK)
        high = stu_hi[:, block, :].reshape(HEADS_S * LIFT_BLOCK, rows)
        low = stu_lo[:, block, :].reshape(HEADS_S * LIFT_BLOCK, rows)
        total = dot(lift_hi[...], high) + (dot(lift_hi[...], low) + dot(lift_lo[...], high))
        lifted[:, block, :] = total.reshape(heads, LIFT_BLOCK, rows)
    for head in range(heads):
        columns = slice(head * HD_T, (head + 1) * HD_T)
        teacher = dot(stacked(key_t, columns), stacked(query_t, columns), ((1,), (1,)))
        teacher = teacher * (HD_T ** (-0.5) * LOG2E)
        top_t = jnp.max(teacher, axis=0, keepdims=True)
        prob_t = jnp.exp2(teacher - top_t)
        exp_t[head] = prob_t
        mixed = lifted[head]
        kl[head : head + 1, :] = jnp.sum(prob_t * (teacher - mixed), axis=0, keepdims=True)
        top_l = jnp.max(mixed, axis=0, keepdims=True)
        prob_l = jnp.exp2(mixed - top_l)
        exp_l[head] = prob_l
        top[0, head : head + 1, :] = top_t
        top[1, head : head + 1, :] = top_l
        for which, best, prob in ((0, top_t, prob_t), (1, top_l, prob_l)):
            total = jnp.sum(prob, axis=0, keepdims=True)
            if carried:
                earlier = before[which, head : head + 1, :]
                higher = jnp.maximum(best, earlier)
                total = total * jnp.exp2(best - higher) + jnp.exp2(earlier - higher)
                best = higher
            lse[which, head : head + 1, :] = best + jnp.log2(total)
    part = rows // row_parts
    for step, ref in enumerate(turned, 1):
        for spot in range(row_parts):
            source = (spot + step) % row_parts * part
            ref[:, :, spot * part : (spot + 1) * part] = lse[:, :, source : source + part]


def back_kernel(row_parts, key_parts, shards, blocks, heads, factor, *refs):
    refs = list(refs)
    lse = [refs.pop(0) for _ in range(row_parts)]
    back_hi, back_lo, query_side = refs[:3]
    maps = [refs[3 + 7 * i : 9 + 7 * i] for i in range(blocks)]
    key_sides = [refs[9 + 7 * i] for i in range(blocks)]
    *outs, scale_t, scale_l, back, mix_acc = refs[3 + 7 * blocks :]
    keys, rows = back.shape[1:]
    part, size = rows // row_parts, keys // key_parts
    sums, pieces = outs[0], outs[1:]

    lse_all = []
    for which in range(2):
        parts = [ref[which] for ref in lse]
        best = functools.reduce(jnp.maximum, parts)
        total = sum(jnp.exp2(value - best) for value in parts)
        lse_all.append(best + jnp.log2(total))
    own = lax.broadcasted_iota(jnp.int32, (heads, rows), 1) < part
    loss = jnp.where(own, lse_all[1] - lse_all[0], 0.0)
    mix_acc[...] = jnp.zeros_like(mix_acc)
    offset = 0
    for exp_t, exp_l, stu_hi, stu_lo, top, kl in maps:
        scale_t[...] = jnp.exp2(top[0] - lse_all[0])
        scale_l[...] = jnp.exp2(top[1] - lse_all[1])
        loss = loss + scale_t[...] * kl[...]
        for start in range(0, exp_t.shape[1], LIFT_BLOCK):
            block = slice(start, start + LIFT_BLOCK)
            excess = (
                exp_l[:, block, :] * scale_l[...][:, None, :] - exp_t[:, block, :] * scale_t[...][:, None, :]
            )
            high, low = split(excess)
            s_high = stu_hi[:, block, :].reshape(HEADS_S * LIFT_BLOCK, rows)
            s_low = stu_lo[:, block, :].reshape(HEADS_S * LIFT_BLOCK, rows)
            f_high = high.reshape(heads * LIFT_BLOCK, rows)
            f_low = low.reshape(heads * LIFT_BLOCK, rows)
            over_rows = ((1,), (1,))
            mix_acc[...] += dot(f_high, s_high, over_rows) + (
                dot(f_high, s_low, over_rows) + dot(f_low, s_high, over_rows)
            )
            for inner in range(0, LIFT_BLOCK, BACK_BLOCK):
                b_high = high[:, inner : inner + BACK_BLOCK, :].reshape(heads * BACK_BLOCK, rows)
                b_low = low[:, inner : inner + BACK_BLOCK, :].reshape(heads * BACK_BLOCK, rows)
                total = dot(back_hi[...], b_high) + (dot(back_hi[...], b_low) + dot(back_lo[...], b_high))
                first = offset + start + inner
                back[:, first : first + BACK_BLOCK, :] = total.astype(BF16).reshape(HEADS_S, BACK_BLOCK, rows)
        offset += exp_t.shape[1]
    loss = jnp.sum(loss, axis=1, keepdims=True) * LN2

    acc = mix_acc[...].reshape(heads, LIFT_BLOCK, HEADS_S * LIFT_BLOCK)
    sub = lax.broadcasted_iota(jnp.int32, acc.shape, 1)
    within = lax.broadcasted_iota(jnp.int32, acc.shape, 2) & (LIFT_BLOCK - 1)
    diagonal = jnp.sum(jnp.where(sub == within, acc, 0.0), axis=1)
    lane = lax.broadcasted_iota(jnp.int32, diagonal.shape, 1)
    slot = lax.broadcasted_iota(jnp.int32, (heads, LANES), 1)
    packed = jnp.where(slot == HEADS_S, loss, 0.0)
    for index in range(HEADS_S):
        inside = (lane >= index * LIFT_BLOCK) & (lane < (index + 1) * LIFT_BLOCK)
        column = jnp.sum(jnp.where(inside, diagonal, 0.0), axis=1, keepdims=True)
        packed = jnp.where(slot == index, column, packed)
    packed = jnp.concatenate([packed, jnp.zeros((LANES - heads, LANES), F32)], axis=0)
    packed = jnp.transpose(packed)[:RIDE_ROWS]
    sums[...] = packed

    place = lax.axis_index("head")
    per = HEADS_S // shards
    count = row_parts + key_parts - 1
    for shard in range(shards):
        own, *others = pieces[shard * count : (shard + 1) * count]
        first = lax.rem(place + shard, shards) * per
        for index in range(per):
            tile = back[first + index]
            columns = slice(index * HD_S, (index + 1) * HD_S)
            sides = [side[first + index] for side in key_sides]
            on_keys = dot(tile, query_side[first + index]) * factor
            on_rows = dot(tile, jnp.concatenate(sides, axis=0), ((0,), (0,))) * factor
            own[:part, columns] = on_rows[:part]
            own[part:, columns] = on_keys[:size]
            for spot in range(1, row_parts):
                others[spot - 1][:part, columns] = on_rows[spot * part : (spot + 1) * part]
            for spot in range(1, key_parts):
                others[row_parts + spot - 2][:size, columns] = on_keys[spot * size : (spot + 1) * size]
        for ref in others:
            if ref.shape[0] > part:
                ref[part:, :] = jnp.zeros((RIDE_ROWS, ref.shape[1]), F32)
                ref[part:, :LANES] = packed


def tally_kernel(*refs):
    *parts, total = refs
    value = parts[0][...]
    for ref in parts[1:]:
        value = value + ref[ref.shape[0] - RIDE_ROWS :, :LANES]
    total[...] = value


def finish(pieces, low, part, small, sums=()):
    def kernel(*refs):
        shares, rest = refs[: len(pieces)], refs[len(pieces) :]
        first, *others = [ref[low : low + part] if ref.shape[0] == 2 * part else ref[:part] for ref in shares]
        rest[len(sums)][0] = sum(others, first)
        if sums:
            mine, other, _, total = rest
            total[...] = mine[...] + other[...]

    shapes = [jax.ShapeDtypeStruct((1, part, pieces[0].shape[1]), F32)]
    shapes += [jax.ShapeDtypeStruct((RIDE_ROWS, LANES), F32)] if sums else []
    return small(kernel, out_shape=shapes, name="finish")(*pieces, *sums)


def close_kernel(mix_scale, loss_scale, total, grad_mix, head_loss):
    heads = grad_mix.shape[1]
    grad_mix[...] = total[:HEADS_S, :heads] * mix_scale
    head_loss[...] = total[HEADS_S : HEADS_S + 1, :heads] * loss_scale


def body(teacher_query, teacher_key, student_query, student_key, head_mix):
    shard_rows = teacher_query.shape[1]
    heads = head_mix.shape[0]
    length = lax.axis_size("seq")
    shards = lax.axis_size("head")
    copies = lax.axis_size("dp")
    row_parts = max(size for size in range(1, math.isqrt(length) + 1) if length % size == 0)
    key_parts = length // row_parts
    rows, keys = row_parts * shard_rows, key_parts * shard_rows

    def along_rows(position, step):
        return position // row_parts * row_parts + (position % row_parts + step) % row_parts

    def along_keys(position, step):
        return (position + step * row_parts) % length

    def fetch(value, target, step):
        return lax.ppermute(value, "seq", [(target(i, step), i) for i in range(length)])

    def deliver(value, target, step, turn):
        pairs = [
            (h * length + i, (h + turn) % shards * length + target(i, step))
            for h in range(shards)
            for i in range(length)
        ]
        return lax.ppermute(value, ("head", "seq"), pairs)

    def fetch_student(value, target, step):
        columns = value.shape[2] // shards
        share = lax.dynamic_slice_in_dim(value, lax.axis_index("head") * columns, columns, 2)
        share = fetch(share, target, step)
        turns = [[(h, (h + turn) % shards) for h in range(shards)] for turn in range(1, shards)]
        return [share] + [lax.ppermute(share, "head", pairs) for pairs in turns]

    own = (teacher_key, teacher_query, student_key, student_query)
    key_t = [fetch(teacher_key, along_keys, d) for d in range(1, key_parts)]
    query_t = [fetch(teacher_query, along_rows, d) for d in range(1, row_parts)]
    key_s = [piece for d in range(1, key_parts) for piece in fetch_student(student_key, along_keys, d)]
    query_s = [piece for d in range(1, row_parts) for piece in fetch_student(student_query, along_rows, d)]
    *own, lift_hi, lift_lo, back_hi, back_lo = prepare(head_mix, own)
    key_t, query_t, key_s, query_s = [[mine, *rest] for mine, rest in zip(own, (key_t, query_t, key_s, query_s))]

    def maps(block_t, block_s, rows_s, before):
        count = len(block_t)
        size = count * shard_rows
        exponents = pltpu.VMEM((heads, size, rows), F32)
        student = pltpu.VMEM((HEADS_S, size, rows), BF16)
        stats = pltpu.VMEM((2, heads, rows), F32)
        cells = heads * size * rows
        return pl.pallas_call(
            functools.partial(
                maps_kernel, row_parts, count, shards, (len(block_s), len(rows_s)), heads, bool(before)
            ),
            out_shape=[exponents, exponents, student, student, stats, pltpu.VMEM((heads, rows), F32)]
            + [pltpu.VMEM((HEADS_S, size, HD_S), BF16)]
            + [pltpu.VMEM((HEADS_S, rows, HD_S), BF16)] * (not before)
            + [stats] * row_parts,
            scratch_shapes=[pltpu.VMEM((heads, size, rows), F32)],
            compiler_params=pltpu.CompilerParams(vmem_limit_bytes=VMEM_LIMIT),
            cost_estimate=pl.CostEstimate(
                flops=cells * 2 * (HD_T + 3 * LIFT_BLOCK * HEADS_S), bytes_accessed=cells * 8, transcendentals=cells * 2
            ),
            name="maps",
        )(*block_t, *query_t, *block_s, *rows_s, *before, lift_hi, lift_lo)

    results = maps(key_t[:1], key_s[:1], query_s, [])
    done, query_side, before, turned = [results[:7]], results[7], results[8:9], results[9:]
    if key_parts > 1:
        results = maps(key_t[1:], key_s[1:], [query_side], before)
        done, before, turned = done + [results[:7]], results[7:8], results[8:]
    lse_parts = [*before] + [fetch(turned[step - 1], along_rows, row_parts - step) for step in range(1, row_parts)]

    weight = shard_rows * length / HEADS_T
    width = HEADS_S * HD_S // shards
    ride = RIDE_ROWS if width >= LANES else 0
    count = row_parts + key_parts - 1
    shapes = []
    for shard in range(shards):
        extra = ride if shard == 0 else 0
        shapes += [(2 * shard_rows, width)] + [(shard_rows + extra, width)] * (count - 1)
    sums, *pieces = pl.pallas_call(
        functools.partial(
            back_kernel, row_parts, key_parts, shards, len(done), heads, weight * HD_S ** (-0.5)
        ),
        out_shape=[jax.ShapeDtypeStruct(shape, F32) for shape in [(RIDE_ROWS, LANES)] + shapes],
        scratch_shapes=[
            pltpu.VMEM((heads, rows), F32),
            pltpu.VMEM((heads, rows), F32),
            pltpu.VMEM((HEADS_S, keys, rows), BF16),
            pltpu.VMEM((heads * LIFT_BLOCK, HEADS_S * LIFT_BLOCK), F32),
        ],
        compiler_params=pltpu.CompilerParams(vmem_limit_bytes=VMEM_LIMIT),
        name="back",
    )(*lse_parts, back_hi, back_lo, query_side, *[ref for block in done for ref in block])

    moves = [(along_rows, step) for step in range(row_parts)] + [(along_keys, step) for step in range(1, key_parts)]
    arrived = [deliver(part, *moves[i % count], i // count) if i else part for i, part in enumerate(pieces)]
    small = functools.partial(pl.pallas_call, compiler_params=pltpu.CompilerParams(vmem_limit_bytes=VMEM_LIMIT // 4))

    def diagonal(across, along):
        return lambda position, _: along_keys(along_rows(position, across), along)

    if ride:
        others = arrived[1:count]
    else:
        others = [fetch(sums, target, step) for target, step in moves[1:]]
    for across in range(1, row_parts):
        others += [fetch(sums, diagonal(across, along), 0) for along in range(1, key_parts)]
    total = small(tally_kernel, out_shape=jax.ShapeDtypeStruct((RIDE_ROWS, LANES), F32), name="tally")(sums, *others)
    def swapped(value, bit):
        return lax.ppermute(value, "dp", [(i, i ^ (1 << bit)) for i in range(copies)])

    for_query = [part for i, part in enumerate(arrived) if i % count < row_parts]
    for_key = [part for i, part in enumerate(arrived) if i % count == 0 or i % count >= row_parts]
    (grad_query,) = finish(for_query, 0, shard_rows, small)
    if copies > 1 and copies & (copies - 1) == 0:
        grad_key, total = finish(for_key, shard_rows, shard_rows, small, (total, swapped(total, 0)))
        for bit in range(1, copies.bit_length() - 1):
            total = total + swapped(total, bit)
    else:
        (grad_key,) = finish(for_key, shard_rows, shard_rows, small)
        mine = total
        for step in range(1, copies):
            total = total + lax.ppermute(mine, "dp", [(i, (i + step) % copies) for i in range(copies)])
    samples = copies * teacher_query.shape[0] * shard_rows * length
    grad_mix, head_loss = small(
        functools.partial(close_kernel, HD_S ** (-0.5) * weight / samples, 1.0 / samples),
        out_shape=(jax.ShapeDtypeStruct((HEADS_S, heads), F32), jax.ShapeDtypeStruct((1, heads), F32)),
        name="close",
    )(total)
    return (grad_query, grad_key, grad_mix.T, head_loss[0])


def solution(mesh):
    return jax.shard_map(
        body,
        mesh=mesh,
        in_specs=(
            P("dp", "seq", "head"),
            P("dp", "seq", "head"),
            P("dp", "seq", None),
            P("dp", "seq", None),
            P("head", None),
        ),
        out_specs=(P("dp", "seq", "head"), P("dp", "seq", "head"), P("head", None), P("head")),
        check_vma=False,
    )
```

```python
import functools
import math

import jax
import jax.numpy as jnp
from jax import lax
from jax.experimental import pallas as pl
from jax.experimental.pallas import tpu as pltpu
from jax.sharding import PartitionSpec as P

HEADS_T = 24
HD_T = 128
HEADS_S = 8
HD_S = 64
LOG2E = math.log2(math.e)
LN2 = math.log(2.0)
LIFT_BLOCK = 32
BACK_BLOCK = 16
RIDE_ROWS = 16
LANES = 128
STUDENT_FLOPS = 64 * 10**8
VMEM_LIMIT = 8 * 1024 * 1024

F32 = jnp.float32
BF16 = jnp.bfloat16


def dot(lhs, rhs, dims=((1,), (0,))):
    return lax.dot_general(lhs, rhs, (dims, ((), ())), preferred_element_type=F32)


def split(value):
    high = value.astype(BF16)
    low = (value - high.astype(F32)).astype(BF16)
    return high, low


def prepare_kernel(count, mix_ref, mix_tr_ref, *refs):
    sources, targets = refs[:count], refs[count : 2 * count]
    lift_hi, lift_lo, back_hi, back_lo, semaphores = refs[2 * count :]
    moves = [pltpu.make_async_copy(sources[i], targets[i], semaphores.at[i]) for i in range(count)]
    for move in moves:
        move.start()

    def kron(values, size):
        rows, columns = values.shape
        lane = lax.broadcasted_iota(jnp.int32, (rows, columns * size), 1)
        spread = jnp.zeros((rows, columns * size), F32)
        for index in range(columns):
            inside = (lane >= index * size) & (lane < (index + 1) * size)
            spread = jnp.where(inside, values[:, index : index + 1], spread)
        full = (rows, size, columns * size)
        sub = lax.broadcasted_iota(jnp.int32, full, 1)
        within = lax.broadcasted_iota(jnp.int32, full, 2) & (size - 1)
        picked = jnp.where(sub == within, spread[:, None, :], 0.0)
        return picked.reshape(rows * size, columns * size)

    scaled = mix_ref[...] * (HD_S ** (-0.5) * LOG2E)
    lift_hi[...], lift_lo[...] = split(kron(scaled, LIFT_BLOCK))
    back_hi[...], back_lo[...] = split(kron(mix_tr_ref[...], BACK_BLOCK))
    for move in moves:
        move.wait()


def prepare(head_mix, arrays):
    heads = head_mix.shape[0]
    lift = pltpu.VMEM((heads * LIFT_BLOCK, HEADS_S * LIFT_BLOCK), BF16)
    back = pltpu.VMEM((HEADS_S * BACK_BLOCK, heads * BACK_BLOCK), BF16)
    count = len(arrays)
    whole = pl.BlockSpec(memory_space=pltpu.VMEM)
    return pl.pallas_call(
        functools.partial(prepare_kernel, count),
        out_shape=[pltpu.VMEM(array.shape, array.dtype) for array in arrays] + [lift, lift, back, back],
        in_specs=[whole, whole] + [pl.BlockSpec(memory_space=pl.ANY)] * count,
        scratch_shapes=[pltpu.SemaphoreType.DMA((count,))],
        compiler_params=pltpu.CompilerParams(vmem_limit_bytes=VMEM_LIMIT // 2),
        name="prepare",
    )(head_mix, head_mix.T, *arrays)


def stacked(refs, columns):
    parts = [ref[0, :, columns] for ref in refs]
    return parts[0] if len(parts) == 1 else jnp.concatenate(parts, axis=0)


def student_kernel(row_parts, key_parts, heads, *refs):
    key_s, query_s, refs = refs[:key_parts], refs[key_parts : key_parts + row_parts], refs[key_parts + row_parts :]
    lift_hi, lift_lo, lifted, exp_l, stu_hi, stu_lo, top, lse = refs
    keys, rows = stu_hi.shape[1:]
    for index in range(HEADS_S):
        columns = slice(index * HD_S, (index + 1) * HD_S)
        student = dot(stacked(key_s, columns), stacked(query_s, columns), ((1,), (1,)))
        stu_hi[index], stu_lo[index] = split(student)
    for start in range(0, keys, LIFT_BLOCK):
        block = slice(start, start + LIFT_BLOCK)
        high = stu_hi[:, block, :].reshape(HEADS_S * LIFT_BLOCK, rows)
        low = stu_lo[:, block, :].reshape(HEADS_S * LIFT_BLOCK, rows)
        total = dot(lift_hi[...], high) + (dot(lift_hi[...], low) + dot(lift_lo[...], high))
        lifted[:, block, :] = total.reshape(heads, LIFT_BLOCK, rows)
    for head in range(heads):
        mixed = lifted[head]
        best = jnp.max(mixed, axis=0, keepdims=True)
        prob = jnp.exp2(mixed - best)
        exp_l[head] = prob
        top[head : head + 1, :] = best
        lse[head : head + 1, :] = best + jnp.log2(jnp.sum(prob, axis=0, keepdims=True))


def teacher_kernel(row_parts, key_parts, heads, offset, carried, *refs):
    key_t, query_t, refs = refs[:key_parts], refs[key_parts : key_parts + row_parts], refs[key_parts + row_parts :]
    lifted, lse_l, *refs = refs
    before = refs.pop(0) if carried else None
    exp_t, top, kl, lse, *turned = refs
    keys, rows = exp_t.shape[1:]
    for head in range(heads):
        columns = slice(head * HD_T, (head + 1) * HD_T)
        teacher = dot(stacked(key_t, columns), stacked(query_t, columns), ((1,), (1,)))
        teacher = teacher * (HD_T ** (-0.5) * LOG2E)
        best = jnp.max(teacher, axis=0, keepdims=True)
        prob = jnp.exp2(teacher - best)
        exp_t[head] = prob
        mixed = lifted[head, offset : offset + keys, :]
        kl[head : head + 1, :] = jnp.sum(prob * (teacher - mixed), axis=0, keepdims=True)
        top[head : head + 1, :] = best
        total = jnp.sum(prob, axis=0, keepdims=True)
        if carried:
            earlier = before[0, head : head + 1, :]
            higher = jnp.maximum(best, earlier)
            total = total * jnp.exp2(best - higher) + jnp.exp2(earlier - higher)
            best = higher
        lse[0, head : head + 1, :] = best + jnp.log2(total)
    lse[1] = lse_l[...]
    part = rows // row_parts
    for step, ref in enumerate(turned, 1):
        for spot in range(row_parts):
            source = (spot + step) % row_parts * part
            ref[:, :, spot * part : (spot + 1) * part] = lse[:, :, source : source + part]


def back_kernel(row_parts, key_parts, shards, blocks, heads, factor, *refs):
    refs = list(refs)
    query_s = [refs.pop(0) for _ in range(row_parts)]
    key_s = [refs.pop(0) for _ in range(key_parts)]
    lse = [refs.pop(0) for _ in range(row_parts)]
    back_hi, back_lo, exp_l, stu_hi, stu_lo, top_l = refs[:6]
    maps = [refs[6 + 3 * i : 9 + 3 * i] for i in range(blocks)]
    *outs, scale_t, scale_l, back, row_side, key_side, mix_acc = refs[6 + 3 * blocks :]
    keys, rows = back.shape[1:]
    part, size = rows // row_parts, keys // key_parts
    sums, pieces = outs[0], outs[1:]

    lse_all = []
    for which in range(2):
        parts = [ref[which] for ref in lse]
        best = functools.reduce(jnp.maximum, parts)
        total = sum(jnp.exp2(value - best) for value in parts)
        lse_all.append(best + jnp.log2(total))
    own = lax.broadcasted_iota(jnp.int32, (heads, rows), 1) < part
    loss = jnp.where(own, lse_all[1] - lse_all[0], 0.0)
    mix_acc[...] = jnp.zeros_like(mix_acc)
    offset = 0
    scale_l[...] = jnp.exp2(top_l[...] - lse_all[1])
    for exp_t, top_t, kl in maps:
        scale_t[...] = jnp.exp2(top_t[...] - lse_all[0])
        loss = loss + scale_t[...] * kl[...]
        for start in range(0, exp_t.shape[1], LIFT_BLOCK):
            block = slice(start, start + LIFT_BLOCK)
            place = slice(offset + start, offset + start + LIFT_BLOCK)
            excess = (
                exp_l[:, place, :] * scale_l[...][:, None, :] - exp_t[:, block, :] * scale_t[...][:, None, :]
            )
            high, low = split(excess)
            s_high = stu_hi[:, place, :].reshape(HEADS_S * LIFT_BLOCK, rows)
            s_low = stu_lo[:, place, :].reshape(HEADS_S * LIFT_BLOCK, rows)
            f_high = high.reshape(heads * LIFT_BLOCK, rows)
            f_low = low.reshape(heads * LIFT_BLOCK, rows)
            over_rows = ((1,), (1,))
            mix_acc[...] += dot(f_high, s_high, over_rows) + (
                dot(f_high, s_low, over_rows) + dot(f_low, s_high, over_rows)
            )
            for inner in range(0, LIFT_BLOCK, BACK_BLOCK):
                b_high = high[:, inner : inner + BACK_BLOCK, :].reshape(heads * BACK_BLOCK, rows)
                b_low = low[:, inner : inner + BACK_BLOCK, :].reshape(heads * BACK_BLOCK, rows)
                total = dot(back_hi[...], b_high) + (dot(back_hi[...], b_low) + dot(back_lo[...], b_high))
                first = offset + start + inner
                back[:, first : first + BACK_BLOCK, :] = total.astype(BF16).reshape(HEADS_S, BACK_BLOCK, rows)
        offset += exp_t.shape[1]
    loss = jnp.sum(loss, axis=1, keepdims=True) * LN2

    acc = mix_acc[...].reshape(heads, LIFT_BLOCK, HEADS_S * LIFT_BLOCK)
    sub = lax.broadcasted_iota(jnp.int32, acc.shape, 1)
    within = lax.broadcasted_iota(jnp.int32, acc.shape, 2) & (LIFT_BLOCK - 1)
    diagonal = jnp.sum(jnp.where(sub == within, acc, 0.0), axis=1)
    lane = lax.broadcasted_iota(jnp.int32, diagonal.shape, 1)
    slot = lax.broadcasted_iota(jnp.int32, (heads, LANES), 1)
    packed = jnp.where(slot == HEADS_S, loss, 0.0)
    for index in range(HEADS_S):
        inside = (lane >= index * LIFT_BLOCK) & (lane < (index + 1) * LIFT_BLOCK)
        column = jnp.sum(jnp.where(inside, diagonal, 0.0), axis=1, keepdims=True)
        packed = jnp.where(slot == index, column, packed)
    packed = jnp.concatenate([packed, jnp.zeros((LANES - heads, LANES), F32)], axis=0)
    packed = jnp.transpose(packed)[:RIDE_ROWS]
    sums[...] = packed

    for index in range(HEADS_S):
        columns = slice(index * HD_S, (index + 1) * HD_S)
        row_side[index] = stacked(query_s, columns)
        key_side[index] = stacked(key_s, columns)
    place = lax.axis_index("head")
    per = HEADS_S // shards
    count = row_parts + key_parts - 1
    for shard in range(shards):
        own, *others = pieces[shard * count : (shard + 1) * count]
        first = lax.rem(place + shard, shards) * per
        for index in range(per):
            tile = back[first + index]
            columns = slice(index * HD_S, (index + 1) * HD_S)
            on_keys = dot(tile, row_side[first + index]) * factor
            on_rows = dot(tile, key_side[first + index], ((0,), (0,))) * factor
            own[:part, columns] = on_rows[:part]
            own[part:, columns] = on_keys[:size]
            for spot in range(1, row_parts):
                others[spot - 1][:part, columns] = on_rows[spot * part : (spot + 1) * part]
            for spot in range(1, key_parts):
                others[row_parts + spot - 2][:size, columns] = on_keys[spot * size : (spot + 1) * size]
        for ref in others:
            if ref.shape[0] > part:
                ref[part:, :] = jnp.zeros((RIDE_ROWS, ref.shape[1]), F32)
                ref[part:, :LANES] = packed


def tally_kernel(*refs):
    *parts, total = refs
    value = parts[0][...]
    for ref in parts[1:]:
        value = value + ref[ref.shape[0] - RIDE_ROWS :, :LANES]
    total[...] = value


def finish_kernel(row_parts, key_parts, *refs):
    *pieces, grad_query, grad_key = refs
    part = grad_query.shape[1]
    count = row_parts + key_parts - 1
    on_rows, on_keys = [], []
    for i, ref in enumerate(pieces):
        if i % count == 0:
            on_rows.append(ref[:part])
            on_keys.append(ref[part:])
        elif i % count < row_parts:
            on_rows.append(ref[:part])
        else:
            on_keys.append(ref[:part])
    grad_query[0] = sum(on_rows[1:], on_rows[0])
    grad_key[0] = sum(on_keys[1:], on_keys[0])


def close_kernel(mix_scale, loss_scale, total, grad_mix, head_loss):
    heads = grad_mix.shape[1]
    grad_mix[...] = total[:HEADS_S, :heads] * mix_scale
    head_loss[...] = total[HEADS_S : HEADS_S + 1, :heads] * loss_scale


def body(teacher_query, teacher_key, student_query, student_key, head_mix):
    shard_rows = teacher_query.shape[1]
    heads = head_mix.shape[0]
    length = lax.axis_size("seq")
    shards = lax.axis_size("head")
    copies = lax.axis_size("dp")
    row_parts = max(size for size in range(1, math.isqrt(length) + 1) if length % size == 0)
    key_parts = length // row_parts
    rows, keys = row_parts * shard_rows, key_parts * shard_rows

    def along_rows(position, step):
        return position // row_parts * row_parts + (position % row_parts + step) % row_parts

    def along_keys(position, step):
        return (position + step * row_parts) % length

    def fetch(value, target, step):
        return lax.ppermute(value, "seq", [(target(i, step), i) for i in range(length)])

    def deliver(value, target, step, turn):
        pairs = [
            (h * length + i, (h + turn) % shards * length + target(i, step))
            for h in range(shards)
            for i in range(length)
        ]
        return lax.ppermute(value, ("head", "seq"), pairs)

    own = (teacher_key, teacher_query, student_key, student_query)
    key_t = [fetch(teacher_key, along_keys, d) for d in range(1, key_parts)]
    query_t = [fetch(teacher_query, along_rows, d) for d in range(1, row_parts)]
    key_s = [fetch(student_key, along_keys, d) for d in range(1, key_parts)]
    query_s = [fetch(student_query, along_rows, d) for d in range(1, row_parts)]
    *own, lift_hi, lift_lo, back_hi, back_lo = prepare(head_mix, own)
    key_t, query_t, key_s, query_s = [[mine, *rest] for mine, rest in zip(own, (key_t, query_t, key_s, query_s))]

    exponents = pltpu.VMEM((heads, keys, rows), F32)
    student = pltpu.VMEM((HEADS_S, keys, rows), BF16)
    stats = pltpu.VMEM((heads, rows), F32)
    both = pltpu.VMEM((2, heads, rows), F32)
    lifted, exp_l, stu_hi, stu_lo, top_l, lse_l = pl.pallas_call(
        functools.partial(student_kernel, row_parts, key_parts, heads),
        out_shape=(exponents, exponents, student, student, stats, stats),
        compiler_params=pltpu.CompilerParams(vmem_limit_bytes=VMEM_LIMIT),
        cost_estimate=pl.CostEstimate(flops=STUDENT_FLOPS, bytes_accessed=1, transcendentals=1),
        name="student",
    )(*key_s, *query_s, lift_hi, lift_lo)

    def teacher(block_t, offset, before):
        size = len(block_t) * shard_rows
        return pl.pallas_call(
            functools.partial(teacher_kernel, row_parts, len(block_t), heads, offset, bool(before)),
            out_shape=(pltpu.VMEM((heads, size, rows), F32), stats, stats, both) + (both,) * (row_parts - 1),
            compiler_params=pltpu.CompilerParams(vmem_limit_bytes=VMEM_LIMIT),
            name="teacher",
        )(*block_t, *query_t, lifted, lse_l, *before)

    done, before = [], []
    for first, block in ((0, key_t[:1]), (1, key_t[1:])):
        if block:
            results = teacher(block, first * shard_rows, before)
            done.append(results[:3])
            before, turned = results[3:4], results[4:]
    lse_parts = [*before] + [fetch(turned[step - 1], along_rows, row_parts - step) for step in range(1, row_parts)]

    weight = shard_rows * length / HEADS_T
    width = HEADS_S * HD_S // shards
    ride = RIDE_ROWS if width >= LANES else 0
    count = row_parts + key_parts - 1
    shapes = []
    for shard in range(shards):
        extra = ride if shard == 0 else 0
        shapes += [(2 * shard_rows, width)] + [(shard_rows + extra, width)] * (count - 1)
    sums, *pieces = pl.pallas_call(
        functools.partial(
            back_kernel, row_parts, key_parts, shards, len(done), heads, weight * HD_S ** (-0.5)
        ),
        out_shape=[jax.ShapeDtypeStruct(shape, F32) for shape in [(RIDE_ROWS, LANES)] + shapes],
        scratch_shapes=[
            pltpu.VMEM((heads, rows), F32),
            pltpu.VMEM((heads, rows), F32),
            pltpu.VMEM((HEADS_S, keys, rows), BF16),
            pltpu.VMEM((HEADS_S, rows, HD_S), BF16),
            pltpu.VMEM((HEADS_S, keys, HD_S), BF16),
            pltpu.VMEM((heads * LIFT_BLOCK, HEADS_S * LIFT_BLOCK), F32),
        ],
        compiler_params=pltpu.CompilerParams(vmem_limit_bytes=VMEM_LIMIT),
        name="back",
    )(
        *query_s, *key_s, *lse_parts, back_hi, back_lo, exp_l, stu_hi, stu_lo, top_l,
        *[ref for block in done for ref in block],
    )

    moves = [(along_rows, step) for step in range(row_parts)] + [(along_keys, step) for step in range(1, key_parts)]
    arrived = [deliver(part, *moves[i % count], i // count) if i else part for i, part in enumerate(pieces)]
    small = functools.partial(pl.pallas_call, compiler_params=pltpu.CompilerParams(vmem_limit_bytes=VMEM_LIMIT // 4))

    def diagonal(across, along):
        return lambda position, _: along_keys(along_rows(position, across), along)

    if ride:
        others = arrived[1:count]
    else:
        others = [fetch(sums, target, step) for target, step in moves[1:]]
    for across in range(1, row_parts):
        others += [fetch(sums, diagonal(across, along), 0) for along in range(1, key_parts)]
    total = small(tally_kernel, out_shape=jax.ShapeDtypeStruct((RIDE_ROWS, LANES), F32), name="tally")(sums, *others)
    if copies & (copies - 1) == 0:
        for bit in range(copies.bit_length() - 1):
            total = total + lax.ppermute(total, "dp", [(i, i ^ (1 << bit)) for i in range(copies)])
    else:
        mine = total
        for step in range(1, copies):
            total = total + lax.ppermute(mine, "dp", [(i, (i + step) % copies) for i in range(copies)])

    grad = jax.ShapeDtypeStruct((1, shard_rows, width), F32)
    grad_query, grad_key = small(
        functools.partial(finish_kernel, row_parts, key_parts), out_shape=(grad, grad), name="finish"
    )(*arrived)
    samples = copies * teacher_query.shape[0] * shard_rows * length
    grad_mix, head_loss = small(
        functools.partial(close_kernel, HD_S ** (-0.5) * weight / samples, 1.0 / samples),
        out_shape=(jax.ShapeDtypeStruct((HEADS_S, heads), F32), jax.ShapeDtypeStruct((1, heads), F32)),
        name="close",
    )(total)
    return (grad_query, grad_key, grad_mix.T, head_loss[0])


def solution(mesh):
    return jax.shard_map(
        body,
        mesh=mesh,
        in_specs=(
            P("dp", "seq", "head"),
            P("dp", "seq", "head"),
            P("dp", "seq", None),
            P("dp", "seq", None),
            P("head", None),
        ),
        out_specs=(P("dp", "seq", "head"), P("dp", "seq", "head"), P("head", None), P("head")),
        check_vma=False,
    )
```

```python
import functools
import math

import jax
import jax.numpy as jnp
from jax import lax
from jax.experimental import pallas as pl
from jax.experimental.pallas import tpu as pltpu
from jax.sharding import PartitionSpec as P

HEADS_T = 24
HD_T = 128
HEADS_S = 8
HD_S = 64
LOG2E = math.log2(math.e)
LN2 = math.log(2.0)
LIFT_BLOCK = 32
BACK_BLOCK = 16
RIDE_ROWS = 16
LANES = 128
STUDENT_FLOPS = 64 * 10**8
VMEM_LIMIT = 8 * 1024 * 1024

F32 = jnp.float32
BF16 = jnp.bfloat16


def dot(lhs, rhs, dims=((1,), (0,))):
    return lax.dot_general(lhs, rhs, (dims, ((), ())), preferred_element_type=F32)


def split(value):
    high = value.astype(BF16)
    low = (value - high.astype(F32)).astype(BF16)
    return high, low


def prepare_kernel(count, mix_ref, mix_tr_ref, *refs):
    sources, targets = refs[:count], refs[count : 2 * count]
    lift_hi, lift_lo, back_hi, back_lo, semaphores = refs[2 * count :]
    moves = [pltpu.make_async_copy(sources[i], targets[i], semaphores.at[i]) for i in range(count)]
    for move in moves:
        move.start()

    def kron(values, size):
        rows, columns = values.shape
        lane = lax.broadcasted_iota(jnp.int32, (rows, columns * size), 1)
        spread = jnp.zeros((rows, columns * size), F32)
        for index in range(columns):
            inside = (lane >= index * size) & (lane < (index + 1) * size)
            spread = jnp.where(inside, values[:, index : index + 1], spread)
        full = (rows, size, columns * size)
        sub = lax.broadcasted_iota(jnp.int32, full, 1)
        within = lax.broadcasted_iota(jnp.int32, full, 2) & (size - 1)
        picked = jnp.where(sub == within, spread[:, None, :], 0.0)
        return picked.reshape(rows * size, columns * size)

    scaled = mix_ref[...] * (HD_S ** (-0.5) * LOG2E)
    lift_hi[...], lift_lo[...] = split(kron(scaled, LIFT_BLOCK))
    back_hi[...], back_lo[...] = split(kron(mix_tr_ref[...], BACK_BLOCK))
    for move in moves:
        move.wait()


def prepare(head_mix, arrays):
    heads = head_mix.shape[0]
    lift = pltpu.VMEM((heads * LIFT_BLOCK, HEADS_S * LIFT_BLOCK), BF16)
    back = pltpu.VMEM((HEADS_S * BACK_BLOCK, heads * BACK_BLOCK), BF16)
    count = len(arrays)
    whole = pl.BlockSpec(memory_space=pltpu.VMEM)
    return pl.pallas_call(
        functools.partial(prepare_kernel, count),
        out_shape=[pltpu.VMEM(array.shape, array.dtype) for array in arrays] + [lift, lift, back, back],
        in_specs=[whole, whole] + [pl.BlockSpec(memory_space=pl.ANY)] * count,
        scratch_shapes=[pltpu.SemaphoreType.DMA((count,))],
        compiler_params=pltpu.CompilerParams(vmem_limit_bytes=VMEM_LIMIT // 2),
        name="prepare",
    )(head_mix, head_mix.T, *arrays)


def stacked(refs, columns):
    parts = [ref[0, :, columns] for ref in refs]
    return parts[0] if len(parts) == 1 else jnp.concatenate(parts, axis=0)


def student_kernel(row_parts, key_parts, heads, *refs):
    key_s, query_s, refs = refs[:key_parts], refs[key_parts : key_parts + row_parts], refs[key_parts + row_parts :]
    lift_hi, lift_lo, lifted, exp_l, stu_hi, stu_lo, top, lse = refs
    keys, rows = stu_hi.shape[1:]
    for index in range(HEADS_S):
        columns = slice(index * HD_S, (index + 1) * HD_S)
        student = dot(stacked(key_s, columns), stacked(query_s, columns), ((1,), (1,)))
        stu_hi[index], stu_lo[index] = split(student)
    for start in range(0, keys, LIFT_BLOCK):
        block = slice(start, start + LIFT_BLOCK)
        high = stu_hi[:, block, :].reshape(HEADS_S * LIFT_BLOCK, rows)
        low = stu_lo[:, block, :].reshape(HEADS_S * LIFT_BLOCK, rows)
        total = dot(lift_hi[...], high) + (dot(lift_hi[...], low) + dot(lift_lo[...], high))
        lifted[:, block, :] = total.reshape(heads, LIFT_BLOCK, rows)
    for head in range(heads):
        mixed = lifted[head]
        best = jnp.max(mixed, axis=0, keepdims=True)
        prob = jnp.exp2(mixed - best)
        exp_l[head] = prob
        top[head : head + 1, :] = best
        lse[head : head + 1, :] = best + jnp.log2(jnp.sum(prob, axis=0, keepdims=True))


def teacher_kernel(row_parts, key_parts, heads, offset, carried, *refs):
    key_t, query_t, refs = refs[:key_parts], refs[key_parts : key_parts + row_parts], refs[key_parts + row_parts :]
    lifted, lse_l, *refs = refs
    before = refs.pop(0) if carried else None
    exp_t, top, kl, lse, *turned = refs
    keys, rows = exp_t.shape[1:]
    for head in range(heads):
        columns = slice(head * HD_T, (head + 1) * HD_T)
        teacher = dot(stacked(key_t, columns), stacked(query_t, columns), ((1,), (1,)))
        teacher = teacher * (HD_T ** (-0.5) * LOG2E)
        best = jnp.max(teacher, axis=0, keepdims=True)
        prob = jnp.exp2(teacher - best)
        exp_t[head] = prob
        mixed = lifted[head, offset : offset + keys, :]
        kl[head : head + 1, :] = jnp.sum(prob * (teacher - mixed), axis=0, keepdims=True)
        top[head : head + 1, :] = best
        total = jnp.sum(prob, axis=0, keepdims=True)
        if carried:
            earlier = before[0, head : head + 1, :]
            higher = jnp.maximum(best, earlier)
            total = total * jnp.exp2(best - higher) + jnp.exp2(earlier - higher)
            best = higher
        lse[0, head : head + 1, :] = best + jnp.log2(total)
    lse[1] = lse_l[...]
    part = rows // row_parts
    for step, ref in enumerate(turned, 1):
        for spot in range(row_parts):
            source = (spot + step) % row_parts * part
            ref[:, :, spot * part : (spot + 1) * part] = lse[:, :, source : source + part]


def back_kernel(row_parts, key_parts, shards, blocks, heads, factor, *refs):
    refs = list(refs)
    query_s = [refs.pop(0) for _ in range(row_parts)]
    key_s = [refs.pop(0) for _ in range(key_parts)]
    lse = [refs.pop(0) for _ in range(row_parts)]
    back_hi, back_lo, exp_l, stu_hi, stu_lo, top_l = refs[:6]
    maps = [refs[6 + 3 * i : 9 + 3 * i] for i in range(blocks)]
    *outs, scale_t, scale_l, back, row_side, key_side, mix_acc = refs[6 + 3 * blocks :]
    keys, rows = back.shape[1:]
    part, size = rows // row_parts, keys // key_parts
    sums, pieces = outs[0], outs[1:]

    lse_all = []
    for which in range(2):
        parts = [ref[which] for ref in lse]
        best = functools.reduce(jnp.maximum, parts)
        total = sum(jnp.exp2(value - best) for value in parts)
        lse_all.append(best + jnp.log2(total))
    own = lax.broadcasted_iota(jnp.int32, (heads, rows), 1) < part
    loss = jnp.where(own, lse_all[1] - lse_all[0], 0.0)
    mix_acc[...] = jnp.zeros_like(mix_acc)
    offset = 0
    scale_l[...] = jnp.exp2(top_l[...] - lse_all[1])
    for exp_t, top_t, kl in maps:
        scale_t[...] = jnp.exp2(top_t[...] - lse_all[0])
        loss = loss + scale_t[...] * kl[...]
        for start in range(0, exp_t.shape[1], LIFT_BLOCK):
            block = slice(start, start + LIFT_BLOCK)
            place = slice(offset + start, offset + start + LIFT_BLOCK)
            excess = (
                exp_l[:, place, :] * scale_l[...][:, None, :] - exp_t[:, block, :] * scale_t[...][:, None, :]
            )
            high, low = split(excess)
            s_high = stu_hi[:, place, :].reshape(HEADS_S * LIFT_BLOCK, rows)
            s_low = stu_lo[:, place, :].reshape(HEADS_S * LIFT_BLOCK, rows)
            f_high = high.reshape(heads * LIFT_BLOCK, rows)
            f_low = low.reshape(heads * LIFT_BLOCK, rows)
            over_rows = ((1,), (1,))
            mix_acc[...] += dot(f_high, s_high, over_rows) + (
                dot(f_high, s_low, over_rows) + dot(f_low, s_high, over_rows)
            )
            for inner in range(0, LIFT_BLOCK, BACK_BLOCK):
                b_high = high[:, inner : inner + BACK_BLOCK, :].reshape(heads * BACK_BLOCK, rows)
                b_low = low[:, inner : inner + BACK_BLOCK, :].reshape(heads * BACK_BLOCK, rows)
                total = dot(back_hi[...], b_high) + (dot(back_hi[...], b_low) + dot(back_lo[...], b_high))
                first = offset + start + inner
                back[:, first : first + BACK_BLOCK, :] = total.astype(BF16).reshape(HEADS_S, BACK_BLOCK, rows)
        offset += exp_t.shape[1]
    loss = jnp.sum(loss, axis=1, keepdims=True) * LN2

    acc = mix_acc[...].reshape(heads, LIFT_BLOCK, HEADS_S * LIFT_BLOCK)
    sub = lax.broadcasted_iota(jnp.int32, acc.shape, 1)
    within = lax.broadcasted_iota(jnp.int32, acc.shape, 2) & (LIFT_BLOCK - 1)
    diagonal = jnp.sum(jnp.where(sub == within, acc, 0.0), axis=1)
    lane = lax.broadcasted_iota(jnp.int32, diagonal.shape, 1)
    slot = lax.broadcasted_iota(jnp.int32, (heads, LANES), 1)
    packed = jnp.where(slot == HEADS_S, loss, 0.0)
    for index in range(HEADS_S):
        inside = (lane >= index * LIFT_BLOCK) & (lane < (index + 1) * LIFT_BLOCK)
        column = jnp.sum(jnp.where(inside, diagonal, 0.0), axis=1, keepdims=True)
        packed = jnp.where(slot == index, column, packed)
    packed = jnp.concatenate([packed, jnp.zeros((LANES - heads, LANES), F32)], axis=0)
    packed = jnp.transpose(packed)[:RIDE_ROWS]
    sums[...] = packed

    for index in range(HEADS_S):
        columns = slice(index * HD_S, (index + 1) * HD_S)
        row_side[index] = stacked(query_s, columns)
        key_side[index] = stacked(key_s, columns)
    place = lax.axis_index("head")
    per = HEADS_S // shards
    count = row_parts + key_parts - 1
    for shard in range(shards):
        own, *others = pieces[shard * count : (shard + 1) * count]
        first = lax.rem(place + shard, shards) * per
        for index in range(per):
            tile = back[first + index]
            columns = slice(index * HD_S, (index + 1) * HD_S)
            on_keys = dot(tile, row_side[first + index]) * factor
            on_rows = dot(tile, key_side[first + index], ((0,), (0,))) * factor
            own[:part, columns] = on_rows[:part]
            own[part:, columns] = on_keys[:size]
            for spot in range(1, row_parts):
                others[spot - 1][:part, columns] = on_rows[spot * part : (spot + 1) * part]
            for spot in range(1, key_parts):
                others[row_parts + spot - 2][:size, columns] = on_keys[spot * size : (spot + 1) * size]
        for ref in others:
            if ref.shape[0] > part:
                ref[part:, :] = jnp.zeros((RIDE_ROWS, ref.shape[1]), F32)
                ref[part:, :LANES] = packed


def tally_kernel(*refs):
    *parts, total = refs
    value = parts[0][...]
    for ref in parts[1:]:
        value = value + ref[ref.shape[0] - RIDE_ROWS :, :LANES]
    total[...] = value


def finish_kernel(row_parts, key_parts, addends, mix_scale, loss_scale, *refs):
    *pieces, grad_query, grad_key, grad_mix, head_loss = refs
    terms, pieces = pieces[:addends], pieces[addends:]
    part = grad_query.shape[1]
    heads = grad_mix.shape[1]
    count = row_parts + key_parts - 1
    total = terms[0][...]
    for ref in terms[1:]:
        total = total + ref[...]
    grad_mix[...] = total[:HEADS_S, :heads] * mix_scale
    head_loss[...] = total[HEADS_S : HEADS_S + 1, :heads] * loss_scale
    on_rows, on_keys = [], []
    for i, ref in enumerate(pieces):
        if i % count == 0:
            on_rows.append(ref[:part])
            on_keys.append(ref[part:])
        elif i % count < row_parts:
            on_rows.append(ref[:part])
        else:
            on_keys.append(ref[:part])
    grad_query[0] = sum(on_rows[1:], on_rows[0])
    grad_key[0] = sum(on_keys[1:], on_keys[0])


def body(teacher_query, teacher_key, student_query, student_key, head_mix):
    shard_rows = teacher_query.shape[1]
    heads = head_mix.shape[0]
    length = lax.axis_size("seq")
    shards = lax.axis_size("head")
    copies = lax.axis_size("dp")
    row_parts = max(size for size in range(1, math.isqrt(length) + 1) if length % size == 0)
    key_parts = length // row_parts
    rows, keys = row_parts * shard_rows, key_parts * shard_rows

    def along_rows(position, step):
        return position // row_parts * row_parts + (position % row_parts + step) % row_parts

    def along_keys(position, step):
        return (position + step * row_parts) % length

    def fetch(value, target, step):
        return lax.ppermute(value, "seq", [(target(i, step), i) for i in range(length)])

    def deliver(value, target, step, turn):
        pairs = [
            (h * length + i, (h + turn) % shards * length + target(i, step))
            for h in range(shards)
            for i in range(length)
        ]
        return lax.ppermute(value, ("head", "seq"), pairs)

    own = (teacher_key, teacher_query, student_key, student_query)
    key_t = [fetch(teacher_key, along_keys, d) for d in range(1, key_parts)]
    query_t = [fetch(teacher_query, along_rows, d) for d in range(1, row_parts)]
    key_s = [fetch(student_key, along_keys, d) for d in range(1, key_parts)]
    query_s = [fetch(student_query, along_rows, d) for d in range(1, row_parts)]
    *own, lift_hi, lift_lo, back_hi, back_lo = prepare(head_mix, own)
    key_t, query_t, key_s, query_s = [[mine, *rest] for mine, rest in zip(own, (key_t, query_t, key_s, query_s))]

    exponents = pltpu.VMEM((heads, keys, rows), F32)
    student = pltpu.VMEM((HEADS_S, keys, rows), BF16)
    stats = pltpu.VMEM((heads, rows), F32)
    both = pltpu.VMEM((2, heads, rows), F32)
    lifted, exp_l, stu_hi, stu_lo, top_l, lse_l = pl.pallas_call(
        functools.partial(student_kernel, row_parts, key_parts, heads),
        out_shape=(exponents, exponents, student, student, stats, stats),
        compiler_params=pltpu.CompilerParams(vmem_limit_bytes=VMEM_LIMIT),
        cost_estimate=pl.CostEstimate(flops=STUDENT_FLOPS, bytes_accessed=1, transcendentals=1),
        name="student",
    )(*key_s, *query_s, lift_hi, lift_lo)

    def teacher(block_t, offset, before):
        size = len(block_t) * shard_rows
        return pl.pallas_call(
            functools.partial(teacher_kernel, row_parts, len(block_t), heads, offset, bool(before)),
            out_shape=(pltpu.VMEM((heads, size, rows), F32), stats, stats, both) + (both,) * (row_parts - 1),
            compiler_params=pltpu.CompilerParams(vmem_limit_bytes=VMEM_LIMIT),
            name="teacher",
        )(*block_t, *query_t, lifted, lse_l, *before)

    done, before = [], []
    for first, block in ((0, key_t[:1]), (1, key_t[1:])):
        if block:
            results = teacher(block, first * shard_rows, before)
            done.append(results[:3])
            before, turned = results[3:4], results[4:]
    lse_parts = [*before] + [fetch(turned[step - 1], along_rows, row_parts - step) for step in range(1, row_parts)]

    weight = shard_rows * length / HEADS_T
    width = HEADS_S * HD_S // shards
    ride = RIDE_ROWS if width >= LANES else 0
    count = row_parts + key_parts - 1
    shapes = []
    for shard in range(shards):
        extra = ride if shard == 0 else 0
        shapes += [(2 * shard_rows, width)] + [(shard_rows + extra, width)] * (row_parts - 1)
        shapes += [(shard_rows, width)] * (key_parts - 1)
    sums, *pieces = pl.pallas_call(
        functools.partial(
            back_kernel, row_parts, key_parts, shards, len(done), heads, weight * HD_S ** (-0.5)
        ),
        out_shape=[jax.ShapeDtypeStruct(shape, F32) for shape in [(RIDE_ROWS, LANES)] + shapes],
        scratch_shapes=[
            pltpu.VMEM((heads, rows), F32),
            pltpu.VMEM((heads, rows), F32),
            pltpu.VMEM((HEADS_S, keys, rows), BF16),
            pltpu.VMEM((HEADS_S, rows, HD_S), BF16),
            pltpu.VMEM((HEADS_S, keys, HD_S), BF16),
            pltpu.VMEM((heads * LIFT_BLOCK, HEADS_S * LIFT_BLOCK), F32),
        ],
        compiler_params=pltpu.CompilerParams(vmem_limit_bytes=VMEM_LIMIT),
        name="back",
    )(
        *query_s, *key_s, *lse_parts, back_hi, back_lo, exp_l, stu_hi, stu_lo, top_l,
        *[ref for block in done for ref in block],
    )

    moves = [(along_rows, step) for step in range(row_parts)] + [(along_keys, step) for step in range(1, key_parts)]
    arrived = [deliver(part, *moves[i % count], i // count) if i else part for i, part in enumerate(pieces)]
    small = functools.partial(pl.pallas_call, compiler_params=pltpu.CompilerParams(vmem_limit_bytes=VMEM_LIMIT // 4))

    def everyone(value, axis):
        size = lax.axis_size(axis)
        if size & (size - 1) == 0:
            for bit in range(size.bit_length() - 1):
                value = value + lax.ppermute(value, axis, [(i, i ^ (1 << bit)) for i in range(size)])
            return value
        mine = value
        for step in range(1, size):
            value = value + lax.ppermute(mine, axis, [(i, (i + step) % size) for i in range(size)])
        return value

    others = arrived[1:row_parts] if ride else [fetch(sums, along_rows, step) for step in range(1, row_parts)]
    total = small(tally_kernel, out_shape=jax.ShapeDtypeStruct((RIDE_ROWS, LANES), F32), name="tally")(sums, *others)
    total = everyone(total, "dp")
    terms = [total] + [fetch(total, along_keys, step) for step in range(1, key_parts)]

    grad = jax.ShapeDtypeStruct((1, shard_rows, width), F32)
    samples = copies * teacher_query.shape[0] * shard_rows * length
    scales = (HD_S ** (-0.5) * weight / samples, 1.0 / samples)
    grad_query, grad_key, grad_mix, head_loss = small(
        functools.partial(finish_kernel, row_parts, key_parts, len(terms), *scales),
        out_shape=(
            grad,
            grad,
            jax.ShapeDtypeStruct((HEADS_S, heads), F32),
            jax.ShapeDtypeStruct((1, heads), F32),
        ),
        name="finish",
    )(*terms, *arrived)
    return (grad_query, grad_key, grad_mix.T, head_loss[0])


def solution(mesh):
    return jax.shard_map(
        body,
        mesh=mesh,
        in_specs=(
            P("dp", "seq", "head"),
            P("dp", "seq", "head"),
            P("dp", "seq", None),
            P("dp", "seq", None),
            P("head", None),
        ),
        out_specs=(P("dp", "seq", "head"), P("dp", "seq", "head"), P("head", None), P("head")),
        check_vma=False,
    )
```

```python
import functools
import math

import jax
import jax.numpy as jnp
from jax import lax
from jax.experimental import pallas as pl
from jax.experimental.pallas import tpu as pltpu
from jax.sharding import PartitionSpec as P

HEADS_T = 24
HD_T = 128
HEADS_S = 8
HD_S = 64
LOG2E = math.log2(math.e)
LN2 = math.log(2.0)
LIFT_BLOCK = 32
BACK_BLOCK = 16
RIDE_ROWS = 16
LANES = 128
STUDENT_FLOPS = 64 * 10**8
VMEM_LIMIT = 8 * 1024 * 1024

F32 = jnp.float32
BF16 = jnp.bfloat16
F16 = jnp.float16
MIX_TOP = 0.25
VALUE_TOP = 6.0


def dot(lhs, rhs, dims=((1,), (0,))):
    return lax.dot_general(lhs, rhs, (dims, ((), ())), preferred_element_type=F32)


def room(bound):
    return 2.0 ** math.floor(math.log2(float(jnp.finfo(F16).max) / (1.01 * bound)))


def split(value):
    high = value.astype(BF16)
    low = (value - high.astype(F32)).astype(BF16)
    return high, low


def prepare_kernel(count, mix_ref, mix_tr_ref, *refs):
    sources, targets = refs[:count], refs[count : 2 * count]
    lift_hi, lift_lo, back_hi, back_lo, semaphores = refs[2 * count :]
    moves = [pltpu.make_async_copy(sources[i], targets[i], semaphores.at[i]) for i in range(count)]
    for move in moves:
        move.start()

    def kron(values, size):
        rows, columns = values.shape
        lane = lax.broadcasted_iota(jnp.int32, (rows, columns * size), 1)
        spread = jnp.zeros((rows, columns * size), F32)
        for index in range(columns):
            inside = (lane >= index * size) & (lane < (index + 1) * size)
            spread = jnp.where(inside, values[:, index : index + 1], spread)
        full = (rows, size, columns * size)
        sub = lax.broadcasted_iota(jnp.int32, full, 1)
        within = lax.broadcasted_iota(jnp.int32, full, 2) & (size - 1)
        picked = jnp.where(sub == within, spread[:, None, :], 0.0)
        return picked.reshape(rows * size, columns * size)

    scaled = mix_ref[...] * (HD_S ** (-0.5) * LOG2E)
    lift_hi[...], lift_lo[...] = split(kron(scaled, LIFT_BLOCK))
    back_hi[...], back_lo[...] = split(kron(mix_tr_ref[...], BACK_BLOCK))
    for move in moves:
        move.wait()


def prepare(head_mix, arrays):
    heads = head_mix.shape[0]
    lift = pltpu.VMEM((heads * LIFT_BLOCK, HEADS_S * LIFT_BLOCK), BF16)
    back = pltpu.VMEM((HEADS_S * BACK_BLOCK, heads * BACK_BLOCK), BF16)
    count = len(arrays)
    whole = pl.BlockSpec(memory_space=pltpu.VMEM)
    return pl.pallas_call(
        functools.partial(prepare_kernel, count),
        out_shape=[pltpu.VMEM(array.shape, array.dtype) for array in arrays] + [lift, lift, back, back],
        in_specs=[whole, whole] + [pl.BlockSpec(memory_space=pl.ANY)] * count,
        scratch_shapes=[pltpu.SemaphoreType.DMA((count,))],
        compiler_params=pltpu.CompilerParams(vmem_limit_bytes=VMEM_LIMIT // 2),
        name="prepare",
    )(head_mix, head_mix.T, *arrays)


def stacked(refs, columns):
    parts = [ref[0, :, columns] for ref in refs]
    return parts[0] if len(parts) == 1 else jnp.concatenate(parts, axis=0)


def student_kernel(row_parts, key_parts, heads, *refs):
    key_s, query_s, refs = refs[:key_parts], refs[key_parts : key_parts + row_parts], refs[key_parts + row_parts :]
    lift_hi, lift_lo, lifted, exp_l, stu_hi, stu_lo, top, lse = refs
    keys, rows = stu_hi.shape[1:]
    for index in range(HEADS_S):
        columns = slice(index * HD_S, (index + 1) * HD_S)
        student = dot(stacked(key_s, columns), stacked(query_s, columns), ((1,), (1,)))
        stu_hi[index], stu_lo[index] = split(student)
    for start in range(0, keys, LIFT_BLOCK):
        block = slice(start, start + LIFT_BLOCK)
        high = stu_hi[:, block, :].reshape(HEADS_S * LIFT_BLOCK, rows)
        low = stu_lo[:, block, :].reshape(HEADS_S * LIFT_BLOCK, rows)
        total = dot(lift_hi[...], high) + (dot(lift_hi[...], low) + dot(lift_lo[...], high))
        lifted[:, block, :] = total.reshape(heads, LIFT_BLOCK, rows)
    for head in range(heads):
        mixed = lifted[head]
        best = jnp.max(mixed, axis=0, keepdims=True)
        prob = jnp.exp2(mixed - best)
        exp_l[head] = prob
        top[head : head + 1, :] = best
        lse[head : head + 1, :] = best + jnp.log2(jnp.sum(prob, axis=0, keepdims=True))


def teacher_kernel(row_parts, key_parts, heads, offset, carried, *refs):
    key_t, query_t, refs = refs[:key_parts], refs[key_parts : key_parts + row_parts], refs[key_parts + row_parts :]
    lifted, lse_l, *refs = refs
    before = refs.pop(0) if carried else None
    exp_t, top, kl, lse, *turned = refs
    keys, rows = exp_t.shape[1:]
    for head in range(heads):
        columns = slice(head * HD_T, (head + 1) * HD_T)
        teacher = dot(stacked(key_t, columns), stacked(query_t, columns), ((1,), (1,)))
        teacher = teacher * (HD_T ** (-0.5) * LOG2E)
        best = jnp.max(teacher, axis=0, keepdims=True)
        prob = jnp.exp2(teacher - best)
        exp_t[head] = prob
        mixed = lifted[head, offset : offset + keys, :]
        kl[head : head + 1, :] = jnp.sum(prob * (teacher - mixed), axis=0, keepdims=True)
        top[head : head + 1, :] = best
        total = jnp.sum(prob, axis=0, keepdims=True)
        if carried:
            earlier = before[0, head : head + 1, :]
            higher = jnp.maximum(best, earlier)
            total = total * jnp.exp2(best - higher) + jnp.exp2(earlier - higher)
            best = higher
        lse[0, head : head + 1, :] = best + jnp.log2(total)
    lse[1] = lse_l[...]
    part = rows // row_parts
    for step, ref in enumerate(turned, 1):
        for spot in range(row_parts):
            source = (spot + step) % row_parts * part
            ref[:, :, spot * part : (spot + 1) * part] = lse[:, :, source : source + part]


def back_kernel(row_parts, key_parts, shards, blocks, heads, factors, *refs):
    refs = list(refs)
    query_s = [refs.pop(0) for _ in range(row_parts)]
    key_s = [refs.pop(0) for _ in range(key_parts)]
    lse = [refs.pop(0) for _ in range(row_parts)]
    back_hi, back_lo, exp_l, stu_hi, stu_lo, top_l = refs[:6]
    maps = [refs[6 + 3 * i : 9 + 3 * i] for i in range(blocks)]
    *outs, scale_t, scale_l, back, row_side, key_side, mix_acc = refs[6 + 3 * blocks :]
    keys, rows = back.shape[1:]
    part, size = rows // row_parts, keys // key_parts
    sums, pieces = outs[0], outs[1:]

    lse_all = []
    for which in range(2):
        parts = [ref[which] for ref in lse]
        best = functools.reduce(jnp.maximum, parts)
        total = sum(jnp.exp2(value - best) for value in parts)
        lse_all.append(best + jnp.log2(total))
    own = lax.broadcasted_iota(jnp.int32, (heads, rows), 1) < part
    loss = jnp.where(own, lse_all[1] - lse_all[0], 0.0)
    mix_acc[...] = jnp.zeros_like(mix_acc)
    offset = 0
    scale_l[...] = jnp.exp2(top_l[...] - lse_all[1])
    for exp_t, top_t, kl in maps:
        scale_t[...] = jnp.exp2(top_t[...] - lse_all[0])
        loss = loss + scale_t[...] * kl[...]
        for start in range(0, exp_t.shape[1], LIFT_BLOCK):
            block = slice(start, start + LIFT_BLOCK)
            place = slice(offset + start, offset + start + LIFT_BLOCK)
            excess = (
                exp_l[:, place, :] * scale_l[...][:, None, :] - exp_t[:, block, :] * scale_t[...][:, None, :]
            )
            high, low = split(excess)
            s_high = stu_hi[:, place, :].reshape(HEADS_S * LIFT_BLOCK, rows)
            s_low = stu_lo[:, place, :].reshape(HEADS_S * LIFT_BLOCK, rows)
            f_high = high.reshape(heads * LIFT_BLOCK, rows)
            f_low = low.reshape(heads * LIFT_BLOCK, rows)
            over_rows = ((1,), (1,))
            mix_acc[...] += dot(f_high, s_high, over_rows) + (
                dot(f_high, s_low, over_rows) + dot(f_low, s_high, over_rows)
            )
            for inner in range(0, LIFT_BLOCK, BACK_BLOCK):
                b_high = high[:, inner : inner + BACK_BLOCK, :].reshape(heads * BACK_BLOCK, rows)
                b_low = low[:, inner : inner + BACK_BLOCK, :].reshape(heads * BACK_BLOCK, rows)
                total = dot(back_hi[...], b_high) + (dot(back_hi[...], b_low) + dot(back_lo[...], b_high))
                first = offset + start + inner
                back[:, first : first + BACK_BLOCK, :] = total.astype(BF16).reshape(HEADS_S, BACK_BLOCK, rows)
        offset += exp_t.shape[1]
    loss = jnp.sum(loss, axis=1, keepdims=True) * LN2

    acc = mix_acc[...].reshape(heads, LIFT_BLOCK, HEADS_S * LIFT_BLOCK)
    sub = lax.broadcasted_iota(jnp.int32, acc.shape, 1)
    within = lax.broadcasted_iota(jnp.int32, acc.shape, 2) & (LIFT_BLOCK - 1)
    diagonal = jnp.sum(jnp.where(sub == within, acc, 0.0), axis=1)
    lane = lax.broadcasted_iota(jnp.int32, diagonal.shape, 1)
    slot = lax.broadcasted_iota(jnp.int32, (heads, LANES), 1)
    packed = jnp.where(slot == HEADS_S, loss, 0.0)
    for index in range(HEADS_S):
        inside = (lane >= index * LIFT_BLOCK) & (lane < (index + 1) * LIFT_BLOCK)
        column = jnp.sum(jnp.where(inside, diagonal, 0.0), axis=1, keepdims=True)
        packed = jnp.where(slot == index, column, packed)
    packed = jnp.concatenate([packed, jnp.zeros((LANES - heads, LANES), F32)], axis=0)
    packed = jnp.transpose(packed)[:RIDE_ROWS]
    sums[...] = packed

    for index in range(HEADS_S):
        columns = slice(index * HD_S, (index + 1) * HD_S)
        row_side[index] = stacked(query_s, columns)
        key_side[index] = stacked(key_s, columns)
    place = lax.axis_index("head")
    per = HEADS_S // shards
    count = row_parts + key_parts - 1
    for shard in range(shards):
        own, *others = pieces[shard * count : (shard + 1) * count]
        first = lax.rem(place + shard, shards) * per
        for index in range(per):
            tile = back[first + index]
            columns = slice(index * HD_S, (index + 1) * HD_S)
            on_keys = dot(tile, row_side[first + index]) * factors[1]
            on_rows = dot(tile, key_side[first + index], ((0,), (0,))) * factors[0]
            own[:part, columns] = on_rows[:part]
            own[part:, columns] = on_keys[:size]
            for spot in range(1, row_parts):
                others[spot - 1][:part, columns] = on_rows[spot * part : (spot + 1) * part]
            for spot in range(1, key_parts):
                others[row_parts + spot - 2][:size, columns] = on_keys[spot * size : (spot + 1) * size]
        for ref in others:
            if ref.shape[0] > part:
                high, low = split(packed * factors[2])
                ref[part:, :LANES] = high.astype(F32)
                ref[part:, LANES:] = low.astype(F32)


def close_kernel(mix_scale, loss_scale, total, grad_mix, head_loss):
    heads = grad_mix.shape[1]
    grad_mix[...] = total[:HEADS_S, :heads] * mix_scale
    head_loss[...] = total[HEADS_S : HEADS_S + 1, :heads] * loss_scale


def body(teacher_query, teacher_key, student_query, student_key, head_mix):
    shard_rows = teacher_query.shape[1]
    heads = head_mix.shape[0]
    length = lax.axis_size("seq")
    shards = lax.axis_size("head")
    copies = lax.axis_size("dp")
    row_parts = max(size for size in range(1, math.isqrt(length) + 1) if length % size == 0)
    key_parts = length // row_parts
    rows, keys = row_parts * shard_rows, key_parts * shard_rows

    def along_rows(position, step):
        return position // row_parts * row_parts + (position % row_parts + step) % row_parts

    def along_keys(position, step):
        return (position + step * row_parts) % length

    def fetch(value, target, step):
        return lax.ppermute(value, "seq", [(target(i, step), i) for i in range(length)])

    def deliver(value, target, step, turn):
        pairs = [
            (h * length + i, (h + turn) % shards * length + target(i, step))
            for h in range(shards)
            for i in range(length)
        ]
        return lax.ppermute(value, ("head", "seq"), pairs)

    own = (teacher_key, teacher_query, student_key, student_query)
    key_t = [fetch(teacher_key, along_keys, d) for d in range(1, key_parts)]
    query_t = [fetch(teacher_query, along_rows, d) for d in range(1, row_parts)]
    key_s = [fetch(student_key, along_keys, d) for d in range(1, key_parts)]
    query_s = [fetch(student_query, along_rows, d) for d in range(1, row_parts)]
    *own, lift_hi, lift_lo, back_hi, back_lo = prepare(head_mix, own)
    key_t, query_t, key_s, query_s = [[mine, *rest] for mine, rest in zip(own, (key_t, query_t, key_s, query_s))]

    exponents = pltpu.VMEM((heads, keys, rows), F32)
    student = pltpu.VMEM((HEADS_S, keys, rows), BF16)
    stats = pltpu.VMEM((heads, rows), F32)
    both = pltpu.VMEM((2, heads, rows), F32)
    lifted, exp_l, stu_hi, stu_lo, top_l, lse_l = pl.pallas_call(
        functools.partial(student_kernel, row_parts, key_parts, heads),
        out_shape=(exponents, exponents, student, student, stats, stats),
        compiler_params=pltpu.CompilerParams(vmem_limit_bytes=VMEM_LIMIT),
        cost_estimate=pl.CostEstimate(flops=STUDENT_FLOPS, bytes_accessed=1, transcendentals=1),
        name="student",
    )(*key_s, *query_s, lift_hi, lift_lo)

    def teacher(block_t, offset, before):
        size = len(block_t) * shard_rows
        return pl.pallas_call(
            functools.partial(teacher_kernel, row_parts, len(block_t), heads, offset, bool(before)),
            out_shape=(pltpu.VMEM((heads, size, rows), F32), stats, stats, both) + (both,) * (row_parts - 1),
            compiler_params=pltpu.CompilerParams(vmem_limit_bytes=VMEM_LIMIT),
            name="teacher",
        )(*block_t, *query_t, lifted, lse_l, *before)

    done, before = [], []
    for first, block in ((0, key_t[:1]), (1, key_t[1:])):
        if block:
            results = teacher(block, first * shard_rows, before)
            done.append(results[:3])
            before, turned = results[3:4], results[4:]
    lse_parts = [*before] + [fetch(turned[step - 1], along_rows, row_parts - step) for step in range(1, row_parts)]

    weight = shard_rows * length / HEADS_T
    width = HEADS_S * HD_S // shards
    ride = RIDE_ROWS if width == 2 * LANES else 0
    factor = weight * HD_S ** (-0.5)
    room_query = room(2.0 * heads * MIX_TOP * VALUE_TOP * factor)
    room_key = room(rows * heads * MIX_TOP * VALUE_TOP * factor)
    room_sums = room(2.0 * rows * HD_S * VALUE_TOP**2)
    count = row_parts + key_parts - 1
    shapes = []
    for shard in range(shards):
        extra = ride if shard == 0 else 0
        shapes += [(2 * shard_rows, width)] + [(shard_rows + extra, width)] * (count - 1)
    sums, *pieces = pl.pallas_call(
        functools.partial(
            back_kernel,
            row_parts,
            key_parts,
            shards,
            len(done),
            heads,
            (factor * room_query, factor * room_key, room_sums),
        ),
        out_shape=[jax.ShapeDtypeStruct(shape, F32) for shape in [(RIDE_ROWS, LANES)] + shapes],
        scratch_shapes=[
            pltpu.VMEM((heads, rows), F32),
            pltpu.VMEM((heads, rows), F32),
            pltpu.VMEM((HEADS_S, keys, rows), BF16),
            pltpu.VMEM((HEADS_S, rows, HD_S), BF16),
            pltpu.VMEM((HEADS_S, keys, HD_S), BF16),
            pltpu.VMEM((heads * LIFT_BLOCK, HEADS_S * LIFT_BLOCK), F32),
        ],
        compiler_params=pltpu.CompilerParams(vmem_limit_bytes=VMEM_LIMIT),
        name="back",
    )(
        *query_s, *key_s, *lse_parts, back_hi, back_lo, exp_l, stu_hi, stu_lo, top_l,
        *[ref for block in done for ref in block],
    )

    moves = [(along_rows, step) for step in range(row_parts)] + [(along_keys, step) for step in range(1, key_parts)]
    arrived = [
        deliver(part.astype(F16), *moves[i % count], i // count) if i else part for i, part in enumerate(pieces)
    ]
    small = functools.partial(pl.pallas_call, compiler_params=pltpu.CompilerParams(vmem_limit_bytes=VMEM_LIMIT // 4))

    def diagonal(across, along):
        return lambda position, _: along_keys(along_rows(position, across), along)

    if ride:
        rides = [part[shard_rows:].astype(F32) for part in arrived[1:count]]
        others = [(part[:, :LANES] + part[:, LANES:]) * (1.0 / room_sums) for part in rides]
    else:
        others = [fetch(sums, target, step) for target, step in moves[1:]]
    for across in range(1, row_parts):
        others += [fetch(sums, diagonal(across, along), 0) for along in range(1, key_parts)]
    total = sum(others, sums)
    if copies & (copies - 1) == 0:
        for bit in range(copies.bit_length() - 1):
            total = total + lax.ppermute(total, "dp", [(i, i ^ (1 << bit)) for i in range(copies)])
    else:
        mine = total
        for step in range(1, copies):
            total = total + lax.ppermute(mine, "dp", [(i, (i + step) % copies) for i in range(copies)])

    for_query = [part[:shard_rows].astype(F32) for i, part in enumerate(arrived) if i % count < row_parts]
    for_key = [
        part[-shard_rows:].astype(F32) if i % count == 0 else part[:shard_rows].astype(F32)
        for i, part in enumerate(arrived)
        if i % count == 0 or i % count >= row_parts
    ]
    grad_query = (sum(for_query[1:], for_query[0]) * (1.0 / room_query))[None]
    grad_key = (sum(for_key[1:], for_key[0]) * (1.0 / room_key))[None]
    samples = copies * teacher_query.shape[0] * shard_rows * length
    grad_mix, head_loss = small(
        functools.partial(close_kernel, HD_S ** (-0.5) * weight / samples, 1.0 / samples),
        out_shape=(jax.ShapeDtypeStruct((HEADS_S, heads), F32), jax.ShapeDtypeStruct((1, heads), F32)),
        name="close",
    )(total)
    return (grad_query, grad_key, grad_mix.T, head_loss[0])


def solution(mesh):
    return jax.shard_map(
        body,
        mesh=mesh,
        in_specs=(
            P("dp", "seq", "head"),
            P("dp", "seq", "head"),
            P("dp", "seq", None),
            P("dp", "seq", None),
            P("head", None),
        ),
        out_specs=(P("dp", "seq", "head"), P("dp", "seq", "head"), P("head", None), P("head")),
        check_vma=False,
    )
```

```python
import functools
import math

import jax
import jax.numpy as jnp
from jax import lax
from jax.experimental import pallas as pl
from jax.experimental.pallas import tpu as pltpu
from jax.sharding import PartitionSpec as P

HEADS_T = 24
HD_T = 128
HEADS_S = 8
HD_S = 64
LOG2E = math.log2(math.e)
LN2 = math.log(2.0)
LIFT_BLOCK = 32
BACK_BLOCK = 16
RIDE_ROWS = 16
LANES = 128
STUDENT_FLOPS = 64 * 10**8
VMEM_LIMIT = 8 * 1024 * 1024

F32 = jnp.float32
BF16 = jnp.bfloat16
F16 = jnp.float16
MIX_TOP = 0.25
VALUE_TOP = 6.0


def dot(lhs, rhs, dims=((1,), (0,))):
    return lax.dot_general(lhs, rhs, (dims, ((), ())), preferred_element_type=F32)


def room(bound):
    return 2.0 ** math.floor(math.log2(float(jnp.finfo(F16).max) / (1.01 * bound)))


def split(value):
    high = value.astype(BF16)
    low = (value - high.astype(F32)).astype(BF16)
    return high, low


def prepare_kernel(count, mix_ref, mix_tr_ref, *refs):
    sources, targets = refs[:count], refs[count : 2 * count]
    lift_hi, lift_lo, back_both, semaphores = refs[2 * count :]
    moves = [pltpu.make_async_copy(sources[i], targets[i], semaphores.at[i]) for i in range(count)]
    for move in moves:
        move.start()

    def kron(values, size):
        rows, columns = values.shape
        lane = lax.broadcasted_iota(jnp.int32, (rows, columns * size), 1)
        spread = jnp.zeros((rows, columns * size), F32)
        for index in range(columns):
            inside = (lane >= index * size) & (lane < (index + 1) * size)
            spread = jnp.where(inside, values[:, index : index + 1], spread)
        full = (rows, size, columns * size)
        sub = lax.broadcasted_iota(jnp.int32, full, 1)
        within = lax.broadcasted_iota(jnp.int32, full, 2) & (size - 1)
        picked = jnp.where(sub == within, spread[:, None, :], 0.0)
        return picked.reshape(rows * size, columns * size)

    scaled = mix_ref[...] * (HD_S ** (-0.5) * LOG2E)
    lift_hi[...], lift_lo[...] = split(kron(scaled, LIFT_BLOCK))
    high, low = split(kron(mix_tr_ref[...], BACK_BLOCK))
    back_both[: high.shape[0]] = high
    back_both[high.shape[0] :] = low
    for move in moves:
        move.wait()


def prepare(head_mix, arrays):
    heads = head_mix.shape[0]
    lift = pltpu.VMEM((heads * LIFT_BLOCK, HEADS_S * LIFT_BLOCK), BF16)
    back = pltpu.VMEM((2 * HEADS_S * BACK_BLOCK, heads * BACK_BLOCK), BF16)
    count = len(arrays)
    whole = pl.BlockSpec(memory_space=pltpu.VMEM)
    return pl.pallas_call(
        functools.partial(prepare_kernel, count),
        out_shape=[pltpu.VMEM(array.shape, array.dtype) for array in arrays] + [lift, lift, back],
        in_specs=[whole, whole] + [pl.BlockSpec(memory_space=pl.ANY)] * count,
        scratch_shapes=[pltpu.SemaphoreType.DMA((count,))],
        compiler_params=pltpu.CompilerParams(vmem_limit_bytes=VMEM_LIMIT // 2),
        name="prepare",
    )(head_mix, head_mix.T, *arrays)


def stacked(refs, columns):
    parts = [ref[0, :, columns] for ref in refs]
    return parts[0] if len(parts) == 1 else jnp.concatenate(parts, axis=0)


def student_kernel(row_parts, key_parts, heads, *refs):
    key_s, query_s, refs = refs[:key_parts], refs[key_parts : key_parts + row_parts], refs[key_parts + row_parts :]
    lift_hi, lift_lo, lifted, exp_l, stu_hi, stu_lo, top, lse = refs
    keys, rows = stu_hi.shape[1:]
    for index in range(HEADS_S):
        columns = slice(index * HD_S, (index + 1) * HD_S)
        student = dot(stacked(key_s, columns), stacked(query_s, columns), ((1,), (1,)))
        stu_hi[index], stu_lo[index] = split(student)
    for start in range(0, keys, LIFT_BLOCK):
        block = slice(start, start + LIFT_BLOCK)
        high = stu_hi[:, block, :].reshape(HEADS_S * LIFT_BLOCK, rows)
        low = stu_lo[:, block, :].reshape(HEADS_S * LIFT_BLOCK, rows)
        total = dot(lift_hi[...], high) + (dot(lift_hi[...], low) + dot(lift_lo[...], high))
        lifted[:, block, :] = total.reshape(heads, LIFT_BLOCK, rows)
    for head in range(heads):
        mixed = lifted[head]
        best = jnp.max(mixed, axis=0, keepdims=True)
        prob = jnp.exp2(mixed - best)
        exp_l[head] = prob
        top[head : head + 1, :] = best
        lse[head : head + 1, :] = best + jnp.log2(jnp.sum(prob, axis=0, keepdims=True))


def teacher_kernel(row_parts, key_parts, heads, offset, carried, *refs):
    key_t, query_t, refs = refs[:key_parts], refs[key_parts : key_parts + row_parts], refs[key_parts + row_parts :]
    lifted, lse_l, *refs = refs
    before = refs.pop(0) if carried else None
    exp_t, top, kl, lse, *turned = refs
    keys, rows = exp_t.shape[1:]
    for head in range(heads):
        columns = slice(head * HD_T, (head + 1) * HD_T)
        teacher = dot(stacked(key_t, columns), stacked(query_t, columns), ((1,), (1,)))
        teacher = teacher * (HD_T ** (-0.5) * LOG2E)
        best = jnp.max(teacher, axis=0, keepdims=True)
        prob = jnp.exp2(teacher - best)
        exp_t[head] = prob
        mixed = lifted[head, offset : offset + keys, :]
        kl[head : head + 1, :] = jnp.sum(prob * (teacher - mixed), axis=0, keepdims=True)
        top[head : head + 1, :] = best
        total = jnp.sum(prob, axis=0, keepdims=True)
        if carried:
            earlier = before[0, head : head + 1, :]
            higher = jnp.maximum(best, earlier)
            total = total * jnp.exp2(best - higher) + jnp.exp2(earlier - higher)
            best = higher
        lse[0, head : head + 1, :] = best + jnp.log2(total)
    lse[1] = lse_l[...]
    part = rows // row_parts
    for step, ref in enumerate(turned, 1):
        for spot in range(row_parts):
            source = (spot + step) % row_parts * part
            ref[:, :, spot * part : (spot + 1) * part] = lse[:, :, source : source + part]


def back_kernel(row_parts, key_parts, shards, blocks, heads, factors, *refs):
    refs = list(refs)
    query_s = [refs.pop(0) for _ in range(row_parts)]
    key_s = [refs.pop(0) for _ in range(key_parts)]
    lse = [refs.pop(0) for _ in range(row_parts)]
    back_both, exp_l, stu_hi, stu_lo, top_l = refs[:5]
    maps = [refs[5 + 3 * i : 8 + 3 * i] for i in range(blocks)]
    *outs, scale_t, scale_l, back, row_side, key_side, mix_acc = refs[5 + 3 * blocks :]
    keys, rows = back.shape[1:]
    part, size = rows // row_parts, keys // key_parts
    sums, pieces = outs[0], outs[1:]

    lse_all = []
    for which in range(2):
        parts = [ref[which] for ref in lse]
        best = functools.reduce(jnp.maximum, parts)
        total = sum(jnp.exp2(value - best) for value in parts)
        lse_all.append(best + jnp.log2(total))
    own = lax.broadcasted_iota(jnp.int32, (heads, rows), 1) < part
    loss = jnp.where(own, lse_all[1] - lse_all[0], 0.0)
    mix_acc[...] = jnp.zeros_like(mix_acc)
    offset = 0
    scale_l[...] = jnp.exp2(top_l[...] - lse_all[1])
    for exp_t, top_t, kl in maps:
        scale_t[...] = jnp.exp2(top_t[...] - lse_all[0])
        loss = loss + scale_t[...] * kl[...]
        for start in range(0, exp_t.shape[1], LIFT_BLOCK):
            block = slice(start, start + LIFT_BLOCK)
            place = slice(offset + start, offset + start + LIFT_BLOCK)
            excess = (
                exp_l[:, place, :] * scale_l[...][:, None, :] - exp_t[:, block, :] * scale_t[...][:, None, :]
            )
            high, low = split(excess)
            s_high = stu_hi[:, place, :].reshape(HEADS_S * LIFT_BLOCK, rows)
            s_low = stu_lo[:, place, :].reshape(HEADS_S * LIFT_BLOCK, rows)
            f_high = high.reshape(heads * LIFT_BLOCK, rows)
            f_low = low.reshape(heads * LIFT_BLOCK, rows)
            over_rows = ((1,), (1,))
            mix_acc[...] += dot(f_high, s_high, over_rows) + (
                dot(f_high, s_low, over_rows) + dot(f_low, s_high, over_rows)
            )
            for inner in range(0, LIFT_BLOCK, BACK_BLOCK):
                b_high = high[:, inner : inner + BACK_BLOCK, :].reshape(heads * BACK_BLOCK, rows)
                b_low = low[:, inner : inner + BACK_BLOCK, :].reshape(heads * BACK_BLOCK, rows)
                half = HEADS_S * BACK_BLOCK
                twice = dot(back_both[...], b_high)
                total = twice[:half] + (dot(back_both[:half], b_low) + twice[half:])
                first = offset + start + inner
                back[:, first : first + BACK_BLOCK, :] = total.astype(BF16).reshape(HEADS_S, BACK_BLOCK, rows)
        offset += exp_t.shape[1]
    loss = jnp.sum(loss, axis=1, keepdims=True) * LN2

    acc = mix_acc[...].reshape(heads, LIFT_BLOCK, HEADS_S * LIFT_BLOCK)
    sub = lax.broadcasted_iota(jnp.int32, acc.shape, 1)
    within = lax.broadcasted_iota(jnp.int32, acc.shape, 2) & (LIFT_BLOCK - 1)
    diagonal = jnp.sum(jnp.where(sub == within, acc, 0.0), axis=1)
    lane = lax.broadcasted_iota(jnp.int32, diagonal.shape, 1)
    slot = lax.broadcasted_iota(jnp.int32, (heads, LANES), 1)
    packed = jnp.where(slot == HEADS_S, loss, 0.0)
    for index in range(HEADS_S):
        inside = (lane >= index * LIFT_BLOCK) & (lane < (index + 1) * LIFT_BLOCK)
        column = jnp.sum(jnp.where(inside, diagonal, 0.0), axis=1, keepdims=True)
        packed = jnp.where(slot == index, column, packed)
    packed = jnp.concatenate([packed, jnp.zeros((LANES - heads, LANES), F32)], axis=0)
    packed = jnp.transpose(packed)[:RIDE_ROWS]
    sums[...] = packed

    for index in range(HEADS_S):
        columns = slice(index * HD_S, (index + 1) * HD_S)
        row_side[index] = stacked(query_s, columns)
        key_side[index] = stacked(key_s, columns)
    place = lax.axis_index("head")
    per = HEADS_S // shards
    count = row_parts + key_parts - 1
    for shard in range(shards):
        own, *others = pieces[shard * count : (shard + 1) * count]
        first = lax.rem(place + shard, shards) * per
        for index in range(per):
            tile = back[first + index]
            columns = slice(index * HD_S, (index + 1) * HD_S)
            on_keys = dot(tile, row_side[first + index]) * factors[1]
            on_rows = dot(tile, key_side[first + index], ((0,), (0,))) * factors[0]
            own[:part, columns] = on_rows[:part]
            own[part:, columns] = on_keys[:size]
            for spot in range(1, row_parts):
                others[spot - 1][:part, columns] = on_rows[spot * part : (spot + 1) * part]
            for spot in range(1, key_parts):
                others[row_parts + spot - 2][:size, columns] = on_keys[spot * size : (spot + 1) * size]
        for ref in others:
            if ref.shape[0] > part:
                high, low = split(packed * factors[2])
                ref[part:, :LANES] = high.astype(F32)
                ref[part:, LANES:] = low.astype(F32)


def close_kernel(mix_scale, loss_scale, total, grad_mix, head_loss):
    heads = grad_mix.shape[1]
    grad_mix[...] = total[:HEADS_S, :heads] * mix_scale
    head_loss[...] = total[HEADS_S : HEADS_S + 1, :heads] * loss_scale


def body(teacher_query, teacher_key, student_query, student_key, head_mix):
    shard_rows = teacher_query.shape[1]
    heads = head_mix.shape[0]
    length = lax.axis_size("seq")
    shards = lax.axis_size("head")
    copies = lax.axis_size("dp")
    row_parts = max(size for size in range(1, math.isqrt(length) + 1) if length % size == 0)
    key_parts = length // row_parts
    rows, keys = row_parts * shard_rows, key_parts * shard_rows

    def along_rows(position, step):
        return position // row_parts * row_parts + (position % row_parts + step) % row_parts

    def along_keys(position, step):
        return (position + step * row_parts) % length

    def fetch(value, target, step):
        return lax.ppermute(value, "seq", [(target(i, step), i) for i in range(length)])

    def deliver(value, target, step, turn):
        pairs = [
            (h * length + i, (h + turn) % shards * length + target(i, step))
            for h in range(shards)
            for i in range(length)
        ]
        return lax.ppermute(value, ("head", "seq"), pairs)

    own = (teacher_key, teacher_query, student_key, student_query)
    key_t = [fetch(teacher_key, along_keys, d) for d in range(1, key_parts)]
    query_t = [fetch(teacher_query, along_rows, d) for d in range(1, row_parts)]
    key_s = [fetch(student_key, along_keys, d) for d in range(1, key_parts)]
    query_s = [fetch(student_query, along_rows, d) for d in range(1, row_parts)]
    *own, lift_hi, lift_lo, back_both = prepare(head_mix, own)
    key_t, query_t, key_s, query_s = [[mine, *rest] for mine, rest in zip(own, (key_t, query_t, key_s, query_s))]

    exponents = pltpu.VMEM((heads, keys, rows), F32)
    student = pltpu.VMEM((HEADS_S, keys, rows), BF16)
    stats = pltpu.VMEM((heads, rows), F32)
    both = pltpu.VMEM((2, heads, rows), F32)
    lifted, exp_l, stu_hi, stu_lo, top_l, lse_l = pl.pallas_call(
        functools.partial(student_kernel, row_parts, key_parts, heads),
        out_shape=(exponents, exponents, student, student, stats, stats),
        compiler_params=pltpu.CompilerParams(vmem_limit_bytes=VMEM_LIMIT),
        cost_estimate=pl.CostEstimate(flops=STUDENT_FLOPS, bytes_accessed=1, transcendentals=1),
        name="student",
    )(*key_s, *query_s, lift_hi, lift_lo)

    def teacher(block_t, offset, before):
        size = len(block_t) * shard_rows
        return pl.pallas_call(
            functools.partial(teacher_kernel, row_parts, len(block_t), heads, offset, bool(before)),
            out_shape=(pltpu.VMEM((heads, size, rows), F32), stats, stats, both) + (both,) * (row_parts - 1),
            compiler_params=pltpu.CompilerParams(vmem_limit_bytes=VMEM_LIMIT),
            name="teacher",
        )(*block_t, *query_t, lifted, lse_l, *before)

    done, before = [], []
    for first, block in ((0, key_t[:1]), (1, key_t[1:])):
        if block:
            results = teacher(block, first * shard_rows, before)
            done.append(results[:3])
            before, turned = results[3:4], results[4:]
    lse_parts = [*before] + [fetch(turned[step - 1], along_rows, row_parts - step) for step in range(1, row_parts)]

    weight = shard_rows * length / HEADS_T
    width = HEADS_S * HD_S // shards
    ride = RIDE_ROWS if width == 2 * LANES else 0
    factor = weight * HD_S ** (-0.5)
    room_query = room(2.0 * heads * MIX_TOP * VALUE_TOP * factor)
    room_key = room(rows * heads * MIX_TOP * VALUE_TOP * factor)
    room_sums = room(2.0 * rows * HD_S * VALUE_TOP**2)
    count = row_parts + key_parts - 1
    shapes = []
    for shard in range(shards):
        extra = ride if shard == 0 else 0
        shapes += [(2 * shard_rows, width)] + [(shard_rows + extra, width)] * (count - 1)
    sums, *pieces = pl.pallas_call(
        functools.partial(
            back_kernel,
            row_parts,
            key_parts,
            shards,
            len(done),
            heads,
            (factor * room_query, factor * room_key, room_sums),
        ),
        out_shape=[jax.ShapeDtypeStruct(shape, F32) for shape in [(RIDE_ROWS, LANES)] + shapes],
        scratch_shapes=[
            pltpu.VMEM((heads, rows), F32),
            pltpu.VMEM((heads, rows), F32),
            pltpu.VMEM((HEADS_S, keys, rows), BF16),
            pltpu.VMEM((HEADS_S, rows, HD_S), BF16),
            pltpu.VMEM((HEADS_S, keys, HD_S), BF16),
            pltpu.VMEM((heads * LIFT_BLOCK, HEADS_S * LIFT_BLOCK), F32),
        ],
        compiler_params=pltpu.CompilerParams(vmem_limit_bytes=VMEM_LIMIT),
        name="back",
    )(
        *query_s, *key_s, *lse_parts, back_both, exp_l, stu_hi, stu_lo, top_l,
        *[ref for block in done for ref in block],
    )

    moves = [(along_rows, step) for step in range(row_parts)] + [(along_keys, step) for step in range(1, key_parts)]
    arrived = [
        deliver(part.astype(F16), *moves[i % count], i // count) if i else part for i, part in enumerate(pieces)
    ]
    small = functools.partial(pl.pallas_call, compiler_params=pltpu.CompilerParams(vmem_limit_bytes=VMEM_LIMIT // 4))

    def diagonal(across, along):
        return lambda position, _: along_keys(along_rows(position, across), along)

    if ride:
        rides = [part[shard_rows:].astype(F32) for part in arrived[1:count]]
        others = [(part[:, :LANES] + part[:, LANES:]) * (1.0 / room_sums) for part in rides]
    else:
        others = [fetch(sums, target, step) for target, step in moves[1:]]
    for across in range(1, row_parts):
        others += [fetch(sums, diagonal(across, along), 0) for along in range(1, key_parts)]
    total = sum(others, sums)
    for_query = [part[:shard_rows].astype(F32) for i, part in enumerate(arrived) if i % count < row_parts]
    for_key = [
        part[-shard_rows:].astype(F32) if i % count == 0 else part[:shard_rows].astype(F32)
        for i, part in enumerate(arrived)
        if i % count == 0 or i % count >= row_parts
    ]
    grad_query = (sum(for_query[1:], for_query[0]) * (1.0 / room_query))[None]
    grad_key = (sum(for_key[1:], for_key[0]) * (1.0 / room_key))[None]
    last = total
    if copies > 1 and copies & (copies - 1) == 0:
        for bit in range(copies.bit_length() - 1):
            total = total if bit == 0 else total + last
            last = lax.ppermute(total, "dp", [(i, i ^ (1 << bit)) for i in range(copies)])
    else:
        last = sum(
            [lax.ppermute(total, "dp", [(i, (i + step) % copies) for i in range(copies)]) for step in range(1, copies)],
            jnp.zeros_like(total),
        )
    last, grad_query, grad_key = lax.optimization_barrier((last, grad_query, grad_key))
    total = total + last
    samples = copies * teacher_query.shape[0] * shard_rows * length
    grad_mix, head_loss = small(
        functools.partial(close_kernel, HD_S ** (-0.5) * weight / samples, 1.0 / samples),
        out_shape=(jax.ShapeDtypeStruct((HEADS_S, heads), F32), jax.ShapeDtypeStruct((1, heads), F32)),
        name="close",
    )(total)
    return (grad_query, grad_key, grad_mix.T, head_loss[0])


def solution(mesh):
    return jax.shard_map(
        body,
        mesh=mesh,
        in_specs=(
            P("dp", "seq", "head"),
            P("dp", "seq", "head"),
            P("dp", "seq", None),
            P("dp", "seq", None),
            P("head", None),
        ),
        out_specs=(P("dp", "seq", "head"), P("dp", "seq", "head"), P("head", None), P("head")),
        check_vma=False,
    )
```

```python
import functools
import math

import jax
import jax.numpy as jnp
from jax import lax
from jax.experimental import pallas as pl
from jax.experimental.pallas import tpu as pltpu
from jax.sharding import PartitionSpec as P

HEADS_T = 24
HD_T = 128
HEADS_S = 8
HD_S = 64
LOG2E = math.log2(math.e)
LN2 = math.log(2.0)
LIFT_BLOCK = 32
BACK_BLOCK = 16
RIDE_ROWS = 16
LANES = 128
STUDENT_FLOPS = 30*10**8
VMEM_LIMIT = 8 * 1024 * 1024

F32 = jnp.float32
BF16 = jnp.bfloat16
F16 = jnp.float16
MIX_TOP = 0.25
VALUE_TOP = 6.0


def dot(lhs, rhs, dims=((1,), (0,))):
    return lax.dot_general(lhs, rhs, (dims, ((), ())), preferred_element_type=F32)


def room(bound):
    return 2.0 ** math.floor(math.log2(float(jnp.finfo(F16).max) / (1.01 * bound)))


def split(value):
    high = value.astype(BF16)
    low = (value - high.astype(F32)).astype(BF16)
    return high, low


def prepare_kernel(count, mix_ref, mix_tr_ref, *refs):
    sources, targets = refs[:count], refs[count : 2 * count]
    lift_hi, lift_lo, back_both, semaphores = refs[2 * count :]
    moves = [pltpu.make_async_copy(sources[i], targets[i], semaphores.at[i]) for i in range(count)]
    for move in moves:
        move.start()

    def kron(values, size):
        rows, columns = values.shape
        lane = lax.broadcasted_iota(jnp.int32, (rows, columns * size), 1)
        spread = jnp.zeros((rows, columns * size), F32)
        for index in range(columns):
            inside = (lane >= index * size) & (lane < (index + 1) * size)
            spread = jnp.where(inside, values[:, index : index + 1], spread)
        full = (rows, size, columns * size)
        sub = lax.broadcasted_iota(jnp.int32, full, 1)
        within = lax.broadcasted_iota(jnp.int32, full, 2) & (size - 1)
        picked = jnp.where(sub == within, spread[:, None, :], 0.0)
        return picked.reshape(rows * size, columns * size)

    scaled = mix_ref[...] * (HD_S ** (-0.5) * LOG2E)
    lift_hi[...], lift_lo[...] = split(kron(scaled, LIFT_BLOCK))
    high, low = split(kron(mix_tr_ref[...], BACK_BLOCK))
    back_both[: high.shape[0]] = high
    back_both[high.shape[0] :] = low
    for move in moves:
        move.wait()


def prepare(head_mix, arrays):
    heads = head_mix.shape[0]
    lift = pltpu.VMEM((heads * LIFT_BLOCK, HEADS_S * LIFT_BLOCK), BF16)
    back = pltpu.VMEM((2 * HEADS_S * BACK_BLOCK, heads * BACK_BLOCK), BF16)
    count = len(arrays)
    whole = pl.BlockSpec(memory_space=pltpu.VMEM)
    return pl.pallas_call(
        functools.partial(prepare_kernel, count),
        out_shape=[pltpu.VMEM(array.shape, array.dtype) for array in arrays] + [lift, lift, back],
        in_specs=[whole, whole] + [pl.BlockSpec(memory_space=pl.ANY)] * count,
        scratch_shapes=[pltpu.SemaphoreType.DMA((count,))],
        compiler_params=pltpu.CompilerParams(vmem_limit_bytes=VMEM_LIMIT // 2),
        name="prepare",
    )(head_mix, head_mix.T, *arrays)


def stacked(refs, columns):
    parts = [ref[0, :, columns] for ref in refs]
    return parts[0] if len(parts) == 1 else jnp.concatenate(parts, axis=0)


def share_kernel(count, *refs):
    sources, targets, semaphores = refs[:count], refs[count : 2 * count], refs[-1]
    size = targets[0].shape[1]
    start = pl.multiple_of(lax.axis_index("head") * size, size)
    moves = [
        pltpu.make_async_copy(source.at[:, pl.ds(start, size), :], target, semaphores.at[i])
        for i, (source, target) in enumerate(zip(sources, targets))
    ]
    for move in moves:
        move.start()
    for move in moves:
        move.wait()


def by_head(shards, pieces, side):
    place = lax.axis_index("head")
    own, *others = pieces
    part = own.shape[1]
    for index in range(HEADS_S):
        columns = slice(index * HD_S, (index + 1) * HD_S)
        side[index, :part] = own[0, :, columns]
        for i, piece in enumerate(others):
            size = piece.shape[1]
            first = (i // shards + 1) * part + lax.rem(place + shards - i % shards, shards) * size
            side[index, pl.ds(pl.multiple_of(first, size), size), :] = piece[0, :, columns]


def student_kernel(counts, shards, heads, *refs):
    key_s, query_s, refs = refs[: counts[0]], refs[counts[0] : sum(counts)], refs[sum(counts) :]
    lift_hi, lift_lo, lifted, exp_l, stu_hi, stu_lo, top, lse, key_side, query_side = refs
    keys, rows = stu_hi.shape[1:]
    by_head(shards, key_s, key_side)
    by_head(shards, query_s, query_side)
    for index in range(HEADS_S):
        stu_hi[index], stu_lo[index] = split(dot(key_side[index], query_side[index], ((1,), (1,))))
    for start in range(0, keys, LIFT_BLOCK):
        block = slice(start, start + LIFT_BLOCK)
        high = stu_hi[:, block, :].reshape(HEADS_S * LIFT_BLOCK, rows)
        low = stu_lo[:, block, :].reshape(HEADS_S * LIFT_BLOCK, rows)
        total = dot(lift_hi[...], high) + (dot(lift_hi[...], low) + dot(lift_lo[...], high))
        lifted[:, block, :] = total.reshape(heads, LIFT_BLOCK, rows)
    for head in range(heads):
        mixed = lifted[head]
        best = jnp.max(mixed, axis=0, keepdims=True)
        prob = jnp.exp2(mixed - best)
        exp_l[head] = prob
        top[head : head + 1, :] = best
        lse[head : head + 1, :] = best + jnp.log2(jnp.sum(prob, axis=0, keepdims=True))


def teacher_kernel(row_parts, key_parts, heads, offset, carried, *refs):
    key_t, query_t, refs = refs[:key_parts], refs[key_parts : key_parts + row_parts], refs[key_parts + row_parts :]
    lifted, lse_l, *refs = refs
    before = refs.pop(0) if carried else None
    exp_t, top, kl, lse, *turned = refs
    keys, rows = exp_t.shape[1:]
    for head in range(heads):
        columns = slice(head * HD_T, (head + 1) * HD_T)
        teacher = dot(stacked(key_t, columns), stacked(query_t, columns), ((1,), (1,)))
        teacher = teacher * (HD_T ** (-0.5) * LOG2E)
        best = jnp.max(teacher, axis=0, keepdims=True)
        prob = jnp.exp2(teacher - best)
        exp_t[head] = prob
        mixed = lifted[head, offset : offset + keys, :]
        kl[head : head + 1, :] = jnp.sum(prob * (teacher - mixed), axis=0, keepdims=True)
        top[head : head + 1, :] = best
        total = jnp.sum(prob, axis=0, keepdims=True)
        if carried:
            earlier = before[0, head : head + 1, :]
            higher = jnp.maximum(best, earlier)
            total = total * jnp.exp2(best - higher) + jnp.exp2(earlier - higher)
            best = higher
        lse[0, head : head + 1, :] = best + jnp.log2(total)
    lse[1] = lse_l[...]
    part = rows // row_parts
    for step, ref in enumerate(turned, 1):
        for spot in range(row_parts):
            source = (spot + step) % row_parts * part
            ref[:, :, spot * part : (spot + 1) * part] = lse[:, :, source : source + part]


def back_kernel(row_parts, key_parts, shards, blocks, heads, factors, *refs):
    refs = list(refs)
    row_side, key_side = refs.pop(0), refs.pop(0)
    lse = [refs.pop(0) for _ in range(row_parts)]
    back_both, exp_l, stu_hi, stu_lo, top_l = refs[:5]
    maps = [refs[5 + 3 * i : 8 + 3 * i] for i in range(blocks)]
    *outs, scale_t, scale_l, back, mix_acc = refs[5 + 3 * blocks :]
    keys, rows = back.shape[1:]
    part, size = rows // row_parts, keys // key_parts
    sums, pieces = outs[0], outs[1:]

    lse_all = []
    for which in range(2):
        parts = [ref[which] for ref in lse]
        best = functools.reduce(jnp.maximum, parts)
        total = sum(jnp.exp2(value - best) for value in parts)
        lse_all.append(best + jnp.log2(total))
    own = lax.broadcasted_iota(jnp.int32, (heads, rows), 1) < part
    loss = jnp.where(own, lse_all[1] - lse_all[0], 0.0)
    mix_acc[...] = jnp.zeros_like(mix_acc)
    offset = 0
    scale_l[...] = jnp.exp2(top_l[...] - lse_all[1])
    for exp_t, top_t, kl in maps:
        scale_t[...] = jnp.exp2(top_t[...] - lse_all[0])
        loss = loss + scale_t[...] * kl[...]
        for start in range(0, exp_t.shape[1], LIFT_BLOCK):
            block = slice(start, start + LIFT_BLOCK)
            place = slice(offset + start, offset + start + LIFT_BLOCK)
            excess = (
                exp_l[:, place, :] * scale_l[...][:, None, :] - exp_t[:, block, :] * scale_t[...][:, None, :]
            )
            high, low = split(excess)
            s_high = stu_hi[:, place, :].reshape(HEADS_S * LIFT_BLOCK, rows)
            s_low = stu_lo[:, place, :].reshape(HEADS_S * LIFT_BLOCK, rows)
            f_high = high.reshape(heads * LIFT_BLOCK, rows)
            f_low = low.reshape(heads * LIFT_BLOCK, rows)
            over_rows = ((1,), (1,))
            mix_acc[...] += dot(f_high, s_high, over_rows) + (
                dot(f_high, s_low, over_rows) + dot(f_low, s_high, over_rows)
            )
            for inner in range(0, LIFT_BLOCK, BACK_BLOCK):
                b_high = high[:, inner : inner + BACK_BLOCK, :].reshape(heads * BACK_BLOCK, rows)
                b_low = low[:, inner : inner + BACK_BLOCK, :].reshape(heads * BACK_BLOCK, rows)
                half = HEADS_S * BACK_BLOCK
                twice = dot(back_both[...], b_high)
                total = twice[:half] + (dot(back_both[:half], b_low) + twice[half:])
                first = offset + start + inner
                back[:, first : first + BACK_BLOCK, :] = total.astype(BF16).reshape(HEADS_S, BACK_BLOCK, rows)
        offset += exp_t.shape[1]
    loss = jnp.sum(loss, axis=1, keepdims=True) * LN2

    acc = mix_acc[...].reshape(heads, LIFT_BLOCK, HEADS_S * LIFT_BLOCK)
    sub = lax.broadcasted_iota(jnp.int32, acc.shape, 1)
    within = lax.broadcasted_iota(jnp.int32, acc.shape, 2) & (LIFT_BLOCK - 1)
    diagonal = jnp.sum(jnp.where(sub == within, acc, 0.0), axis=1)
    lane = lax.broadcasted_iota(jnp.int32, diagonal.shape, 1)
    slot = lax.broadcasted_iota(jnp.int32, (heads, LANES), 1)
    packed = jnp.where(slot == HEADS_S, loss, 0.0)
    for index in range(HEADS_S):
        inside = (lane >= index * LIFT_BLOCK) & (lane < (index + 1) * LIFT_BLOCK)
        column = jnp.sum(jnp.where(inside, diagonal, 0.0), axis=1, keepdims=True)
        packed = jnp.where(slot == index, column, packed)
    packed = jnp.concatenate([packed, jnp.zeros((LANES - heads, LANES), F32)], axis=0)
    packed = jnp.transpose(packed)[:RIDE_ROWS]
    sums[...] = packed

    place = lax.axis_index("head")
    per = HEADS_S // shards
    count = row_parts + key_parts - 1
    for shard in range(shards):
        own, *others = pieces[shard * count : (shard + 1) * count]
        first = lax.rem(place + shard, shards) * per
        for index in range(per):
            tile = back[first + index]
            columns = slice(index * HD_S, (index + 1) * HD_S)
            on_keys = dot(tile, row_side[first + index]) * factors[1]
            on_rows = dot(tile, key_side[first + index], ((0,), (0,))) * factors[0]
            own[:part, columns] = on_rows[:part]
            own[part:, columns] = on_keys[:size]
            for spot in range(1, row_parts):
                others[spot - 1][:part, columns] = on_rows[spot * part : (spot + 1) * part]
            for spot in range(1, key_parts):
                others[row_parts + spot - 2][:size, columns] = on_keys[spot * size : (spot + 1) * size]
        for ref in others:
            if ref.shape[0] > part:
                high, low = split(packed * factors[2])
                ref[part:, :LANES] = high.astype(F32)
                ref[part:, LANES:] = low.astype(F32)


def close_kernel(mix_scale, loss_scale, total, grad_mix, head_loss):
    heads = grad_mix.shape[1]
    grad_mix[...] = total[:HEADS_S, :heads] * mix_scale
    head_loss[...] = total[HEADS_S : HEADS_S + 1, :heads] * loss_scale


def body(teacher_query, teacher_key, student_query, student_key, head_mix):
    shard_rows = teacher_query.shape[1]
    heads = head_mix.shape[0]
    length = lax.axis_size("seq")
    shards = lax.axis_size("head")
    copies = lax.axis_size("dp")
    row_parts = max(size for size in range(1, math.isqrt(length) + 1) if length % size == 0)
    key_parts = length // row_parts
    rows, keys = row_parts * shard_rows, key_parts * shard_rows

    def along_rows(position, step):
        return position // row_parts * row_parts + (position % row_parts + step) % row_parts

    def along_keys(position, step):
        return (position + step * row_parts) % length

    def fetch(value, target, step):
        return lax.ppermute(value, "seq", [(target(i, step), i) for i in range(length)])

    def deliver(value, target, step, turn):
        pairs = [
            (h * length + i, (h + turn) % shards * length + target(i, step))
            for h in range(shards)
            for i in range(length)
        ]
        return lax.ppermute(value, ("head", "seq"), pairs)

    own = (teacher_key, teacher_query, student_key, student_query)
    key_t = [fetch(teacher_key, along_keys, d) for d in range(1, key_parts)]
    query_t = [fetch(teacher_query, along_rows, d) for d in range(1, row_parts)]
    share = pltpu.VMEM((1, shard_rows // shards, HEADS_S * HD_S), BF16)
    shares = pl.pallas_call(
        functools.partial(share_kernel, 2),
        out_shape=(share, share),
        in_specs=[pl.BlockSpec(memory_space=pl.ANY)] * 2,
        scratch_shapes=[pltpu.SemaphoreType.DMA((2,))],
        compiler_params=pltpu.CompilerParams(vmem_limit_bytes=VMEM_LIMIT // 4),
        name="share",
    )(*[pltpu.with_memory_space_constraint(array, pltpu.HBM) for array in (student_key, student_query)])

    def fetch_student(value, target, step):
        value = fetch(value, target, step)
        turns = [[(h, (h + turn) % shards) for h in range(shards)] for turn in range(1, shards)]
        return [value] + [lax.ppermute(value, "head", pairs) for pairs in turns]

    key_s = [piece for d in range(1, key_parts) for piece in fetch_student(shares[0], along_keys, d)]
    query_s = [piece for d in range(1, row_parts) for piece in fetch_student(shares[1], along_rows, d)]
    *own, lift_hi, lift_lo, back_both = prepare(head_mix, own)
    key_t, query_t, key_s, query_s = [[mine, *rest] for mine, rest in zip(own, (key_t, query_t, key_s, query_s))]

    exponents = pltpu.VMEM((heads, keys, rows), F32)
    student = pltpu.VMEM((HEADS_S, keys, rows), BF16)
    stats = pltpu.VMEM((heads, rows), F32)
    both = pltpu.VMEM((2, heads, rows), F32)
    sides = [pltpu.VMEM((HEADS_S, size, HD_S), BF16) for size in (keys, rows)]
    lifted, exp_l, stu_hi, stu_lo, top_l, lse_l, key_side, row_side = pl.pallas_call(
        functools.partial(student_kernel, (len(key_s), len(query_s)), shards, heads),
        out_shape=(exponents, exponents, student, student, stats, stats, *sides),
        compiler_params=pltpu.CompilerParams(vmem_limit_bytes=VMEM_LIMIT),
        cost_estimate=pl.CostEstimate(flops=STUDENT_FLOPS, bytes_accessed=1, transcendentals=1),
        name="student",
    )(*key_s, *query_s, lift_hi, lift_lo)

    def teacher(block_t, offset, before):
        size = len(block_t) * shard_rows
        return pl.pallas_call(
            functools.partial(teacher_kernel, row_parts, len(block_t), heads, offset, bool(before)),
            out_shape=(pltpu.VMEM((heads, size, rows), F32), stats, stats, both) + (both,) * (row_parts - 1),
            compiler_params=pltpu.CompilerParams(vmem_limit_bytes=VMEM_LIMIT),
            name="teacher",
        )(*block_t, *query_t, lifted, lse_l, *before)

    done, before = [], []
    for first, block in ((0, key_t[:1]), (1, key_t[1:])):
        if block:
            results = teacher(block, first * shard_rows, before)
            done.append(results[:3])
            before, turned = results[3:4], results[4:]
    lse_parts = [*before] + [fetch(turned[step - 1], along_rows, row_parts - step) for step in range(1, row_parts)]

    weight = shard_rows * length / HEADS_T
    width = HEADS_S * HD_S // shards
    ride = RIDE_ROWS if width == 2 * LANES else 0
    factor = weight * HD_S ** (-0.5)
    room_query = room(2.0 * heads * MIX_TOP * VALUE_TOP * factor)
    room_key = room(rows * heads * MIX_TOP * VALUE_TOP * factor)
    room_sums = room(2.0 * rows * HD_S * VALUE_TOP**2)
    count = row_parts + key_parts - 1
    shapes = []
    for shard in range(shards):
        extra = ride if shard == 0 else 0
        shapes += [(2 * shard_rows, width)] + [(shard_rows + extra, width)] * (count - 1)
    sums, *pieces = pl.pallas_call(
        functools.partial(
            back_kernel,
            row_parts,
            key_parts,
            shards,
            len(done),
            heads,
            (factor * room_query, factor * room_key, room_sums),
        ),
        out_shape=[jax.ShapeDtypeStruct(shape, F32) for shape in [(RIDE_ROWS, LANES)] + shapes],
        scratch_shapes=[
            pltpu.VMEM((heads, rows), F32),
            pltpu.VMEM((heads, rows), F32),
            pltpu.VMEM((HEADS_S, keys, rows), BF16),
            pltpu.VMEM((heads * LIFT_BLOCK, HEADS_S * LIFT_BLOCK), F32),
        ],
        compiler_params=pltpu.CompilerParams(vmem_limit_bytes=VMEM_LIMIT),
        name="back",
    )(
        row_side, key_side, *lse_parts, back_both, exp_l, stu_hi, stu_lo, top_l,
        *[ref for block in done for ref in block],
    )

    moves = [(along_rows, step) for step in range(row_parts)] + [(along_keys, step) for step in range(1, key_parts)]
    arrived = [
        deliver(part.astype(F16), *moves[i % count], i // count) if i else part for i, part in enumerate(pieces)
    ]
    small = functools.partial(pl.pallas_call, compiler_params=pltpu.CompilerParams(vmem_limit_bytes=VMEM_LIMIT // 4))

    def diagonal(across, along):
        return lambda position, _: along_keys(along_rows(position, across), along)

    if ride:
        rides = [part[shard_rows:].astype(F32) for part in arrived[1:count]]
        others = [(part[:, :LANES] + part[:, LANES:]) * (1.0 / room_sums) for part in rides]
    else:
        others = [fetch(sums, target, step) for target, step in moves[1:]]
    for across in range(1, row_parts):
        others += [fetch(sums, diagonal(across, along), 0) for along in range(1, key_parts)]
    total = sum(others, sums)
    for_query = [part[:shard_rows].astype(F32) for i, part in enumerate(arrived) if i % count < row_parts]
    for_key = [
        part[-shard_rows:].astype(F32) if i % count == 0 else part[:shard_rows].astype(F32)
        for i, part in enumerate(arrived)
        if i % count == 0 or i % count >= row_parts
    ]
    grad_query = (sum(for_query[1:], for_query[0]) * (1.0 / room_query))[None]
    grad_key = (sum(for_key[1:], for_key[0]) * (1.0 / room_key))[None]
    last = total
    if copies > 1 and copies & (copies - 1) == 0:
        for bit in range(copies.bit_length() - 1):
            total = total if bit == 0 else total + last
            last = lax.ppermute(total, "dp", [(i, i ^ (1 << bit)) for i in range(copies)])
    else:
        last = sum(
            [lax.ppermute(total, "dp", [(i, (i + step) % copies) for i in range(copies)]) for step in range(1, copies)],
            jnp.zeros_like(total),
        )
    last, grad_query, grad_key = lax.optimization_barrier((last, grad_query, grad_key))
    total = total + last
    samples = copies * teacher_query.shape[0] * shard_rows * length
    grad_mix, head_loss = small(
        functools.partial(close_kernel, HD_S ** (-0.5) * weight / samples, 1.0 / samples),
        out_shape=(jax.ShapeDtypeStruct((HEADS_S, heads), F32), jax.ShapeDtypeStruct((1, heads), F32)),
        name="close",
    )(total)
    return (grad_query, grad_key, grad_mix.T, head_loss[0])


def solution(mesh):
    return jax.shard_map(
        body,
        mesh=mesh,
        in_specs=(
            P("dp", "seq", "head"),
            P("dp", "seq", "head"),
            P("dp", "seq", None),
            P("dp", "seq", None),
            P("head", None),
        ),
        out_specs=(P("dp", "seq", "head"), P("dp", "seq", "head"), P("head", None), P("head")),
        check_vma=False,
    )
```

```python
import functools
import math

import jax
import jax.numpy as jnp
from jax import lax
from jax.experimental import pallas as pl
from jax.experimental.pallas import tpu as pltpu
from jax.sharding import PartitionSpec as P

HEADS_T = 24
HD_T = 128
HEADS_S = 8
HD_S = 64
LOG2E = math.log2(math.e)
LN2 = math.log(2.0)
LIFT_BLOCK = 32
BACK_BLOCK = 16
RIDE_ROWS = 16
LANES = 128
STUDENT_FLOPS = 30*10**8
VMEM_LIMIT = 8 * 1024 * 1024

F32 = jnp.float32
BF16 = jnp.bfloat16
F16 = jnp.float16
MIX_TOP = 0.25
VALUE_TOP = 6.0


def dot(lhs, rhs, dims=((1,), (0,))):
    return lax.dot_general(lhs, rhs, (dims, ((), ())), preferred_element_type=F32)


def room(bound):
    return 2.0 ** math.floor(math.log2(float(jnp.finfo(F16).max) / (1.01 * bound)))


def split(value):
    high = value.astype(BF16)
    low = (value - high.astype(F32)).astype(BF16)
    return high, low


def prepare_kernel(count, mix_ref, mix_tr_ref, *refs):
    sources, targets = refs[:count], refs[count : 2 * count]
    lift_hi, lift_lo, back_both, semaphores = refs[2 * count :]
    moves = [pltpu.make_async_copy(sources[i], targets[i], semaphores.at[i]) for i in range(count)]
    for move in moves:
        move.start()

    def kron(values, size):
        rows, columns = values.shape
        lane = lax.broadcasted_iota(jnp.int32, (rows, columns * size), 1)
        spread = jnp.zeros((rows, columns * size), F32)
        for index in range(columns):
            inside = (lane >= index * size) & (lane < (index + 1) * size)
            spread = jnp.where(inside, values[:, index : index + 1], spread)
        full = (rows, size, columns * size)
        sub = lax.broadcasted_iota(jnp.int32, full, 1)
        within = lax.broadcasted_iota(jnp.int32, full, 2) & (size - 1)
        picked = jnp.where(sub == within, spread[:, None, :], 0.0)
        return picked.reshape(rows * size, columns * size)

    scaled = mix_ref[...] * (HD_S ** (-0.5) * LOG2E)
    lift_hi[...], lift_lo[...] = split(kron(scaled, LIFT_BLOCK))
    high, low = split(kron(mix_tr_ref[...], BACK_BLOCK))
    back_both[: high.shape[0]] = high
    back_both[high.shape[0] :] = low
    for move in moves:
        move.wait()


def prepare(head_mix, arrays):
    heads = head_mix.shape[0]
    lift = pltpu.VMEM((heads * LIFT_BLOCK, HEADS_S * LIFT_BLOCK), BF16)
    back = pltpu.VMEM((2 * HEADS_S * BACK_BLOCK, heads * BACK_BLOCK), BF16)
    count = len(arrays)
    whole = pl.BlockSpec(memory_space=pltpu.VMEM)
    return pl.pallas_call(
        functools.partial(prepare_kernel, count),
        out_shape=[pltpu.VMEM(array.shape, array.dtype) for array in arrays] + [lift, lift, back],
        in_specs=[whole, whole] + [pl.BlockSpec(memory_space=pl.ANY)] * count,
        scratch_shapes=[pltpu.SemaphoreType.DMA((count,))],
        compiler_params=pltpu.CompilerParams(vmem_limit_bytes=VMEM_LIMIT // 2),
        name="prepare",
    )(head_mix, head_mix.T, *[pltpu.with_memory_space_constraint(array, pltpu.HBM) for array in arrays])


def stacked(refs, columns):
    parts = [ref[0, :, columns] for ref in refs]
    return parts[0] if len(parts) == 1 else jnp.concatenate(parts, axis=0)


def share_kernel(count, *refs):
    sources, targets, semaphores = refs[:count], refs[count : 2 * count], refs[-1]
    size = targets[0].shape[1]
    start = pl.multiple_of(lax.axis_index("head") * size, size)
    moves = [
        pltpu.make_async_copy(source.at[:, pl.ds(start, size), :], target, semaphores.at[i])
        for i, (source, target) in enumerate(zip(sources, targets))
    ]
    for move in moves:
        move.start()
    for move in moves:
        move.wait()


def by_head(shards, pieces, side):
    place = lax.axis_index("head")
    own, *others = pieces
    part = own.shape[1]
    for index in range(HEADS_S):
        columns = slice(index * HD_S, (index + 1) * HD_S)
        side[index, :part] = own[0, :, columns]
        for i, piece in enumerate(others):
            size = piece.shape[1]
            first = (i // shards + 1) * part + lax.rem(place + shards - i % shards, shards) * size
            side[index, pl.ds(pl.multiple_of(first, size), size), :] = piece[0, :, columns]


def student_kernel(counts, shards, heads, *refs):
    key_s, query_s, refs = refs[: counts[0]], refs[counts[0] : sum(counts)], refs[sum(counts) :]
    lift_hi, lift_lo, lifted, exp_l, stu_hi, stu_lo, top, lse, key_side, query_side = refs
    keys, rows = stu_hi.shape[1:]
    by_head(shards, key_s, key_side)
    by_head(shards, query_s, query_side)
    for index in range(HEADS_S):
        stu_hi[index], stu_lo[index] = split(dot(key_side[index], query_side[index], ((1,), (1,))))
    for start in range(0, keys, LIFT_BLOCK):
        block = slice(start, start + LIFT_BLOCK)
        high = stu_hi[:, block, :].reshape(HEADS_S * LIFT_BLOCK, rows)
        low = stu_lo[:, block, :].reshape(HEADS_S * LIFT_BLOCK, rows)
        total = dot(lift_hi[...], high) + (dot(lift_hi[...], low) + dot(lift_lo[...], high))
        lifted[:, block, :] = total.reshape(heads, LIFT_BLOCK, rows)
    for head in range(heads):
        mixed = lifted[head]
        best = jnp.max(mixed, axis=0, keepdims=True)
        prob = jnp.exp2(mixed - best)
        exp_l[head] = prob
        top[head : head + 1, :] = best
        lse[head : head + 1, :] = best + jnp.log2(jnp.sum(prob, axis=0, keepdims=True))


def teacher_kernel(row_parts, key_parts, heads, offset, carried, *refs):
    key_t, query_t, refs = refs[:key_parts], refs[key_parts : key_parts + row_parts], refs[key_parts + row_parts :]
    lifted, lse_l, *refs = refs
    before = refs.pop(0) if carried else None
    exp_t, top, kl, lse, *turned = refs
    keys, rows = exp_t.shape[1:]
    for head in range(heads):
        columns = slice(head * HD_T, (head + 1) * HD_T)
        teacher = dot(stacked(key_t, columns), stacked(query_t, columns), ((1,), (1,)))
        teacher = teacher * (HD_T ** (-0.5) * LOG2E)
        best = jnp.max(teacher, axis=0, keepdims=True)
        prob = jnp.exp2(teacher - best)
        exp_t[head] = prob
        mixed = lifted[head, offset : offset + keys, :]
        kl[head : head + 1, :] = jnp.sum(prob * (teacher - mixed), axis=0, keepdims=True)
        top[head : head + 1, :] = best
        total = jnp.sum(prob, axis=0, keepdims=True)
        if carried:
            earlier = before[0, head : head + 1, :]
            higher = jnp.maximum(best, earlier)
            total = total * jnp.exp2(best - higher) + jnp.exp2(earlier - higher)
            best = higher
        lse[0, head : head + 1, :] = best + jnp.log2(total)
    lse[1] = lse_l[...]
    part = rows // row_parts
    for step, ref in enumerate(turned, 1):
        for spot in range(row_parts):
            source = (spot + step) % row_parts * part
            ref[:, :, spot * part : (spot + 1) * part] = lse[:, :, source : source + part]


def back_kernel(row_parts, key_parts, shards, blocks, heads, factors, *refs):
    refs = list(refs)
    row_side, key_side = refs.pop(0), refs.pop(0)
    lse = [refs.pop(0) for _ in range(row_parts)]
    back_both, exp_l, stu_hi, stu_lo, top_l = refs[:5]
    maps = [refs[5 + 3 * i : 8 + 3 * i] for i in range(blocks)]
    *outs, scale_t, scale_l, back, mix_acc = refs[5 + 3 * blocks :]
    keys, rows = back.shape[1:]
    part, size = rows // row_parts, keys // key_parts
    sums, pieces = outs[0], outs[1:]

    lse_all = []
    for which in range(2):
        parts = [ref[which] for ref in lse]
        best = functools.reduce(jnp.maximum, parts)
        total = sum(jnp.exp2(value - best) for value in parts)
        lse_all.append(best + jnp.log2(total))
    own = lax.broadcasted_iota(jnp.int32, (heads, rows), 1) < part
    loss = jnp.where(own, lse_all[1] - lse_all[0], 0.0)
    mix_acc[...] = jnp.zeros_like(mix_acc)
    offset = 0
    scale_l[...] = jnp.exp2(top_l[...] - lse_all[1])
    for exp_t, top_t, kl in maps:
        scale_t[...] = jnp.exp2(top_t[...] - lse_all[0])
        loss = loss + scale_t[...] * kl[...]
        for start in range(0, exp_t.shape[1], LIFT_BLOCK):
            block = slice(start, start + LIFT_BLOCK)
            place = slice(offset + start, offset + start + LIFT_BLOCK)
            excess = (
                exp_l[:, place, :] * scale_l[...][:, None, :] - exp_t[:, block, :] * scale_t[...][:, None, :]
            )
            high, low = split(excess)
            s_high = stu_hi[:, place, :].reshape(HEADS_S * LIFT_BLOCK, rows)
            s_low = stu_lo[:, place, :].reshape(HEADS_S * LIFT_BLOCK, rows)
            f_high = high.reshape(heads * LIFT_BLOCK, rows)
            f_low = low.reshape(heads * LIFT_BLOCK, rows)
            over_rows = ((1,), (1,))
            mix_acc[...] += dot(f_high, s_high, over_rows) + (
                dot(f_high, s_low, over_rows) + dot(f_low, s_high, over_rows)
            )
            for inner in range(0, LIFT_BLOCK, BACK_BLOCK):
                b_high = high[:, inner : inner + BACK_BLOCK, :].reshape(heads * BACK_BLOCK, rows)
                b_low = low[:, inner : inner + BACK_BLOCK, :].reshape(heads * BACK_BLOCK, rows)
                half = HEADS_S * BACK_BLOCK
                twice = dot(back_both[...], b_high)
                total = twice[:half] + (dot(back_both[:half], b_low) + twice[half:])
                first = offset + start + inner
                back[:, first : first + BACK_BLOCK, :] = total.astype(BF16).reshape(HEADS_S, BACK_BLOCK, rows)
        offset += exp_t.shape[1]
    loss = jnp.sum(loss, axis=1, keepdims=True) * LN2

    acc = mix_acc[...].reshape(heads, LIFT_BLOCK, HEADS_S * LIFT_BLOCK)
    sub = lax.broadcasted_iota(jnp.int32, acc.shape, 1)
    within = lax.broadcasted_iota(jnp.int32, acc.shape, 2) & (LIFT_BLOCK - 1)
    diagonal = jnp.sum(jnp.where(sub == within, acc, 0.0), axis=1)
    lane = lax.broadcasted_iota(jnp.int32, diagonal.shape, 1)
    slot = lax.broadcasted_iota(jnp.int32, (heads, LANES), 1)
    packed = jnp.where(slot == HEADS_S, loss, 0.0)
    for index in range(HEADS_S):
        inside = (lane >= index * LIFT_BLOCK) & (lane < (index + 1) * LIFT_BLOCK)
        column = jnp.sum(jnp.where(inside, diagonal, 0.0), axis=1, keepdims=True)
        packed = jnp.where(slot == index, column, packed)
    packed = jnp.concatenate([packed, jnp.zeros((LANES - heads, LANES), F32)], axis=0)
    packed = jnp.transpose(packed)[:RIDE_ROWS]
    sums[...] = packed

    place = lax.axis_index("head")
    per = HEADS_S // shards
    count = row_parts + key_parts - 1
    for shard in range(shards):
        own, *others = pieces[shard * count : (shard + 1) * count]
        first = lax.rem(place + shard, shards) * per
        for index in range(per):
            tile = back[first + index]
            columns = slice(index * HD_S, (index + 1) * HD_S)
            on_keys = dot(tile, row_side[first + index]) * factors[1]
            on_rows = dot(tile, key_side[first + index], ((0,), (0,))) * factors[0]
            own[:part, columns] = on_rows[:part]
            own[part:, columns] = on_keys[:size]
            for spot in range(1, row_parts):
                others[spot - 1][:part, columns] = on_rows[spot * part : (spot + 1) * part]
            for spot in range(1, key_parts):
                others[row_parts + spot - 2][:size, columns] = on_keys[spot * size : (spot + 1) * size]
        for ref in others:
            if ref.shape[0] > part:
                high, low = split(packed * factors[2])
                ref[part:, :LANES] = high.astype(F32)
                ref[part:, LANES:] = low.astype(F32)


def close_kernel(mix_scale, loss_scale, total, grad_mix, head_loss):
    heads = grad_mix.shape[1]
    grad_mix[...] = total[:HEADS_S, :heads] * mix_scale
    head_loss[...] = total[HEADS_S : HEADS_S + 1, :heads] * loss_scale


def body(teacher_query, teacher_key, student_query, student_key, head_mix):
    shard_rows = teacher_query.shape[1]
    heads = head_mix.shape[0]
    length = lax.axis_size("seq")
    shards = lax.axis_size("head")
    copies = lax.axis_size("dp")
    row_parts = max(size for size in range(1, math.isqrt(length) + 1) if length % size == 0)
    key_parts = length // row_parts
    rows, keys = row_parts * shard_rows, key_parts * shard_rows

    def along_rows(position, step):
        return position // row_parts * row_parts + (position % row_parts + step) % row_parts

    def along_keys(position, step):
        return (position + step * row_parts) % length

    def fetch(value, target, step):
        return lax.ppermute(value, "seq", [(target(i, step), i) for i in range(length)])

    def deliver(value, target, step, turn):
        pairs = [
            (h * length + i, (h + turn) % shards * length + target(i, step))
            for h in range(shards)
            for i in range(length)
        ]
        return lax.ppermute(value, ("head", "seq"), pairs)

    own = (teacher_key, teacher_query, student_key, student_query)
    key_t = [fetch(teacher_key, along_keys, d) for d in range(1, key_parts)]
    query_t = [fetch(teacher_query, along_rows, d) for d in range(1, row_parts)]
    share = pltpu.VMEM((1, shard_rows // shards, HEADS_S * HD_S), BF16)
    shares = pl.pallas_call(
        functools.partial(share_kernel, 2),
        out_shape=(share, share),
        in_specs=[pl.BlockSpec(memory_space=pl.ANY)] * 2,
        scratch_shapes=[pltpu.SemaphoreType.DMA((2,))],
        compiler_params=pltpu.CompilerParams(vmem_limit_bytes=VMEM_LIMIT // 4),
        name="share",
    )(*[pltpu.with_memory_space_constraint(array, pltpu.HBM) for array in (student_key, student_query)])

    def fetch_student(value, target, step):
        value = fetch(value, target, step)
        turns = [[(h, (h + turn) % shards) for h in range(shards)] for turn in range(1, shards)]
        return [value] + [lax.ppermute(value, "head", pairs) for pairs in turns]

    key_s = [piece for d in range(1, key_parts) for piece in fetch_student(shares[0], along_keys, d)]
    query_s = [piece for d in range(1, row_parts) for piece in fetch_student(shares[1], along_rows, d)]
    *own, lift_hi, lift_lo, back_both = prepare(head_mix, own)
    key_t, query_t, key_s, query_s = [[mine, *rest] for mine, rest in zip(own, (key_t, query_t, key_s, query_s))]

    exponents = pltpu.VMEM((heads, keys, rows), F32)
    student = pltpu.VMEM((HEADS_S, keys, rows), BF16)
    stats = pltpu.VMEM((heads, rows), F32)
    both = pltpu.VMEM((2, heads, rows), F32)
    sides = [pltpu.VMEM((HEADS_S, size, HD_S), BF16) for size in (keys, rows)]
    lifted, exp_l, stu_hi, stu_lo, top_l, lse_l, key_side, row_side = pl.pallas_call(
        functools.partial(student_kernel, (len(key_s), len(query_s)), shards, heads),
        out_shape=(exponents, exponents, student, student, stats, stats, *sides),
        compiler_params=pltpu.CompilerParams(vmem_limit_bytes=VMEM_LIMIT),
        cost_estimate=pl.CostEstimate(flops=STUDENT_FLOPS, bytes_accessed=1, transcendentals=1),
        name="student",
    )(*key_s, *query_s, lift_hi, lift_lo)

    def teacher(block_t, offset, before):
        size = len(block_t) * shard_rows
        return pl.pallas_call(
            functools.partial(teacher_kernel, row_parts, len(block_t), heads, offset, bool(before)),
            out_shape=(pltpu.VMEM((heads, size, rows), F32), stats, stats, both) + (both,) * (row_parts - 1),
            compiler_params=pltpu.CompilerParams(vmem_limit_bytes=VMEM_LIMIT),
            name="teacher",
        )(*block_t, *query_t, lifted, lse_l, *before)

    done, before = [], []
    for first, block in ((0, key_t[:1]), (1, key_t[1:])):
        if block:
            results = teacher(block, first * shard_rows, before)
            done.append(results[:3])
            before, turned = results[3:4], results[4:]
    lse_parts = [*before] + [fetch(turned[step - 1], along_rows, row_parts - step) for step in range(1, row_parts)]

    weight = shard_rows * length / HEADS_T
    width = HEADS_S * HD_S // shards
    ride = RIDE_ROWS if width == 2 * LANES else 0
    factor = weight * HD_S ** (-0.5)
    room_query = room(2.0 * heads * MIX_TOP * VALUE_TOP * factor)
    room_key = room(rows * heads * MIX_TOP * VALUE_TOP * factor)
    room_sums = room(2.0 * rows * HD_S * VALUE_TOP**2)
    count = row_parts + key_parts - 1
    shapes = []
    for shard in range(shards):
        extra = ride if shard == 0 else 0
        shapes += [(2 * shard_rows, width)] + [(shard_rows + extra, width)] * (count - 1)
    sums, *pieces = pl.pallas_call(
        functools.partial(
            back_kernel,
            row_parts,
            key_parts,
            shards,
            len(done),
            heads,
            (factor * room_query, factor * room_key, room_sums),
        ),
        out_shape=[jax.ShapeDtypeStruct(shape, F32) for shape in [(RIDE_ROWS, LANES)] + shapes],
        scratch_shapes=[
            pltpu.VMEM((heads, rows), F32),
            pltpu.VMEM((heads, rows), F32),
            pltpu.VMEM((HEADS_S, keys, rows), BF16),
            pltpu.VMEM((heads * LIFT_BLOCK, HEADS_S * LIFT_BLOCK), F32),
        ],
        compiler_params=pltpu.CompilerParams(vmem_limit_bytes=VMEM_LIMIT),
        name="back",
    )(
        row_side, key_side, *lse_parts, back_both, exp_l, stu_hi, stu_lo, top_l,
        *[ref for block in done for ref in block],
    )

    moves = [(along_rows, step) for step in range(row_parts)] + [(along_keys, step) for step in range(1, key_parts)]
    arrived = [
        deliver(part.astype(F16), *moves[i % count], i // count) if i else part for i, part in enumerate(pieces)
    ]
    small = functools.partial(pl.pallas_call, compiler_params=pltpu.CompilerParams(vmem_limit_bytes=VMEM_LIMIT // 4))

    def diagonal(across, along):
        return lambda position, _: along_keys(along_rows(position, across), along)

    if ride:
        rides = [part[shard_rows:].astype(F32) for part in arrived[1:count]]
        others = [(part[:, :LANES] + part[:, LANES:]) * (1.0 / room_sums) for part in rides]
    else:
        others = [fetch(sums, target, step) for target, step in moves[1:]]
    for across in range(1, row_parts):
        others += [fetch(sums, diagonal(across, along), 0) for along in range(1, key_parts)]
    total = sum(others, sums)
    for_query = [part[:shard_rows].astype(F32) for i, part in enumerate(arrived) if i % count < row_parts]
    for_key = [
        part[-shard_rows:].astype(F32) if i % count == 0 else part[:shard_rows].astype(F32)
        for i, part in enumerate(arrived)
        if i % count == 0 or i % count >= row_parts
    ]
    grad_query = (sum(for_query[1:], for_query[0]) * (1.0 / room_query))[None]
    grad_key = (sum(for_key[1:], for_key[0]) * (1.0 / room_key))[None]
    last = total
    if copies > 1 and copies & (copies - 1) == 0:
        for bit in range(copies.bit_length() - 1):
            total = total if bit == 0 else total + last
            last = lax.ppermute(total, "dp", [(i, i ^ (1 << bit)) for i in range(copies)])
    else:
        last = sum(
            [lax.ppermute(total, "dp", [(i, (i + step) % copies) for i in range(copies)]) for step in range(1, copies)],
            jnp.zeros_like(total),
        )
    last, grad_query, grad_key = lax.optimization_barrier((last, grad_query, grad_key))
    total = total + last
    samples = copies * teacher_query.shape[0] * shard_rows * length
    grad_mix, head_loss = small(
        functools.partial(close_kernel, HD_S ** (-0.5) * weight / samples, 1.0 / samples),
        out_shape=(jax.ShapeDtypeStruct((HEADS_S, heads), F32), jax.ShapeDtypeStruct((1, heads), F32)),
        name="close",
    )(total)
    return (grad_query, grad_key, grad_mix.T, head_loss[0])


def solution(mesh):
    return jax.shard_map(
        body,
        mesh=mesh,
        in_specs=(
            P("dp", "seq", "head"),
            P("dp", "seq", "head"),
            P("dp", "seq", None),
            P("dp", "seq", None),
            P("head", None),
        ),
        out_specs=(P("dp", "seq", "head"), P("dp", "seq", "head"), P("head", None), P("head")),
        check_vma=False,
    )
```

```python
import functools
import math

import jax
import jax.numpy as jnp
from jax import lax
from jax.experimental import pallas as pl
from jax.experimental.pallas import tpu as pltpu
from jax.sharding import PartitionSpec as P

HEADS_T = 24
HD_T = 128
HEADS_S = 8
HD_S = 64
LOG2E = math.log2(math.e)
LN2 = math.log(2.0)
LIFT_BLOCK = 32
BACK_BLOCK = 16
RIDE_ROWS = 16
LANES = 128
STUDENT_FLOPS = 30*10**8
VMEM_LIMIT = 8 * 1024 * 1024

F32 = jnp.float32
BF16 = jnp.bfloat16
F16 = jnp.float16
MIX_TOP = 0.25
VALUE_TOP = 6.0


def dot(lhs, rhs, dims=((1,), (0,))):
    return lax.dot_general(lhs, rhs, (dims, ((), ())), preferred_element_type=F32)


def room(bound):
    return 2.0 ** math.floor(math.log2(float(jnp.finfo(F16).max) / (1.01 * bound)))


def split(value):
    high = value.astype(BF16)
    low = (value - high.astype(F32)).astype(BF16)
    return high, low


def prepare_kernel(count, mix_ref, mix_tr_ref, *refs):
    sources, targets = refs[:count], refs[count : 2 * count]
    lift_hi, lift_lo, back_both, semaphores = refs[2 * count :]
    moves = [pltpu.make_async_copy(sources[i], targets[i], semaphores.at[i]) for i in range(count)]
    for move in moves:
        move.start()

    def kron(values, size):
        rows, columns = values.shape
        lane = lax.broadcasted_iota(jnp.int32, (rows, columns * size), 1)
        spread = jnp.zeros((rows, columns * size), F32)
        for index in range(columns):
            inside = (lane >= index * size) & (lane < (index + 1) * size)
            spread = jnp.where(inside, values[:, index : index + 1], spread)
        full = (rows, size, columns * size)
        sub = lax.broadcasted_iota(jnp.int32, full, 1)
        within = lax.broadcasted_iota(jnp.int32, full, 2) & (size - 1)
        picked = jnp.where(sub == within, spread[:, None, :], 0.0)
        return picked.reshape(rows * size, columns * size)

    scaled = mix_ref[...] * (HD_S ** (-0.5) * LOG2E)
    lift_hi[...], lift_lo[...] = split(kron(scaled, LIFT_BLOCK))
    high, low = split(kron(mix_tr_ref[...], BACK_BLOCK))
    back_both[: high.shape[0]] = high
    back_both[high.shape[0] :] = low
    for move in moves:
        move.wait()


def prepare(head_mix, arrays):
    heads = head_mix.shape[0]
    lift = pltpu.VMEM((heads * LIFT_BLOCK, HEADS_S * LIFT_BLOCK), BF16)
    back = pltpu.VMEM((2 * HEADS_S * BACK_BLOCK, heads * BACK_BLOCK), BF16)
    count = len(arrays)
    whole = pl.BlockSpec(memory_space=pltpu.VMEM)
    return pl.pallas_call(
        functools.partial(prepare_kernel, count),
        out_shape=[pltpu.VMEM(array.shape, array.dtype) for array in arrays] + [lift, lift, back],
        in_specs=[whole, whole] + [pl.BlockSpec(memory_space=pl.ANY)] * count,
        scratch_shapes=[pltpu.SemaphoreType.DMA((count,))],
        compiler_params=pltpu.CompilerParams(vmem_limit_bytes=VMEM_LIMIT // 2),
        name="prepare",
    )(head_mix, head_mix.T, *[pltpu.with_memory_space_constraint(array, pltpu.HBM) for array in arrays])


def stacked(refs, columns):
    parts = [ref[0, :, columns] for ref in refs]
    return parts[0] if len(parts) == 1 else jnp.concatenate(parts, axis=0)


def share_kernel(count, *refs):
    sources, targets, semaphores = refs[:count], refs[count : 2 * count], refs[-1]
    size = targets[0].shape[1]
    start = pl.multiple_of(lax.axis_index("head") * size, size)
    moves = [
        pltpu.make_async_copy(source.at[:, pl.ds(start, size), :], target, semaphores.at[i])
        for i, (source, target) in enumerate(zip(sources, targets))
    ]
    for move in moves:
        move.start()
    for move in moves:
        move.wait()


def by_head(shards, pieces, side):
    place = lax.axis_index("head")
    own, *others = pieces
    part = own.shape[1]
    for index in range(HEADS_S):
        columns = slice(index * HD_S, (index + 1) * HD_S)
        side[index, :part] = own[0, :, columns]
        for i, piece in enumerate(others):
            size = piece.shape[1]
            first = (i // shards + 1) * part + lax.rem(place + shards - i % shards, shards) * size
            side[index, pl.ds(pl.multiple_of(first, size), size), :] = piece[0, :, columns]


def student_kernel(counts, shards, heads, *refs):
    key_s, query_s, refs = refs[: counts[0]], refs[counts[0] : sum(counts)], refs[sum(counts) :]
    lift_hi, lift_lo, lifted, exp_l, stu_hi, stu_lo, top, lse, key_side, query_side = refs
    keys, rows = stu_hi.shape[1:]
    by_head(shards, key_s, key_side)
    by_head(shards, query_s, query_side)
    for index in range(HEADS_S):
        stu_hi[index], stu_lo[index] = split(dot(key_side[index], query_side[index], ((1,), (1,))))
    for start in range(0, keys, LIFT_BLOCK):
        block = slice(start, start + LIFT_BLOCK)
        high = stu_hi[:, block, :].reshape(HEADS_S * LIFT_BLOCK, rows)
        low = stu_lo[:, block, :].reshape(HEADS_S * LIFT_BLOCK, rows)
        total = dot(lift_hi[...], high) + (dot(lift_hi[...], low) + dot(lift_lo[...], high))
        lifted[:, block, :] = total.reshape(heads, LIFT_BLOCK, rows)
    for head in range(heads):
        mixed = lifted[head]
        best = jnp.max(mixed, axis=0, keepdims=True)
        prob = jnp.exp2(mixed - best)
        exp_l[head] = prob
        top[head : head + 1, :] = best
        lse[head : head + 1, :] = best + jnp.log2(jnp.sum(prob, axis=0, keepdims=True))


def teacher_kernel(row_parts, key_parts, heads, offset, carried, *refs):
    key_t, query_t, refs = refs[:key_parts], refs[key_parts : key_parts + row_parts], refs[key_parts + row_parts :]
    lifted, lse_l, *refs = refs
    before = refs.pop(0) if carried else None
    exp_t, top, kl, lse, *turned = refs
    keys, rows = exp_t.shape[1:]
    for head in range(heads):
        columns = slice(head * HD_T, (head + 1) * HD_T)
        teacher = dot(stacked(key_t, columns), stacked(query_t, columns), ((1,), (1,)))
        teacher = teacher * (HD_T ** (-0.5) * LOG2E)
        best = jnp.max(teacher, axis=0, keepdims=True)
        prob = jnp.exp2(teacher - best)
        exp_t[head] = prob
        mixed = lifted[head, offset : offset + keys, :]
        kl[head : head + 1, :] = jnp.sum(prob * (teacher - mixed), axis=0, keepdims=True)
        top[head : head + 1, :] = best
        total = jnp.sum(prob, axis=0, keepdims=True)
        if carried:
            earlier = before[0, head : head + 1, :]
            higher = jnp.maximum(best, earlier)
            total = total * jnp.exp2(best - higher) + jnp.exp2(earlier - higher)
            best = higher
        lse[0, head : head + 1, :] = best + jnp.log2(total)
    lse[1] = lse_l[...]
    part = rows // row_parts
    for step, ref in enumerate(turned, 1):
        for spot in range(row_parts):
            source = (spot + step) % row_parts * part
            ref[:, :, spot * part : (spot + 1) * part] = lse[:, :, source : source + part]


def back_kernel(row_parts, key_parts, shards, blocks, heads, factors, *refs):
    refs = list(refs)
    row_side, key_side = refs.pop(0), refs.pop(0)
    lse = [refs.pop(0) for _ in range(row_parts)]
    back_both, exp_l, stu_hi, stu_lo, top_l = refs[:5]
    maps = [refs[5 + 3 * i : 8 + 3 * i] for i in range(blocks)]
    *outs, scale_t, scale_l, back, mix_acc = refs[5 + 3 * blocks :]
    keys, rows = back.shape[1:]
    part, size = rows // row_parts, keys // key_parts
    sums, pieces = outs[0], outs[1:]

    lse_all = []
    for which in range(2):
        parts = [ref[which] for ref in lse]
        best = functools.reduce(jnp.maximum, parts)
        total = sum(jnp.exp2(value - best) for value in parts)
        lse_all.append(best + jnp.log2(total))
    own = lax.broadcasted_iota(jnp.int32, (heads, rows), 1) < part
    loss = jnp.where(own, lse_all[1] - lse_all[0], 0.0)
    mix_acc[...] = jnp.zeros_like(mix_acc)
    offset = 0
    scale_l[...] = jnp.exp2(top_l[...] - lse_all[1])
    for exp_t, top_t, kl in maps:
        scale_t[...] = jnp.exp2(top_t[...] - lse_all[0])
        loss = loss + scale_t[...] * kl[...]
        for start in range(0, exp_t.shape[1], LIFT_BLOCK):
            block = slice(start, start + LIFT_BLOCK)
            place = slice(offset + start, offset + start + LIFT_BLOCK)
            excess = (
                exp_l[:, place, :] * scale_l[...][:, None, :] - exp_t[:, block, :] * scale_t[...][:, None, :]
            )
            high, low = split(excess)
            s_high = stu_hi[:, place, :].reshape(HEADS_S * LIFT_BLOCK, rows)
            s_low = stu_lo[:, place, :].reshape(HEADS_S * LIFT_BLOCK, rows)
            f_high = high.reshape(heads * LIFT_BLOCK, rows)
            f_low = low.reshape(heads * LIFT_BLOCK, rows)
            over_rows = ((1,), (1,))
            mix_acc[...] += dot(f_high, s_high, over_rows) + (
                dot(f_high, s_low, over_rows) + dot(f_low, s_high, over_rows)
            )
            for inner in range(0, LIFT_BLOCK, BACK_BLOCK):
                b_high = high[:, inner : inner + BACK_BLOCK, :].reshape(heads * BACK_BLOCK, rows)
                b_low = low[:, inner : inner + BACK_BLOCK, :].reshape(heads * BACK_BLOCK, rows)
                half = HEADS_S * BACK_BLOCK
                twice = dot(back_both[...], b_high)
                total = twice[:half] + (dot(back_both[:half], b_low) + twice[half:])
                first = offset + start + inner
                back[:, first : first + BACK_BLOCK, :] = total.astype(BF16).reshape(HEADS_S, BACK_BLOCK, rows)
        offset += exp_t.shape[1]
    loss = jnp.sum(loss, axis=1, keepdims=True) * LN2

    acc = mix_acc[...].reshape(heads, LIFT_BLOCK, HEADS_S * LIFT_BLOCK)
    sub = lax.broadcasted_iota(jnp.int32, acc.shape, 1)
    within = lax.broadcasted_iota(jnp.int32, acc.shape, 2) & (LIFT_BLOCK - 1)
    diagonal = jnp.sum(jnp.where(sub == within, acc, 0.0), axis=1)
    lane = lax.broadcasted_iota(jnp.int32, diagonal.shape, 1)
    slot = lax.broadcasted_iota(jnp.int32, (heads, LANES), 1)
    packed = jnp.where(slot == HEADS_S, loss, 0.0)
    for index in range(HEADS_S):
        inside = (lane >= index * LIFT_BLOCK) & (lane < (index + 1) * LIFT_BLOCK)
        column = jnp.sum(jnp.where(inside, diagonal, 0.0), axis=1, keepdims=True)
        packed = jnp.where(slot == index, column, packed)
    packed = jnp.concatenate([packed, jnp.zeros((LANES - heads, LANES), F32)], axis=0)
    packed = jnp.transpose(packed)[:RIDE_ROWS]
    sums[...] = packed

    place = lax.axis_index("head")
    per = HEADS_S // shards
    count = row_parts + key_parts - 1
    for shard in range(shards):
        own, *others = pieces[shard * count : (shard + 1) * count]
        first = lax.rem(place + shard, shards) * per
        for index in range(per):
            tile = back[first + index]
            columns = slice(index * HD_S, (index + 1) * HD_S)
            on_keys = dot(tile, row_side[first + index]) * factors[1]
            on_rows = dot(tile, key_side[first + index], ((0,), (0,))) * factors[0]
            own[:part, columns] = on_rows[:part]
            own[part:, columns] = on_keys[:size]
            for spot in range(1, row_parts):
                others[spot - 1][:part, columns] = on_rows[spot * part : (spot + 1) * part]
            for spot in range(1, key_parts):
                others[row_parts + spot - 2][:size, columns] = on_keys[spot * size : (spot + 1) * size]
        for ref in others:
            if ref.shape[0] > part:
                high, low = split(packed * factors[2])
                ref[part:, :LANES] = high.astype(F32)
                ref[part:, LANES:] = low.astype(F32)


def close_kernel(mix_scale, loss_scale, total, grad_mix, head_loss):
    heads = grad_mix.shape[1]
    grad_mix[...] = total[:HEADS_S, :heads] * mix_scale
    head_loss[...] = total[HEADS_S : HEADS_S + 1, :heads] * loss_scale


def body(teacher_query, teacher_key, student_query, student_key, head_mix):
    shard_rows = teacher_query.shape[1]
    heads = head_mix.shape[0]
    length = lax.axis_size("seq")
    shards = lax.axis_size("head")
    copies = lax.axis_size("dp")
    row_parts = max(size for size in range(1, math.isqrt(length) + 1) if length % size == 0)
    key_parts = length // row_parts
    rows, keys = row_parts * shard_rows, key_parts * shard_rows

    def along_rows(position, step):
        return position // row_parts * row_parts + (position % row_parts + step) % row_parts

    def along_keys(position, step):
        return (position + step * row_parts) % length

    def fetch(value, target, step):
        return lax.ppermute(value, "seq", [(target(i, step), i) for i in range(length)])

    def deliver(value, target, step, turn):
        pairs = [
            (h * length + i, (h + turn) % shards * length + target(i, step))
            for h in range(shards)
            for i in range(length)
        ]
        return lax.ppermute(value, ("head", "seq"), pairs)

    own = (teacher_key, teacher_query, student_key, student_query)
    key_t = [fetch(teacher_key, along_keys, d) for d in range(1, key_parts)]
    query_t = [fetch(teacher_query, along_rows, d) for d in range(1, row_parts)]
    share = pltpu.VMEM((1, shard_rows // shards, HEADS_S * HD_S), BF16)
    shares = pl.pallas_call(
        functools.partial(share_kernel, 2),
        out_shape=(share, share),
        in_specs=[pl.BlockSpec(memory_space=pl.ANY)] * 2,
        scratch_shapes=[pltpu.SemaphoreType.DMA((2,))],
        compiler_params=pltpu.CompilerParams(vmem_limit_bytes=VMEM_LIMIT // 4),
        name="share",
    )(*[pltpu.with_memory_space_constraint(array, pltpu.HBM) for array in (student_key, student_query)])

    def fetch_student(value, target, step):
        value = fetch(value, target, step)
        turns = [[(h, (h + turn) % shards) for h in range(shards)] for turn in range(1, shards)]
        return [value] + [lax.ppermute(value, "head", pairs) for pairs in turns]

    key_s = [piece for d in range(1, key_parts) for piece in fetch_student(shares[0], along_keys, d)]
    query_s = [piece for d in range(1, row_parts) for piece in fetch_student(shares[1], along_rows, d)]
    *own, lift_hi, lift_lo, back_both = prepare(head_mix, own)
    key_t, query_t, key_s, query_s = [[mine, *rest] for mine, rest in zip(own, (key_t, query_t, key_s, query_s))]

    exponents = pltpu.VMEM((heads, keys, rows), F32)
    student = pltpu.VMEM((HEADS_S, keys, rows), BF16)
    stats = pltpu.VMEM((heads, rows), F32)
    both = pltpu.VMEM((2, heads, rows), F32)
    sides = [pltpu.VMEM((HEADS_S, size, HD_S), BF16) for size in (keys, rows)]
    lifted, exp_l, stu_hi, stu_lo, top_l, lse_l, key_side, row_side = pl.pallas_call(
        functools.partial(student_kernel, (len(key_s), len(query_s)), shards, heads),
        out_shape=(exponents, exponents, student, student, stats, stats, *sides),
        compiler_params=pltpu.CompilerParams(vmem_limit_bytes=VMEM_LIMIT),
        cost_estimate=pl.CostEstimate(flops=STUDENT_FLOPS, bytes_accessed=1, transcendentals=1),
        name="student",
    )(*key_s, *query_s, lift_hi, lift_lo)

    def teacher(block_t, offset, before, extra):
        size = len(block_t) * shard_rows
        return pl.pallas_call(
            functools.partial(teacher_kernel, row_parts, len(block_t), heads, offset, bool(before)),
            out_shape=(pltpu.VMEM((heads, size, rows), F32), stats, stats, both) + (both,) * extra,
            compiler_params=pltpu.CompilerParams(vmem_limit_bytes=VMEM_LIMIT),
            name="teacher",
        )(*block_t, *query_t, lifted, lse_l, *before)

    done, before = [], []
    for first, block in ((0, key_t[:1]), (1, key_t[1:])):
        if block:
            extra = row_parts - 1 if first or key_parts == 1 else 0
            results = teacher(block, first * shard_rows, before, extra)
            done.append(results[:3])
            before, turned = results[3:4], results[4:]
    lse_parts = [*before] + [fetch(turned[step - 1], along_rows, row_parts - step) for step in range(1, row_parts)]

    weight = shard_rows * length / HEADS_T
    width = HEADS_S * HD_S // shards
    ride = RIDE_ROWS if width == 2 * LANES else 0
    factor = weight * HD_S ** (-0.5)
    room_query = room(2.0 * heads * MIX_TOP * VALUE_TOP * factor)
    room_key = room(rows * heads * MIX_TOP * VALUE_TOP * factor)
    room_sums = room(2.0 * rows * HD_S * VALUE_TOP**2)
    count = row_parts + key_parts - 1
    shapes = []
    for shard in range(shards):
        extra = ride if shard == 0 else 0
        shapes += [(2 * shard_rows, width)] + [(shard_rows + extra, width)] * (count - 1)
    sums, *pieces = pl.pallas_call(
        functools.partial(
            back_kernel,
            row_parts,
            key_parts,
            shards,
            len(done),
            heads,
            (factor * room_query, factor * room_key, room_sums),
        ),
        out_shape=[jax.ShapeDtypeStruct(shape, F32) for shape in [(RIDE_ROWS, LANES)] + shapes],
        scratch_shapes=[
            pltpu.VMEM((heads, rows), F32),
            pltpu.VMEM((heads, rows), F32),
            pltpu.VMEM((HEADS_S, keys, rows), BF16),
            pltpu.VMEM((heads * LIFT_BLOCK, HEADS_S * LIFT_BLOCK), F32),
        ],
        compiler_params=pltpu.CompilerParams(vmem_limit_bytes=VMEM_LIMIT),
        name="back",
    )(
        row_side, key_side, *lse_parts, back_both, exp_l, stu_hi, stu_lo, top_l,
        *[ref for block in done for ref in block],
    )

    moves = [(along_rows, step) for step in range(row_parts)] + [(along_keys, step) for step in range(1, key_parts)]
    arrived = [
        deliver(part.astype(F16), *moves[i % count], i // count) if i else part for i, part in enumerate(pieces)
    ]
    small = functools.partial(pl.pallas_call, compiler_params=pltpu.CompilerParams(vmem_limit_bytes=VMEM_LIMIT // 4))

    def diagonal(across, along):
        return lambda position, _: along_keys(along_rows(position, across), along)

    if ride:
        rides = [part[shard_rows:].astype(F32) for part in arrived[1:count]]
        others = [(part[:, :LANES] + part[:, LANES:]) * (1.0 / room_sums) for part in rides]
    else:
        others = [fetch(sums, target, step) for target, step in moves[1:]]
    for across in range(1, row_parts):
        others += [fetch(sums, diagonal(across, along), 0) for along in range(1, key_parts)]
    total = sum(others, sums)
    for_query = [part[:shard_rows].astype(F32) for i, part in enumerate(arrived) if i % count < row_parts]
    for_key = [
        part[-shard_rows:].astype(F32) if i % count == 0 else part[:shard_rows].astype(F32)
        for i, part in enumerate(arrived)
        if i % count == 0 or i % count >= row_parts
    ]
    grad_query = (sum(for_query[1:], for_query[0]) * (1.0 / room_query))[None]
    grad_key = (sum(for_key[1:], for_key[0]) * (1.0 / room_key))[None]
    last = total
    if copies > 1 and copies & (copies - 1) == 0:
        for bit in range(copies.bit_length() - 1):
            total = total if bit == 0 else total + last
            last = lax.ppermute(total, "dp", [(i, i ^ (1 << bit)) for i in range(copies)])
    else:
        last = sum(
            [lax.ppermute(total, "dp", [(i, (i + step) % copies) for i in range(copies)]) for step in range(1, copies)],
            jnp.zeros_like(total),
        )
    last, grad_query, grad_key = lax.optimization_barrier((last, grad_query, grad_key))
    total = total + last
    samples = copies * teacher_query.shape[0] * shard_rows * length
    grad_mix, head_loss = small(
        functools.partial(close_kernel, HD_S ** (-0.5) * weight / samples, 1.0 / samples),
        out_shape=(jax.ShapeDtypeStruct((HEADS_S, heads), F32), jax.ShapeDtypeStruct((1, heads), F32)),
        name="close",
    )(total)
    return (grad_query, grad_key, grad_mix.T, head_loss[0])


def solution(mesh):
    return jax.shard_map(
        body,
        mesh=mesh,
        in_specs=(
            P("dp", "seq", "head"),
            P("dp", "seq", "head"),
            P("dp", "seq", None),
            P("dp", "seq", None),
            P("head", None),
        ),
        out_specs=(P("dp", "seq", "head"), P("dp", "seq", "head"), P("head", None), P("head")),
        check_vma=False,
    )
```

```python
import functools
import math

import jax
import jax.numpy as jnp
from jax import lax
from jax.experimental import pallas as pl
from jax.experimental.pallas import tpu as pltpu
from jax.sharding import PartitionSpec as P

HEADS_T = 24
HD_T = 128
HEADS_S = 8
HD_S = 64
LOG2E = math.log2(math.e)
LN2 = math.log(2.0)
LIFT_BLOCK = 32
BACK_BLOCK = 16
RIDE_ROWS = 16
LANES = 128
STUDENT_FLOPS = 30*10**8
VMEM_LIMIT = 8 * 1024 * 1024

F32 = jnp.float32
BF16 = jnp.bfloat16
F16 = jnp.float16
MIX_TOP = 0.25
VALUE_TOP = 6.0


def dot(lhs, rhs, dims=((1,), (0,))):
    return lax.dot_general(lhs, rhs, (dims, ((), ())), preferred_element_type=F32)


def room(bound):
    return 2.0 ** math.floor(math.log2(float(jnp.finfo(F16).max) / (1.01 * bound)))


def split(value):
    high = value.astype(BF16)
    low = (value - high.astype(F32)).astype(BF16)
    return high, low


def prepare_kernel(count, mix_ref, mix_tr_ref, *refs):
    sources, targets = refs[:count], refs[count : 2 * count]
    lift_hi, lift_lo, back_both, semaphores = refs[2 * count :]
    moves = [pltpu.make_async_copy(sources[i], targets[i], semaphores.at[i]) for i in range(count)]
    for move in moves:
        move.start()

    def kron(values, size):
        rows, columns = values.shape
        lane = lax.broadcasted_iota(jnp.int32, (rows, columns * size), 1)
        spread = jnp.zeros((rows, columns * size), F32)
        for index in range(columns):
            inside = (lane >= index * size) & (lane < (index + 1) * size)
            spread = jnp.where(inside, values[:, index : index + 1], spread)
        full = (rows, size, columns * size)
        sub = lax.broadcasted_iota(jnp.int32, full, 1)
        within = lax.broadcasted_iota(jnp.int32, full, 2) & (size - 1)
        picked = jnp.where(sub == within, spread[:, None, :], 0.0)
        return picked.reshape(rows * size, columns * size)

    scaled = mix_ref[...] * (HD_S ** (-0.5) * LOG2E)
    lift_hi[...], lift_lo[...] = split(kron(scaled, LIFT_BLOCK))
    high, low = split(kron(mix_tr_ref[...], BACK_BLOCK))
    back_both[: high.shape[0]] = high
    back_both[high.shape[0] :] = low
    for move in moves:
        move.wait()


def prepare(head_mix, arrays):
    heads = head_mix.shape[0]
    lift = pltpu.VMEM((heads * LIFT_BLOCK, HEADS_S * LIFT_BLOCK), BF16)
    back = pltpu.VMEM((2 * HEADS_S * BACK_BLOCK, heads * BACK_BLOCK), BF16)
    count = len(arrays)
    whole = pl.BlockSpec(memory_space=pltpu.VMEM)
    return pl.pallas_call(
        functools.partial(prepare_kernel, count),
        out_shape=[pltpu.VMEM(array.shape, array.dtype) for array in arrays] + [lift, lift, back],
        in_specs=[whole, whole] + [pl.BlockSpec(memory_space=pl.ANY)] * count,
        scratch_shapes=[pltpu.SemaphoreType.DMA((count,))],
        compiler_params=pltpu.CompilerParams(vmem_limit_bytes=VMEM_LIMIT // 2),
        name="prepare",
    )(head_mix, head_mix.T, *[pltpu.with_memory_space_constraint(array, pltpu.HBM) for array in arrays])


def stacked(refs, columns):
    parts = [ref[0, :, columns] for ref in refs]
    return parts[0] if len(parts) == 1 else jnp.concatenate(parts, axis=0)


def share_kernel(count, *refs):
    sources, targets, semaphores = refs[:count], refs[count : 2 * count], refs[-1]
    size = targets[0].shape[1]
    start = pl.multiple_of(lax.axis_index("head") * size, size)
    moves = [
        pltpu.make_async_copy(source.at[:, pl.ds(start, size), :], target, semaphores.at[i])
        for i, (source, target) in enumerate(zip(sources, targets))
    ]
    for move in moves:
        move.start()
    for move in moves:
        move.wait()


def by_head(shards, pieces, side):
    place = lax.axis_index("head")
    own, *others = pieces
    part = own.shape[1]
    for index in range(HEADS_S):
        columns = slice(index * HD_S, (index + 1) * HD_S)
        side[index, :part] = own[0, :, columns]
        for i, piece in enumerate(others):
            size = piece.shape[1]
            first = (i // shards + 1) * part + lax.rem(place + shards - i % shards, shards) * size
            side[index, pl.ds(pl.multiple_of(first, size), size), :] = piece[0, :, columns]


def student_kernel(counts, shards, heads, *refs):
    key_s, query_s, refs = refs[: counts[0]], refs[counts[0] : sum(counts)], refs[sum(counts) :]
    lift_hi, lift_lo, lifted, exp_l, stu_hi, stu_lo, top, lse, key_side, query_side = refs
    keys, rows = stu_hi.shape[1:]
    by_head(shards, key_s, key_side)
    by_head(shards, query_s, query_side)
    for index in range(HEADS_S):
        stu_hi[index], stu_lo[index] = split(dot(key_side[index], query_side[index], ((1,), (1,))))
    for start in range(0, keys, LIFT_BLOCK):
        block = slice(start, start + LIFT_BLOCK)
        high = stu_hi[:, block, :].reshape(HEADS_S * LIFT_BLOCK, rows)
        low = stu_lo[:, block, :].reshape(HEADS_S * LIFT_BLOCK, rows)
        total = dot(lift_hi[...], high) + (dot(lift_hi[...], low) + dot(lift_lo[...], high))
        lifted[:, block, :] = total.reshape(heads, LIFT_BLOCK, rows)
    for head in range(heads):
        mixed = lifted[head]
        best = jnp.max(mixed, axis=0, keepdims=True)
        prob = jnp.exp2(mixed - best)
        exp_l[head] = prob
        top[head : head + 1, :] = best
        lse[head : head + 1, :] = best + jnp.log2(jnp.sum(prob, axis=0, keepdims=True))


def teacher_kernel(row_parts, key_parts, heads, offset, carried, *refs):
    key_t, query_t, refs = refs[:key_parts], refs[key_parts : key_parts + row_parts], refs[key_parts + row_parts :]
    lifted, lse_l, *refs = refs
    before = refs.pop(0) if carried else None
    exp_t, top, kl, lse, *turned = refs
    keys, rows = exp_t.shape[1:]
    for head in range(heads):
        columns = slice(head * HD_T, (head + 1) * HD_T)
        teacher = dot(stacked(key_t, columns), stacked(query_t, columns), ((1,), (1,)))
        teacher = teacher * (HD_T ** (-0.5) * LOG2E)
        best = jnp.max(teacher, axis=0, keepdims=True)
        prob = jnp.exp2(teacher - best)
        exp_t[head] = prob
        mixed = lifted[head, offset : offset + keys, :]
        kl[head : head + 1, :] = jnp.sum(prob * (teacher - mixed), axis=0, keepdims=True)
        top[head : head + 1, :] = best
        total = jnp.sum(prob, axis=0, keepdims=True)
        if carried:
            earlier = before[0, head : head + 1, :]
            higher = jnp.maximum(best, earlier)
            total = total * jnp.exp2(best - higher) + jnp.exp2(earlier - higher)
            best = higher
        lse[0, head : head + 1, :] = best + jnp.log2(total)
    lse[1] = lse_l[...]
    part = rows // row_parts
    for step, ref in enumerate(turned, 1):
        for spot in range(row_parts):
            source = (spot + step) % row_parts * part
            ref[:, :, spot * part : (spot + 1) * part] = lse[:, :, source : source + part]


def back_kernel(row_parts, key_parts, shards, blocks, heads, factors, *refs):
    refs = list(refs)
    row_side, key_side = refs.pop(0), refs.pop(0)
    lse = [refs.pop(0) for _ in range(row_parts)]
    back_both, exp_l, stu_hi, stu_lo, top_l = refs[:5]
    maps = [refs[5 + 3 * i : 8 + 3 * i] for i in range(blocks)]
    *outs, scale_t, scale_l, back, mix_acc = refs[5 + 3 * blocks :]
    keys, rows = back.shape[1:]
    part, size = rows // row_parts, keys // key_parts
    sums, pieces = outs[0], outs[1:]

    lse_all = []
    for which in range(2):
        parts = [ref[which] for ref in lse]
        best = functools.reduce(jnp.maximum, parts)
        total = sum(jnp.exp2(value - best) for value in parts)
        lse_all.append(best + jnp.log2(total))
    own = lax.broadcasted_iota(jnp.int32, (heads, rows), 1) < part
    loss = jnp.where(own, lse_all[1] - lse_all[0], 0.0)
    mix_acc[...] = jnp.zeros_like(mix_acc)
    offset = 0
    scale_l[...] = jnp.exp2(top_l[...] - lse_all[1])
    for exp_t, top_t, kl in maps:
        scale_t[...] = jnp.exp2(top_t[...] - lse_all[0])
        loss = loss + scale_t[...] * kl[...]
        for start in range(0, exp_t.shape[1], LIFT_BLOCK):
            block = slice(start, start + LIFT_BLOCK)
            place = slice(offset + start, offset + start + LIFT_BLOCK)
            excess = (
                exp_l[:, place, :] * scale_l[...][:, None, :] - exp_t[:, block, :] * scale_t[...][:, None, :]
            )
            high, low = split(excess)
            s_high = stu_hi[:, place, :].reshape(HEADS_S * LIFT_BLOCK, rows)
            s_low = stu_lo[:, place, :].reshape(HEADS_S * LIFT_BLOCK, rows)
            f_high = high.reshape(heads * LIFT_BLOCK, rows)
            f_low = low.reshape(heads * LIFT_BLOCK, rows)
            over_rows = ((1,), (1,))
            mix_acc[...] += dot(f_high, s_high, over_rows) + (
                dot(f_high, s_low, over_rows) + dot(f_low, s_high, over_rows)
            )
            for inner in range(0, LIFT_BLOCK, BACK_BLOCK):
                b_high = high[:, inner : inner + BACK_BLOCK, :].reshape(heads * BACK_BLOCK, rows)
                b_low = low[:, inner : inner + BACK_BLOCK, :].reshape(heads * BACK_BLOCK, rows)
                half = HEADS_S * BACK_BLOCK
                twice = dot(back_both[...], b_high)
                total = twice[:half] + (dot(back_both[:half], b_low) + twice[half:])
                first = offset + start + inner
                back[:, first : first + BACK_BLOCK, :] = total.astype(BF16).reshape(HEADS_S, BACK_BLOCK, rows)
        offset += exp_t.shape[1]
    loss = jnp.sum(loss, axis=1, keepdims=True) * LN2

    acc = mix_acc[...].reshape(heads, LIFT_BLOCK, HEADS_S * LIFT_BLOCK)
    sub = lax.broadcasted_iota(jnp.int32, acc.shape, 1)
    within = lax.broadcasted_iota(jnp.int32, acc.shape, 2) & (LIFT_BLOCK - 1)
    diagonal = jnp.sum(jnp.where(sub == within, acc, 0.0), axis=1)
    lane = lax.broadcasted_iota(jnp.int32, diagonal.shape, 1)
    slot = lax.broadcasted_iota(jnp.int32, (heads, LANES), 1)
    packed = jnp.where(slot == HEADS_S, loss, 0.0)
    for index in range(HEADS_S):
        inside = (lane >= index * LIFT_BLOCK) & (lane < (index + 1) * LIFT_BLOCK)
        column = jnp.sum(jnp.where(inside, diagonal, 0.0), axis=1, keepdims=True)
        packed = jnp.where(slot == index, column, packed)
    packed = jnp.concatenate([packed, jnp.zeros((LANES - heads, LANES), F32)], axis=0)
    packed = jnp.transpose(packed)[:RIDE_ROWS]
    sums[...] = packed

    place = lax.axis_index("head")
    per = HEADS_S // shards
    count = row_parts + key_parts - 1
    for shard in range(shards):
        own, *others = pieces[shard * count : (shard + 1) * count]
        first = lax.rem(place + shard, shards) * per
        for index in range(per):
            tile = back[first + index]
            columns = slice(index * HD_S, (index + 1) * HD_S)
            on_keys = dot(tile, row_side[first + index]) * factors[1]
            on_rows = dot(tile, key_side[first + index], ((0,), (0,))) * factors[0]
            own[:part, columns] = on_rows[:part]
            own[part:, columns] = on_keys[:size]
            for spot in range(1, row_parts):
                others[spot - 1][:part, columns] = on_rows[spot * part : (spot + 1) * part]
            for spot in range(1, key_parts):
                others[row_parts + spot - 2][:size, columns] = on_keys[spot * size : (spot + 1) * size]
        for ref in others:
            if ref.shape[0] > part:
                high, low = split(packed * factors[2])
                ref[part:, :LANES] = high.astype(F32)
                ref[part:, LANES:] = low.astype(F32)


def close_kernel(mix_scale, loss_scale, mine, other, grad_mix, head_loss):
    heads = grad_mix.shape[1]
    total = mine[...] + other[...]
    grad_mix[...] = total[:HEADS_S, :heads] * mix_scale
    head_loss[...] = total[HEADS_S : HEADS_S + 1, :heads] * loss_scale


def body(teacher_query, teacher_key, student_query, student_key, head_mix):
    shard_rows = teacher_query.shape[1]
    heads = head_mix.shape[0]
    length = lax.axis_size("seq")
    shards = lax.axis_size("head")
    copies = lax.axis_size("dp")
    row_parts = max(size for size in range(1, math.isqrt(length) + 1) if length % size == 0)
    key_parts = length // row_parts
    rows, keys = row_parts * shard_rows, key_parts * shard_rows

    def along_rows(position, step):
        return position // row_parts * row_parts + (position % row_parts + step) % row_parts

    def along_keys(position, step):
        return (position + step * row_parts) % length

    def fetch(value, target, step):
        return lax.ppermute(value, "seq", [(target(i, step), i) for i in range(length)])

    def deliver(value, target, step, turn):
        pairs = [
            (h * length + i, (h + turn) % shards * length + target(i, step))
            for h in range(shards)
            for i in range(length)
        ]
        return lax.ppermute(value, ("head", "seq"), pairs)

    own = (teacher_key, teacher_query, student_key, student_query)
    key_t = [fetch(teacher_key, along_keys, d) for d in range(1, key_parts)]
    query_t = [fetch(teacher_query, along_rows, d) for d in range(1, row_parts)]
    share = pltpu.VMEM((1, shard_rows // shards, HEADS_S * HD_S), BF16)
    shares = pl.pallas_call(
        functools.partial(share_kernel, 2),
        out_shape=(share, share),
        in_specs=[pl.BlockSpec(memory_space=pl.ANY)] * 2,
        scratch_shapes=[pltpu.SemaphoreType.DMA((2,))],
        compiler_params=pltpu.CompilerParams(vmem_limit_bytes=VMEM_LIMIT // 4),
        name="share",
    )(*[pltpu.with_memory_space_constraint(array, pltpu.HBM) for array in (student_key, student_query)])

    def fetch_student(value, target, step):
        value = fetch(value, target, step)
        turns = [[(h, (h + turn) % shards) for h in range(shards)] for turn in range(1, shards)]
        return [value] + [lax.ppermute(value, "head", pairs) for pairs in turns]

    key_s = [piece for d in range(1, key_parts) for piece in fetch_student(shares[0], along_keys, d)]
    query_s = [piece for d in range(1, row_parts) for piece in fetch_student(shares[1], along_rows, d)]
    *own, lift_hi, lift_lo, back_both = prepare(head_mix, own)
    key_t, query_t, key_s, query_s = [[mine, *rest] for mine, rest in zip(own, (key_t, query_t, key_s, query_s))]

    exponents = pltpu.VMEM((heads, keys, rows), F32)
    student = pltpu.VMEM((HEADS_S, keys, rows), BF16)
    stats = pltpu.VMEM((heads, rows), F32)
    both = pltpu.VMEM((2, heads, rows), F32)
    sides = [pltpu.VMEM((HEADS_S, size, HD_S), BF16) for size in (keys, rows)]
    lifted, exp_l, stu_hi, stu_lo, top_l, lse_l, key_side, row_side = pl.pallas_call(
        functools.partial(student_kernel, (len(key_s), len(query_s)), shards, heads),
        out_shape=(exponents, exponents, student, student, stats, stats, *sides),
        compiler_params=pltpu.CompilerParams(vmem_limit_bytes=VMEM_LIMIT),
        cost_estimate=pl.CostEstimate(flops=STUDENT_FLOPS, bytes_accessed=1, transcendentals=1),
        name="student",
    )(*key_s, *query_s, lift_hi, lift_lo)

    def teacher(block_t, offset, before, extra):
        size = len(block_t) * shard_rows
        return pl.pallas_call(
            functools.partial(teacher_kernel, row_parts, len(block_t), heads, offset, bool(before)),
            out_shape=(pltpu.VMEM((heads, size, rows), F32), stats, stats, both) + (both,) * extra,
            compiler_params=pltpu.CompilerParams(vmem_limit_bytes=VMEM_LIMIT),
            name="teacher",
        )(*block_t, *query_t, lifted, lse_l, *before)

    done, before = [], []
    for first, block in ((0, key_t[:1]), (1, key_t[1:])):
        if block:
            extra = row_parts - 1 if first or key_parts == 1 else 0
            results = teacher(block, first * shard_rows, before, extra)
            done.append(results[:3])
            before, turned = results[3:4], results[4:]
    lse_parts = [*before] + [fetch(turned[step - 1], along_rows, row_parts - step) for step in range(1, row_parts)]

    weight = shard_rows * length / HEADS_T
    width = HEADS_S * HD_S // shards
    ride = RIDE_ROWS if width == 2 * LANES else 0
    factor = weight * HD_S ** (-0.5)
    room_query = room(2.0 * heads * MIX_TOP * VALUE_TOP * factor)
    room_key = room(rows * heads * MIX_TOP * VALUE_TOP * factor)
    room_sums = room(2.0 * rows * HD_S * VALUE_TOP**2)
    count = row_parts + key_parts - 1
    shapes = []
    for shard in range(shards):
        extra = ride if shard == 0 else 0
        shapes += [(2 * shard_rows, width)] + [(shard_rows + extra, width)] * (count - 1)
    sums, *pieces = pl.pallas_call(
        functools.partial(
            back_kernel,
            row_parts,
            key_parts,
            shards,
            len(done),
            heads,
            (factor * room_query, factor * room_key, room_sums),
        ),
        out_shape=[jax.ShapeDtypeStruct(shape, F32) for shape in [(RIDE_ROWS, LANES)] + shapes],
        scratch_shapes=[
            pltpu.VMEM((heads, rows), F32),
            pltpu.VMEM((heads, rows), F32),
            pltpu.VMEM((HEADS_S, keys, rows), BF16),
            pltpu.VMEM((heads * LIFT_BLOCK, HEADS_S * LIFT_BLOCK), F32),
        ],
        compiler_params=pltpu.CompilerParams(vmem_limit_bytes=VMEM_LIMIT),
        name="back",
    )(
        row_side, key_side, *lse_parts, back_both, exp_l, stu_hi, stu_lo, top_l,
        *[ref for block in done for ref in block],
    )

    moves = [(along_rows, step) for step in range(row_parts)] + [(along_keys, step) for step in range(1, key_parts)]
    arrived = [
        deliver(part.astype(F16), *moves[i % count], i // count) if i else part for i, part in enumerate(pieces)
    ]
    small = functools.partial(pl.pallas_call, compiler_params=pltpu.CompilerParams(vmem_limit_bytes=VMEM_LIMIT // 4))

    def diagonal(across, along):
        return lambda position, _: along_keys(along_rows(position, across), along)

    if ride:
        rides = [part[shard_rows:].astype(F32) for part in arrived[1:count]]
        others = [(part[:, :LANES] + part[:, LANES:]) * (1.0 / room_sums) for part in rides]
    else:
        others = [fetch(sums, target, step) for target, step in moves[1:]]
    for across in range(1, row_parts):
        others += [fetch(sums, diagonal(across, along), 0) for along in range(1, key_parts)]
    total = sum(others, sums)
    for_query = [part[:shard_rows].astype(F32) for i, part in enumerate(arrived) if i % count < row_parts]
    for_key = [
        part[-shard_rows:].astype(F32) if i % count == 0 else part[:shard_rows].astype(F32)
        for i, part in enumerate(arrived)
        if i % count == 0 or i % count >= row_parts
    ]
    grad_query = (sum(for_query[1:], for_query[0]) * (1.0 / room_query))[None]
    grad_key = (sum(for_key[1:], for_key[0]) * (1.0 / room_key))[None]
    last = jnp.zeros_like(total)
    if copies > 1 and copies & (copies - 1) == 0:
        for bit in range(copies.bit_length() - 1):
            total = total if bit == 0 else total + last
            last = lax.ppermute(total, "dp", [(i, i ^ (1 << bit)) for i in range(copies)])
    else:
        last = sum(
            [lax.ppermute(total, "dp", [(i, (i + step) % copies) for i in range(copies)]) for step in range(1, copies)],
            jnp.zeros_like(total),
        )
    last, grad_query, grad_key = lax.optimization_barrier((last, grad_query, grad_key))
    samples = copies * teacher_query.shape[0] * shard_rows * length
    grad_mix, head_loss = small(
        functools.partial(close_kernel, HD_S ** (-0.5) * weight / samples, 1.0 / samples),
        out_shape=(jax.ShapeDtypeStruct((HEADS_S, heads), F32), jax.ShapeDtypeStruct((1, heads), F32)),
        name="close",
    )(total, last)
    return (grad_query, grad_key, grad_mix.T, head_loss[0])


def solution(mesh):
    return jax.shard_map(
        body,
        mesh=mesh,
        in_specs=(
            P("dp", "seq", "head"),
            P("dp", "seq", "head"),
            P("dp", "seq", None),
            P("dp", "seq", None),
            P("head", None),
        ),
        out_specs=(P("dp", "seq", "head"), P("dp", "seq", "head"), P("head", None), P("head")),
        check_vma=False,
    )
```

```python
import functools
import math

import jax
import jax.numpy as jnp
from jax import lax
from jax.experimental import pallas as pl
from jax.experimental.pallas import tpu as pltpu
from jax.sharding import PartitionSpec as P

HEADS_T = 24
HD_T = 128
HEADS_S = 8
HD_S = 64
LOG2E = math.log2(math.e)
LN2 = math.log(2.0)
LIFT_BLOCK = 32
BACK_BLOCK = 16
RIDE_ROWS = 16
LANES = 128
STUDENT_FLOPS = 30*10**8
VMEM_LIMIT = 8 * 1024 * 1024

F32 = jnp.float32
BF16 = jnp.bfloat16
F16 = jnp.float16
MIX_TOP = 0.25
VALUE_TOP = 6.0


def dot(lhs, rhs, dims=((1,), (0,))):
    return lax.dot_general(lhs, rhs, (dims, ((), ())), preferred_element_type=F32)


def room(bound):
    return 2.0 ** math.floor(math.log2(float(jnp.finfo(F16).max) / (1.01 * bound)))


def split(value):
    high = value.astype(BF16)
    low = (value - high.astype(F32)).astype(BF16)
    return high, low


def prepare_kernel(count, mix_ref, mix_tr_ref, *refs):
    sources, targets = refs[:count], refs[count : 2 * count]
    lift_hi, lift_lo, back_both, semaphores = refs[2 * count :]
    moves = [pltpu.make_async_copy(sources[i], targets[i], semaphores.at[i]) for i in range(count)]
    for move in moves:
        move.start()

    def kron(values, size):
        rows, columns = values.shape
        lane = lax.broadcasted_iota(jnp.int32, (rows, columns * size), 1)
        spread = jnp.zeros((rows, columns * size), F32)
        for index in range(columns):
            inside = (lane >= index * size) & (lane < (index + 1) * size)
            spread = jnp.where(inside, values[:, index : index + 1], spread)
        full = (rows, size, columns * size)
        sub = lax.broadcasted_iota(jnp.int32, full, 1)
        within = lax.broadcasted_iota(jnp.int32, full, 2) & (size - 1)
        picked = jnp.where(sub == within, spread[:, None, :], 0.0)
        return picked.reshape(rows * size, columns * size)

    scaled = mix_ref[...] * (HD_S ** (-0.5) * LOG2E)
    lift_hi[...], lift_lo[...] = split(kron(scaled, LIFT_BLOCK))
    high, low = split(kron(mix_tr_ref[...], BACK_BLOCK))
    back_both[: high.shape[0]] = high
    back_both[high.shape[0] :] = low
    for move in moves:
        move.wait()


def prepare(head_mix, arrays):
    heads = head_mix.shape[0]
    lift = pltpu.VMEM((heads * LIFT_BLOCK, HEADS_S * LIFT_BLOCK), BF16)
    back = pltpu.VMEM((2 * HEADS_S * BACK_BLOCK, heads * BACK_BLOCK), BF16)
    count = len(arrays)
    whole = pl.BlockSpec(memory_space=pltpu.VMEM)
    return pl.pallas_call(
        functools.partial(prepare_kernel, count),
        out_shape=[pltpu.VMEM(array.shape, array.dtype) for array in arrays] + [lift, lift, back],
        in_specs=[whole, whole] + [pl.BlockSpec(memory_space=pl.ANY)] * count,
        scratch_shapes=[pltpu.SemaphoreType.DMA((count,))],
        compiler_params=pltpu.CompilerParams(vmem_limit_bytes=VMEM_LIMIT // 2),
        name="prepare",
    )(head_mix, head_mix.T, *[pltpu.with_memory_space_constraint(array, pltpu.HBM) for array in arrays])


def stacked(refs, columns):
    parts = [ref[0, :, columns] for ref in refs]
    return parts[0] if len(parts) == 1 else jnp.concatenate(parts, axis=0)


def share_kernel(count, *refs):
    sources, targets, semaphores = refs[:count], refs[count : 2 * count], refs[-1]
    size = targets[0].shape[1]
    start = pl.multiple_of(lax.axis_index("head") * size, size)
    moves = [
        pltpu.make_async_copy(source.at[:, pl.ds(start, size), :], target, semaphores.at[i])
        for i, (source, target) in enumerate(zip(sources, targets))
    ]
    for move in moves:
        move.start()
    for move in moves:
        move.wait()


def by_head(shards, pieces, side):
    place = lax.axis_index("head")
    own, *others = pieces
    part = own.shape[1]
    for index in range(HEADS_S):
        columns = slice(index * HD_S, (index + 1) * HD_S)
        side[index, :part] = own[0, :, columns]
        for i, piece in enumerate(others):
            size = piece.shape[1]
            first = (i // shards + 1) * part + lax.rem(place + shards - i % shards, shards) * size
            side[index, pl.ds(pl.multiple_of(first, size), size), :] = piece[0, :, columns]


def student_kernel(counts, shards, heads, *refs):
    key_s, query_s, refs = refs[: counts[0]], refs[counts[0] : sum(counts)], refs[sum(counts) :]
    lift_hi, lift_lo, lifted, exp_l, stu_hi, stu_lo, top, lse, key_side, query_side = refs
    keys, rows = stu_hi.shape[1:]
    by_head(shards, key_s, key_side)
    by_head(shards, query_s, query_side)
    for index in range(HEADS_S):
        stu_hi[index], stu_lo[index] = split(dot(key_side[index], query_side[index], ((1,), (1,))))
    for start in range(0, keys, LIFT_BLOCK):
        block = slice(start, start + LIFT_BLOCK)
        high = stu_hi[:, block, :].reshape(HEADS_S * LIFT_BLOCK, rows)
        low = stu_lo[:, block, :].reshape(HEADS_S * LIFT_BLOCK, rows)
        total = dot(lift_hi[...], high) + (dot(lift_hi[...], low) + dot(lift_lo[...], high))
        lifted[:, block, :] = total.reshape(heads, LIFT_BLOCK, rows)
    for head in range(heads):
        mixed = lifted[head]
        best = jnp.max(mixed, axis=0, keepdims=True)
        prob = jnp.exp2(mixed - best)
        exp_l[head] = prob
        top[head : head + 1, :] = best
        lse[head : head + 1, :] = best + jnp.log2(jnp.sum(prob, axis=0, keepdims=True))


def teacher_kernel(row_parts, key_parts, heads, offset, carried, *refs):
    key_t, query_t, refs = refs[:key_parts], refs[key_parts : key_parts + row_parts], refs[key_parts + row_parts :]
    lifted, lse_l, *refs = refs
    before = refs.pop(0) if carried else None
    exp_t, top, kl, lse, *turned = refs
    keys, rows = exp_t.shape[1:]
    for head in range(heads):
        columns = slice(head * HD_T, (head + 1) * HD_T)
        teacher = dot(stacked(key_t, columns), stacked(query_t, columns), ((1,), (1,)))
        teacher = teacher * (HD_T ** (-0.5) * LOG2E)
        best = jnp.max(teacher, axis=0, keepdims=True)
        prob = jnp.exp2(teacher - best)
        exp_t[head] = prob
        mixed = lifted[head, offset : offset + keys, :]
        kl[head : head + 1, :] = jnp.sum(prob * (teacher - mixed), axis=0, keepdims=True)
        top[head : head + 1, :] = best
        total = jnp.sum(prob, axis=0, keepdims=True)
        if carried:
            earlier = before[0, head : head + 1, :]
            higher = jnp.maximum(best, earlier)
            total = total * jnp.exp2(best - higher) + jnp.exp2(earlier - higher)
            best = higher
        lse[0, head : head + 1, :] = best + jnp.log2(total)
    lse[1] = lse_l[...]
    part = rows // row_parts
    for step, ref in enumerate(turned, 1):
        for spot in range(row_parts):
            source = (spot + step) % row_parts * part
            ref[:, :, spot * part : (spot + 1) * part] = lse[:, :, source : source + part]


def back_kernel(row_parts, key_parts, shards, blocks, heads, factors, *refs):
    refs = list(refs)
    row_side, key_side = refs.pop(0), refs.pop(0)
    lse = [refs.pop(0) for _ in range(row_parts)]
    back_both, exp_l, stu_hi, stu_lo, top_l = refs[:5]
    maps = [refs[5 + 3 * i : 8 + 3 * i] for i in range(blocks)]
    *outs, scale_t, scale_l, back, mix_acc = refs[5 + 3 * blocks :]
    keys, rows = back.shape[1:]
    part, size = rows // row_parts, keys // key_parts
    sums, pieces = outs[0], outs[1:]

    lse_all = []
    for which in range(2):
        parts = [ref[which] for ref in lse]
        best = functools.reduce(jnp.maximum, parts)
        total = sum(jnp.exp2(value - best) for value in parts)
        lse_all.append(best + jnp.log2(total))
    own = lax.broadcasted_iota(jnp.int32, (heads, rows), 1) < part
    loss = jnp.where(own, lse_all[1] - lse_all[0], 0.0)
    mix_acc[...] = jnp.zeros_like(mix_acc)
    offset = 0
    scale_l[...] = jnp.exp2(top_l[...] - lse_all[1])
    for exp_t, top_t, kl in maps:
        scale_t[...] = jnp.exp2(top_t[...] - lse_all[0])
        loss = loss + scale_t[...] * kl[...]
        for start in range(0, exp_t.shape[1], LIFT_BLOCK):
            block = slice(start, start + LIFT_BLOCK)
            place = slice(offset + start, offset + start + LIFT_BLOCK)
            excess = (
                exp_l[:, place, :] * scale_l[...][:, None, :] - exp_t[:, block, :] * scale_t[...][:, None, :]
            )
            high, low = split(excess)
            s_high = stu_hi[:, place, :].reshape(HEADS_S * LIFT_BLOCK, rows)
            s_low = stu_lo[:, place, :].reshape(HEADS_S * LIFT_BLOCK, rows)
            f_high = high.reshape(heads * LIFT_BLOCK, rows)
            f_low = low.reshape(heads * LIFT_BLOCK, rows)
            over_rows = ((1,), (1,))
            mix_acc[...] += dot(f_high, s_high, over_rows) + (
                dot(f_high, s_low, over_rows) + dot(f_low, s_high, over_rows)
            )
            for inner in range(0, LIFT_BLOCK, BACK_BLOCK):
                b_high = high[:, inner : inner + BACK_BLOCK, :].reshape(heads * BACK_BLOCK, rows)
                b_low = low[:, inner : inner + BACK_BLOCK, :].reshape(heads * BACK_BLOCK, rows)
                half = HEADS_S * BACK_BLOCK
                twice = dot(back_both[...], b_high)
                total = twice[:half] + (dot(back_both[:half], b_low) + twice[half:])
                first = offset + start + inner
                back[:, first : first + BACK_BLOCK, :] = total.astype(BF16).reshape(HEADS_S, BACK_BLOCK, rows)
        offset += exp_t.shape[1]
    loss = jnp.sum(loss, axis=1, keepdims=True) * LN2

    acc = mix_acc[...].reshape(heads, LIFT_BLOCK, HEADS_S * LIFT_BLOCK)
    sub = lax.broadcasted_iota(jnp.int32, acc.shape, 1)
    within = lax.broadcasted_iota(jnp.int32, acc.shape, 2) & (LIFT_BLOCK - 1)
    diagonal = jnp.sum(jnp.where(sub == within, acc, 0.0), axis=1)
    lane = lax.broadcasted_iota(jnp.int32, diagonal.shape, 1)
    slot = lax.broadcasted_iota(jnp.int32, (heads, LANES), 1)
    packed = jnp.where(slot == HEADS_S, loss, 0.0)
    for index in range(HEADS_S):
        inside = (lane >= index * LIFT_BLOCK) & (lane < (index + 1) * LIFT_BLOCK)
        column = jnp.sum(jnp.where(inside, diagonal, 0.0), axis=1, keepdims=True)
        packed = jnp.where(slot == index, column, packed)
    packed = jnp.concatenate([packed, jnp.zeros((LANES - heads, LANES), F32)], axis=0)
    packed = jnp.transpose(packed)[:RIDE_ROWS]
    sums[...] = packed

    place = lax.axis_index("head")
    per = HEADS_S // shards
    count = row_parts + key_parts - 1
    for shard in range(shards):
        own, *others = pieces[shard * count : (shard + 1) * count]
        first = lax.rem(place + shard, shards) * per
        for index in range(per):
            tile = back[first + index]
            columns = slice(index * HD_S, (index + 1) * HD_S)
            on_keys = dot(tile, row_side[first + index]) * factors[1]
            on_rows = dot(tile, key_side[first + index], ((0,), (0,))) * factors[0]
            own[:part, columns] = on_rows[:part]
            own[part:, columns] = on_keys[:size]
            for spot in range(1, row_parts):
                others[spot - 1][:part, columns] = on_rows[spot * part : (spot + 1) * part]
            for spot in range(1, key_parts):
                others[row_parts + spot - 2][:size, columns] = on_keys[spot * size : (spot + 1) * size]
        for ref in others:
            if ref.shape[0] > part:
                high, low = split(packed * factors[2])
                ref[part:, :LANES] = high.astype(F32)
                ref[part:, LANES:] = low.astype(F32)


def close_kernel(mix_scale, loss_scale, mine, other, grad_mix, head_loss):
    heads = grad_mix.shape[1]
    total = mine[...] + other[...]
    grad_mix[...] = total[:HEADS_S, :heads] * mix_scale
    head_loss[...] = total[HEADS_S : HEADS_S + 1, :heads] * loss_scale


def body(teacher_query, teacher_key, student_query, student_key, head_mix):
    shard_rows = teacher_query.shape[1]
    heads = head_mix.shape[0]
    length = lax.axis_size("seq")
    shards = lax.axis_size("head")
    copies = lax.axis_size("dp")
    row_parts = max(size for size in range(1, math.isqrt(length) + 1) if length % size == 0)
    key_parts = length // row_parts
    rows, keys = row_parts * shard_rows, key_parts * shard_rows

    def along_rows(position, step):
        return position // row_parts * row_parts + (position % row_parts + step) % row_parts

    def along_keys(position, step):
        return (position + step * row_parts) % length

    def fetch(value, target, step):
        return lax.ppermute(value, "seq", [(target(i, step), i) for i in range(length)])

    def deliver(value, target, step, turn):
        pairs = [
            (h * length + i, (h + turn) % shards * length + target(i, step))
            for h in range(shards)
            for i in range(length)
        ]
        return lax.ppermute(value, ("head", "seq"), pairs)

    own = (teacher_key, teacher_query, student_key, student_query)
    key_t = [fetch(teacher_key, along_keys, d) for d in range(1, key_parts)]
    query_t = [fetch(teacher_query, along_rows, d) for d in range(1, row_parts)]
    share = pltpu.VMEM((1, shard_rows // shards, HEADS_S * HD_S), BF16)
    shares = pl.pallas_call(
        functools.partial(share_kernel, 2),
        out_shape=(share, share),
        in_specs=[pl.BlockSpec(memory_space=pl.ANY)] * 2,
        scratch_shapes=[pltpu.SemaphoreType.DMA((2,))],
        compiler_params=pltpu.CompilerParams(vmem_limit_bytes=VMEM_LIMIT // 4),
        name="share",
    )(*[pltpu.with_memory_space_constraint(array, pltpu.HBM) for array in (student_key, student_query)])

    def fetch_student(value, target, step):
        value = fetch(value, target, step)
        turns = [[(h, (h + turn) % shards) for h in range(shards)] for turn in range(1, shards)]
        return [value] + [lax.ppermute(value, "head", pairs) for pairs in turns]

    key_s = [piece for d in range(1, key_parts) for piece in fetch_student(shares[0], along_keys, d)]
    query_s = [piece for d in range(1, row_parts) for piece in fetch_student(shares[1], along_rows, d)]
    *own, lift_hi, lift_lo, back_both = prepare(head_mix, own)
    key_t, query_t, key_s, query_s = [[mine, *rest] for mine, rest in zip(own, (key_t, query_t, key_s, query_s))]

    exponents = pltpu.VMEM((heads, keys, rows), F32)
    student = pltpu.VMEM((HEADS_S, keys, rows), BF16)
    stats = pltpu.VMEM((heads, rows), F32)
    both = pltpu.VMEM((2, heads, rows), F32)
    sides = [pltpu.VMEM((HEADS_S, size, HD_S), BF16) for size in (keys, rows)]
    lifted, exp_l, stu_hi, stu_lo, top_l, lse_l, key_side, row_side = pl.pallas_call(
        functools.partial(student_kernel, (len(key_s), len(query_s)), shards, heads),
        out_shape=(exponents, exponents, student, student, stats, stats, *sides),
        compiler_params=pltpu.CompilerParams(vmem_limit_bytes=VMEM_LIMIT),
        cost_estimate=pl.CostEstimate(flops=STUDENT_FLOPS, bytes_accessed=1, transcendentals=1),
        name="student",
    )(*key_s, *query_s, lift_hi, lift_lo)

    def teacher(block_t, offset, before, extra):
        size = len(block_t) * shard_rows
        return pl.pallas_call(
            functools.partial(teacher_kernel, row_parts, len(block_t), heads, offset, bool(before)),
            out_shape=(pltpu.VMEM((heads, size, rows), F32), stats, stats, both) + (both,) * extra,
            compiler_params=pltpu.CompilerParams(vmem_limit_bytes=VMEM_LIMIT),
            name="teacher",
        )(*block_t, *query_t, lifted, lse_l, *before)

    done, before = [], []
    for first, block in ((0, key_t[:1]), (1, key_t[1:])):
        if block:
            extra = row_parts - 1 if first or key_parts == 1 else 0
            results = teacher(block, first * shard_rows, before, extra)
            done.append(results[:3])
            before, turned = results[3:4], results[4:]
    lse_parts = [*before] + [fetch(turned[step - 1], along_rows, row_parts - step) for step in range(1, row_parts)]

    weight = shard_rows * length / HEADS_T
    width = HEADS_S * HD_S // shards
    ride = RIDE_ROWS if width == 2 * LANES else 0
    factor = weight * HD_S ** (-0.5)
    room_query = room(2.0 * heads * MIX_TOP * VALUE_TOP * factor)
    room_key = room(rows * heads * MIX_TOP * VALUE_TOP * factor)
    room_sums = room(2.0 * rows * HD_S * VALUE_TOP**2)
    count = row_parts + key_parts - 1
    shapes = []
    for shard in range(shards):
        extra = ride if shard == 0 else 0
        shapes += [(2 * shard_rows, width)] + [(shard_rows + extra, width)] * (count - 1)
    sums, *pieces = pl.pallas_call(
        functools.partial(
            back_kernel,
            row_parts,
            key_parts,
            shards,
            len(done),
            heads,
            (factor * room_query, factor * room_key, room_sums),
        ),
        out_shape=[jax.ShapeDtypeStruct(shape, F32) for shape in [(RIDE_ROWS, LANES)] + shapes],
        scratch_shapes=[
            pltpu.VMEM((heads, rows), F32),
            pltpu.VMEM((heads, rows), F32),
            pltpu.VMEM((HEADS_S, keys, rows), BF16),
            pltpu.VMEM((heads * LIFT_BLOCK, HEADS_S * LIFT_BLOCK), F32),
        ],
        compiler_params=pltpu.CompilerParams(vmem_limit_bytes=VMEM_LIMIT),
        name="back",
    )(
        row_side, key_side, *lse_parts, back_both, exp_l, stu_hi, stu_lo, top_l,
        *[ref for block in done for ref in block],
    )

    moves = [(along_rows, step) for step in range(row_parts)] + [(along_keys, step) for step in range(1, key_parts)]
    arrived = [
        deliver(part.astype(F16), *moves[i % count], i // count) if i else part for i, part in enumerate(pieces)
    ]
    small = functools.partial(pl.pallas_call, compiler_params=pltpu.CompilerParams(vmem_limit_bytes=VMEM_LIMIT // 4))

    def diagonal(across, along):
        return lambda position, _: along_keys(along_rows(position, across), along)

    if ride:
        rides = [part[shard_rows:].astype(F32) for part in arrived[1:count]]
        others = [(part[:, :LANES] + part[:, LANES:]) * (1.0 / room_sums) for part in rides]
    else:
        others = [fetch(sums, target, step) for target, step in moves[1:]]
    for across in range(1, row_parts):
        others += [fetch(sums, diagonal(across, along), 0) for along in range(1, key_parts)]
    total = sum(others, sums)
    for_query = [part[:shard_rows].astype(F32) for i, part in enumerate(arrived) if i % count < row_parts]
    for_key = [
        part[-shard_rows:].astype(F32) if i % count == 0 else part[:shard_rows].astype(F32)
        for i, part in enumerate(arrived)
        if i % count == 0 or i % count >= row_parts
    ]
    grad_query = (sum(for_query[1:], for_query[0]) * (1.0 / room_query))[None]
    grad_key = (sum(for_key[1:], for_key[0]) * (1.0 / room_key))[None]
    last = jnp.zeros_like(total)
    if copies > 1 and copies & (copies - 1) == 0:
        for bit in range(copies.bit_length() - 1):
            total = total if bit == 0 else total + last
            last = lax.ppermute(total, "dp", [(i, i ^ (1 << bit)) for i in range(copies)])
    else:
        last = sum(
            [lax.ppermute(total, "dp", [(i, (i + step) % copies) for i in range(copies)]) for step in range(1, copies)],
            jnp.zeros_like(total),
        )
    last, grad_key, grad_query = lax.optimization_barrier((last, grad_key, grad_query))
    samples = copies * teacher_query.shape[0] * shard_rows * length
    grad_mix, head_loss = small(
        functools.partial(close_kernel, HD_S ** (-0.5) * weight / samples, 1.0 / samples),
        out_shape=(jax.ShapeDtypeStruct((HEADS_S, heads), F32), jax.ShapeDtypeStruct((1, heads), F32)),
        name="close",
    )(total, last)
    return (grad_query, grad_key, grad_mix.T, head_loss[0])


def solution(mesh):
    return jax.shard_map(
        body,
        mesh=mesh,
        in_specs=(
            P("dp", "seq", "head"),
            P("dp", "seq", "head"),
            P("dp", "seq", None),
            P("dp", "seq", None),
            P("head", None),
        ),
        out_specs=(P("dp", "seq", "head"), P("dp", "seq", "head"), P("head", None), P("head")),
        check_vma=False,
    )
```
